32 devices in a mesh: groups: 1, tm: 32 (over z, y, x, core), users: 1.
Axes of the slice: x: 2, y: 2, z: 4, core: 2. Of those that a mesh axis runs over, the one named last changes fastest.
Arguments:
- item_table: bfloat16 [131072, 256], P('tm'), may hold values from -6 to 6
- item_shard: int32 [32, 8, 1536, 1], P('tm', ('groups', 'users')), may hold values from 0 to 31; in each aligned block of 12288 rows (0 to 12287, 12288 to 24575, ..., all dimensions but the last counted through in order) at most 768 rows name the same one
- item_row: int32 [32, 8, 1536], P('tm', ('groups', 'users')), may hold values from 0 to 4095
- cluster_id: int32 [32, 8, 1536], P('tm', ('groups', 'users')), may hold values from 0 to 1023
- lengths: int32 [8], P(('groups', 'users')), may hold values from 1536 to 49152, as said below
Outputs:
- cluster_means: float32 [8, 1024, 256], P(('groups', 'users'), 'tm')
The draws below stay inside these ranges and needn't reach their ends.
Inputs may be any that keep to these rules, and one draw needn't show every extreme that they name: `item_shard`: among the 8 x 1536 rows of one device (one slab, one half of the users) at most 768 name the same shard, and this bound is reached. `lengths`: some user's history fills all 49152 positions.
All inputs are finite; a program needn't handle non-finite values.
Results may differ from the reference program's by a relative error of at most 0.00035.
Values may be sent and summed in bfloat16 or wider, within the bound.
No kernel may reach another device: no remote copies, remote signals or barrier semaphores. Data moves between devices by JAX's collectives and lax.ppermute only.
A program may use at most 128 MiB of HBM per device.

```python
import math
import jax
import jax.numpy as jnp
import numpy as np
from jax import lax

E = 256
K = 1024
V_DEV = 4096
USER_SUB = 8
L_SLAB = 1536
SLABS = 32
USERS = 8
HIST = 49152
V = 131072
CAP = 768


def draw_lengths(key, part):
    key = jax.random.fold_in(key, 11)
    drawn = jax.random.randint(key, (USERS,), L_SLAB, HIST + 1, dtype=jnp.int32)
    picked = jax.random.randint(jax.random.fold_in(key, 5), (), 0, USERS, dtype=jnp.int32)
    return jnp.where(jnp.arange(USERS, dtype=jnp.int32) == picked, HIST, drawn).astype(jnp.int32)


def with_ends(array, key, low, top_value):
    dims = array.shape
    spot = [jax.random.randint(jax.random.fold_in(key, axis), (), 0, dims[axis]) for axis in range(len(dims))]
    array = array.at[tuple(spot)].set(low)
    longest = dims.index(max(dims))
    spot[longest] = (spot[longest] + 1) % dims[longest]
    return array.at[tuple(spot)].set(top_value)


def block_scale(stream_key, shape, cuts, smallest, largest):
    loudness = 1.0
    for axis_at, shards_of in cuts:
        draws = jax.random.uniform(jax.random.fold_in(jax.random.fold_in(stream_key, 6), axis_at), (shards_of,), jnp.float32, smallest / len(cuts), largest / len(cuts))
        loudness = loudness * jnp.repeat(jnp.exp(draws), shape[axis_at] // shards_of).reshape((-1,) + (1,) * (len(shape) - 1 - axis_at))
    return loudness


def deal_out(stream_key, own, number, rows, amount, top, reach, slope):
    order = jax.random.permutation(stream_key, amount)
    heavy_load, ordinary = shares(amount, rows * top, reach, slope, True), shares(amount, rows * top, reach, slope, False)
    places = jnp.arange(amount)

    def named(tallies, rotation):
        used = int((tallies > 0).sum())
        fixed = max(1, used // 4)
        shifted = fixed + (places - fixed + rotation * (used - fixed)) % max(1, amount - fixed)
        return jnp.zeros((amount,), jnp.int32).at[order[jnp.where(places < fixed, places, shifted)]].set(jnp.asarray(tallies, jnp.int32))

    tallies = jnp.where(number % 4 == 0, named(heavy_load, number // 4), named(ordinary, number - number // 4 - 1))
    mixed = jax.random.permutation(jax.random.fold_in(own, 3), amount)
    source_of, receiver = mixed[0:amount // 2 * 2:2], mixed[1:amount // 2 * 2:2]
    room = jnp.minimum(tallies[source_of] - 1, reach - tallies[receiver]) // 2
    room = jnp.where((source_of == order[0]) | (receiver == order[0]) | (tallies[receiver] == 0), 0, jnp.maximum(room, 0))
    shifted = jax.random.randint(jax.random.fold_in(own, 4), (amount // 2,), 0, 1 << 20) % (room + 1)
    tallies = tallies.at[source_of].add(-shifted).at[receiver].add(shifted)
    labels = jnp.searchsorted(jnp.cumsum(tallies), jnp.arange(rows * top), side="right").astype(jnp.int32)
    table = labels.reshape(top, rows).T
    table = table[jax.random.permutation(jax.random.fold_in(own, 1), rows)]
    rotation = jax.random.randint(jax.random.fold_in(own, 2), (rows, 1), 0, top)
    return jnp.take_along_axis(table, (jnp.arange(top)[None, :] + rotation) % top, axis=1)


def shares(number_of, total, limit, lean, full):
    portions = [(1 << 20) // math.isqrt(standing ** lean) + 1 for standing in range(1, number_of + 1)]
    largest = limit if full else min(limit, max(-(-total // number_of), total * portions[0] // sum(portions)))
    least = 1 if total - largest >= number_of - 1 else 0
    holding, spare = [largest] + [least] * (number_of - 1), total - largest - least * (number_of - 1)
    while spare > 0:
        free = [i for i in range(1, number_of) if holding[i] < largest] or [i for i in range(1, number_of) if holding[i] < limit]
        pool, budget = sum([portions[i] for i in free]), spare
        for i in free:
            extra = min(limit - holding[i], max(1, budget * portions[i] // pool), spare)
            holding[i] = holding[i] + extra
            spare = spare - extra
    return np.array(holding)


def bell_draw(rng, dims, width, limit, cuts=(), kind=jnp.bfloat16):
    result = jax.random.normal(rng, dims, jnp.float32) * width
    if len(cuts) > 0:
        result = block_scale(rng, dims, cuts, -0.22, 0.18) * result
    return jnp.clip(result, min=-limit, max=limit).astype(kind)


def setup_inputs(seed: int = 0, part: int = 0) -> dict:
    splits = jax.random.split(jax.random.key(seed), 6)
    own_keys = jax.random.split(jax.random.fold_in(splits[5], part), 6)
    item_table = bell_draw(splits[0], (V, E), 1.0, 6.0, ((0, 32),))
    item_shard_keys = jax.random.split(jax.random.fold_in(own_keys[1], 1), SLABS * USERS * L_SLAB // (USER_SUB * L_SLAB))
    item_shard_turns = jax.random.permutation(jax.random.fold_in(own_keys[1], 3), SLABS * USERS * L_SLAB // (USER_SUB * L_SLAB))
    item_shard = jax.vmap(lambda own, number: deal_out(jax.random.fold_in(own_keys[1], 2), own, number, USER_SUB * L_SLAB, SLABS, 1, CAP, 2))(item_shard_keys, item_shard_turns).reshape((SLABS, USERS, L_SLAB, 1))
    item_row = with_ends(jax.random.randint(own_keys[2], (SLABS, USERS, L_SLAB), 0, V_DEV), jax.random.fold_in(own_keys[2], 1), 0, V_DEV - 1).astype(jnp.int32)
    cluster_id = with_ends(jax.random.randint(own_keys[3], (SLABS, USERS, L_SLAB), 0, K), jax.random.fold_in(own_keys[3], 1), 0, K - 1).astype(jnp.int32)
    lengths = draw_lengths(jax.random.fold_in(jax.random.fold_in(splits[5], part), 71), part)
    return {"item_table": item_table, "item_shard": item_shard, "item_row": item_row, "cluster_id": cluster_id, "lengths": lengths}


def reference(item_table, item_shard, item_row, cluster_id, lengths):
    item_ids = item_shard[..., 0] * V_DEV + item_row
    slab_ids = jnp.arange(SLABS, dtype=jnp.int32)
    user_base = jnp.arange(USERS, dtype=jnp.int32)[:, None] * K

    def per_slab(running, inputs):
        slab_items, slab_clusters, slab_index = inputs
        position = slab_index * L_SLAB + jnp.arange(L_SLAB, dtype=jnp.int32)[None, :]
        is_live = position < lengths[:, None]
        cluster_keys = jnp.where(is_live, user_base + slab_clusters, USERS * K).reshape(-1)
        fetched = jnp.take(item_table, slab_items.reshape(-1), axis=0).astype(jnp.float32)
        new_sums = running[0] + jax.ops.segment_sum(fetched, cluster_keys, num_segments=USERS * K)
        ones_rows = jnp.ones((USERS * L_SLAB,), jnp.float32)
        new_counts = running[1] + jax.ops.segment_sum(ones_rows, cluster_keys, num_segments=USERS * K)
        return (new_sums, new_counts), None

    start = (jnp.zeros((USERS * K, E), jnp.float32), jnp.zeros((USERS * K,), jnp.float32))
    (cluster_sums, member_counts), _ = lax.scan(per_slab, start, (item_ids, cluster_id, slab_ids))
    cluster_sums = cluster_sums.reshape(USERS, K, E)
    member_counts = member_counts.reshape(USERS, K)
    return cluster_sums / jnp.maximum(member_counts, 1.0)[..., None]
```

```python
import functools

import jax
import jax.numpy as jnp
from jax import lax
from jax.experimental import pallas as pl
from jax.experimental.pallas import tpu as pltpu
from jax.sharding import PartitionSpec as P

K = 1024
LANES = 128
GROUP = 16
FLAG = 1 << 30


def bits_for(count):
    return (count - 1).bit_length()


def user_chains(users):
    third = -(-users * 3 // 8)
    cuts = sorted({0, min(third, users), min(2 * third, users), users})
    return [(lo, hi - lo) for lo, hi in zip(cuts[:-1], cuts[1:])]


def bucket_kernel(n, dest_shift, cell_bits, dummy, live_ref, keys_ref, out_ref, pad):
    rows = keys_ref.shape[0]
    cap_rows = out_ref.shape[1]
    pad[0:rows, :] = keys_ref[...]
    pad[rows:, :] = jnp.full((pad.shape[0] - rows, LANES), dummy, jnp.int32)
    keys = keys_ref[...]
    lane = lax.broadcasted_iota(jnp.int32, (cap_rows, LANES), 1)
    slot = lax.broadcasted_iota(jnp.int32, (cap_rows, LANES), 0) * LANES + lane
    in_group = lane % GROUP
    live = live_ref[0]
    start = jnp.int32(0)
    for d in range(n):
        end = live
        if d < n - 1:
            below = (keys < jnp.int32((d + 1) << dest_shift)).astype(jnp.float32)
            end = jnp.sum(below).astype(jnp.int32)
        count = end - start
        first = lax.div(start, LANES)
        off = start - first * LANES
        block = pad[pl.ds(first, cap_rows + 1), :]
        turned = pltpu.roll(block, lax.rem(LANES - off, LANES), axis=1)
        mine = jnp.where(lane < LANES - off, turned[:cap_rows], turned[1:])
        code = mine & ((1 << dest_shift) - 1)
        cell = code & ((1 << cell_bits) - 1)
        row = lax.shift_right_logical(code, cell_bits)
        code = jnp.where(slot < count, (row << (cell_bits + 1)) | cell, dummy)
        cell = code & ((2 << cell_bits) - 1)
        twice = jnp.zeros((cap_rows, LANES), jnp.int32)
        for back in range(1, GROUP):
            same = (pltpu.roll(cell, back, axis=1) == cell) & (in_group >= back)
            twice = twice | same.astype(jnp.int32)
        twice = jnp.where(code == dummy, 0, twice)
        step = 1
        while step < GROUP:
            twice = twice | pltpu.roll(twice, LANES - step, axis=1)
            step *= 2
        flagged = (in_group == 0) & (twice > 0)
        out_ref[d] = jnp.where(flagged, code | FLAG, code)
        start = end


def add_kernel(n, cap, cell_bits, dummy, cuts, list_ref, own_ref, other_ref, *rest):
    out_refs = rest[: len(cuts)]
    table, sums, sems = rest[len(cuts) :]
    rows = own_ref.shape[0]
    block = 128

    def widen(i, _):
        for part, ref in enumerate((own_ref, other_ref)):
            x = ref[pl.ds(i * block, block), :].astype(jnp.float32)
            at = (part * rows + i * block) * 2
            table[pl.ds(at, block, stride=2), :] = x[:, :LANES]
            table[pl.ds(at + 1, block, stride=2), :] = x[:, LANES:]
        return 0

    lax.fori_loop(0, rows // block, widen, 0)

    def clear(i, _):
        sums[pl.ds(i * 256, 256), :] = jnp.zeros((256, LANES), jnp.float32)
        return 0

    lax.fori_loop(0, sums.shape[0] // 256, clear, 0)
    low = (2 << cell_bits) - 1

    def place(code, first):
        if first:
            code = code & (FLAG - 1)
        cell = (code & low) * 2
        row = lax.shift_right_logical(code, cell_bits + 1) * 2
        return pl.ds(pl.multiple_of(cell, 2), 2), pl.ds(pl.multiple_of(row, 2), 2)

    def source(s, _):
        def more(i):
            return (i < cap) & (list_ref[s, jnp.minimum(i, cap - 1)] != dummy)

        def step(i):
            codes = [list_ref[s, i + k] for k in range(GROUP)]
            places = [place(c, k == 0) for k, c in enumerate(codes)]

            @pl.when(codes[0] < FLAG)
            def _():
                new = [sums[c, :] + table[r, :] for c, r in places]
                for (c, _), v in zip(places, new):
                    sums[c, :] = v

            @pl.when(codes[0] >= FLAG)
            def _():
                for c, r in places:
                    sums[c, :] = sums[c, :] + table[r, :]

            return i + GROUP

        lax.while_loop(more, step, jnp.int32(0))
        return 0

    lax.fori_loop(0, n, source, 0)
    copies = [
        pltpu.make_async_copy(sums.at[pl.ds(at, size), :], ref, sems.at[k])
        for k, ((at, size), ref) in enumerate(zip(cuts, out_refs))
    ]
    for copy in copies:
        copy.start()
    for copy in copies:
        copy.wait()


def per_device(item_table, item_shard, item_row, cluster_id, lengths):
    n = lax.axis_size("tm")
    me = lax.axis_index("tm")
    users, slab = item_row.shape[1:]
    rows, width = item_table.shape
    total = users * slab
    owned = K // n
    m = bits_for(n) - 1
    cells = users * K // 2
    cell_bits = bits_for(cells)
    dest_shift = cell_bits + bits_for(2 * rows)
    cap = 2 * max(2, 2 * total // n)
    cap = -(-cap // LANES) * LANES
    chains = user_chains(users)
    dummy = cells

    shard = item_shard.reshape(users, slab)
    cluster = cluster_id.reshape(users, slab)
    owner = cluster // owned
    dest = (shard & ~1) | (owner & 1)
    away = (owner ^ dest) >> 1
    row = ((shard ^ owner) & 1) * rows + item_row.reshape(users, slab)
    cell_parts = []
    for g, (lo, size) in enumerate(chains):
        bits = [(g + k) % m for k in range(m)]
        spread = jnp.zeros((size, slab), jnp.int32)
        for b in bits:
            spread = spread * 2 + ((away[lo : lo + size] >> b) & 1)
        user = jnp.arange(size, dtype=jnp.int32)[:, None]
        cell_parts.append(
            lo * (K // 2) + (spread * size + user) * owned + cluster[lo : lo + size] % owned
        )
    cell = jnp.concatenate(cell_parts, axis=0)
    position = me * slab + jnp.arange(slab, dtype=jnp.int32)[None, :]
    is_live = position < lengths[:, None]
    key = (dest << dest_shift) | (row << cell_bits) | cell
    key = jnp.where(is_live, key, jnp.int32(2**31 - 1)).reshape(total)
    live = jnp.sum(jnp.clip(lengths - me * slab, 0, slab)).reshape(1)

    high = 32
    hot_high = (cluster // high)[:, :, None] == jnp.arange(K // high, dtype=jnp.int32)
    hot_low = (cluster % high)[:, :, None] == jnp.arange(high, dtype=jnp.int32)
    counts = jnp.einsum(
        "ujh,ujl->uhl",
        (hot_high & is_live[:, :, None]).astype(jnp.bfloat16),
        hot_low.astype(jnp.bfloat16),
        preferred_element_type=jnp.float32,
    ).reshape(users, K)
    owned_counts = lax.psum_scatter(counts, "tm", scatter_dimension=1, tiled=True)

    other = lax.ppermute(item_table, "tm", [(i, i ^ 1) for i in range(n)])

    sorted_keys = lax.sort(key).reshape(total // LANES, LANES)
    cap_rows = cap // LANES
    key_rows = total // LANES
    buckets = pl.pallas_call(
        functools.partial(bucket_kernel, n, dest_shift, cell_bits, dummy),
        out_shape=jax.ShapeDtypeStruct((n, cap_rows, LANES), jnp.int32),
        in_specs=[
            pl.BlockSpec(memory_space=pltpu.SMEM),
            pl.BlockSpec(memory_space=pltpu.VMEM),
        ],
        out_specs=pl.BlockSpec(memory_space=pltpu.VMEM),
        scratch_shapes=[pltpu.VMEM((key_rows + -(-(cap_rows + 1) // 8) * 8, LANES), jnp.int32)],
    )(live, sorted_keys)
    requests = lax.all_to_all(buckets, "tm", split_axis=0, concat_axis=0, tiled=True)
    requests = requests.reshape(n, cap)

    cuts = []
    for lo, size in chains:
        half = size * (K // 4)
        cuts += [(lo * K, half * 2), (lo * K + half * 2, half * 2)]
    sums_rows = -(-(cells + 1) * 2 // 256) * 256
    partials = pl.pallas_call(
        functools.partial(add_kernel, n, cap, cell_bits, dummy, cuts),
        out_shape=[jax.ShapeDtypeStruct((size, LANES), jnp.float32) for _, size in cuts],
        in_specs=[
            pl.BlockSpec(memory_space=pltpu.SMEM),
            pl.BlockSpec(memory_space=pltpu.VMEM),
            pl.BlockSpec(memory_space=pltpu.VMEM),
        ],
        out_specs=[pl.BlockSpec(memory_space=pl.ANY)] * len(cuts),
        scratch_shapes=[
            pltpu.VMEM((rows * 4, LANES), jnp.float32),
            pltpu.VMEM((sums_rows, LANES), jnp.float32),
            pltpu.SemaphoreType.DMA((len(cuts),)),
        ],
        compiler_params=pltpu.CompilerParams(vmem_limit_bytes=40 * 1024 * 1024),
    )(requests, item_table, other)

    keep = list(partials[0::2])
    send = list(partials[1::2])
    for stage in range(m):
        got = []
        for g in range(len(chains)):
            bit = 2 << ((g + stage) % m)
            got.append(lax.ppermute(send[g], "tm", [(i, i ^ bit) for i in range(n)]))
        for g in range(len(chains)):
            half = keep[g].shape[0] // 2
            if stage < m - 1:
                send[g] = keep[g][half:] + got[g][half:]
                keep[g] = keep[g][:half] + got[g][:half]
            else:
                keep[g] = keep[g] + got[g]
    sums = jnp.concatenate(
        [part.reshape(size, owned, width) for part, (_, size) in zip(keep, chains)], axis=0
    )
    return sums / jnp.maximum(owned_counts, 1.0)[..., None]


def solution(mesh):
    return jax.shard_map(
        per_device,
        mesh=mesh,
        in_specs=(
            P("tm", None),
            P("tm", ("groups", "users"), None, None),
            P("tm", ("groups", "users"), None),
            P("tm", ("groups", "users"), None),
            P(("groups", "users")),
        ),
        out_specs=P(("groups", "users"), "tm", None),
        check_vma=False,
    )
```

```python
import functools

import jax
import jax.numpy as jnp
from jax import lax
from jax.experimental import pallas as pl
from jax.experimental.pallas import tpu as pltpu
from jax.sharding import PartitionSpec as P

K = 1024
LANES = 128
SUB = 8
GROUP = 16
FLAG = 1 << 30
NONE = 2**31 - 1
SLOTS = 4


def bits_for(count):
    return (count - 1).bit_length()


def user_chains(users):
    third = -(-users * 3 // 8)
    cuts = sorted({0, min(third, users), min(2 * third, users), users})
    return [(lo, hi - lo) for lo, hi in zip(cuts[:-1], cuts[1:])]


def sort_tiles(tiles):
    count = len(tiles)
    tile_bits = bits_for(count)
    sub = lax.broadcasted_iota(jnp.int32, (SUB, LANES), 0)
    lane = lax.broadcasted_iota(jnp.int32, (SUB, LANES), 1)
    total_bits = tile_bits + 3 + 7

    def bit_mask(bit):
        if bit < tile_bits + 3:
            return ((sub >> (bit - tile_bits)) & 1) == 1
        return ((lane >> (bit - tile_bits - 3)) & 1) == 1

    masks = {b: bit_mask(b) for b in range(tile_bits, total_bits)}
    flips = {b: jnp.where(masks[b], -1, 0) for b in masks}

    def flip(t, phase):
        if phase >= total_bits:
            return 0
        if phase < tile_bits:
            return -1 if (t >> phase) & 1 else 0
        return flips[phase]

    for phase in range(1, total_bits + 1):
        changed = []
        for t in range(count):
            old = flip(t, phase - 1) if phase > 1 else 0
            new = flip(t, phase)
            if isinstance(old, int) and isinstance(new, int):
                turn = old ^ new
                changed.append(tiles[t] if turn == 0 else ~tiles[t])
            else:
                changed.append(tiles[t] ^ (old ^ new))
        tiles = changed
        for bit in reversed(range(phase)):
            if bit < tile_bits:
                step = 1 << bit
                tiles = list(tiles)
                for t in range(count):
                    if not t & step:
                        a, b = tiles[t], tiles[t | step]
                        tiles[t], tiles[t | step] = jnp.minimum(a, b), jnp.maximum(a, b)
                continue
            if bit < tile_bits + 3:
                axis, step, size = 0, 1 << (bit - tile_bits), SUB
            else:
                axis, step, size = 1, 1 << (bit - tile_bits - 3), LANES
            upper = masks[bit]
            moved = []
            for x in tiles:
                down = pltpu.roll(x, step, axis=axis)
                if 2 * step == size:
                    other = down
                else:
                    other = jnp.where(upper, down, pltpu.roll(x, size - step, axis=axis))
                moved.append(
                    jnp.where(upper, jnp.maximum(x, other), jnp.minimum(x, other))
                )
            tiles = moved
    return tiles


def prepare_kernel(
    n, owned, table_rows, dest_shift, cell_bits, cap_rows, count_rows, dummy, chains,
    scalars_ref, shard_ref, row_ref, cluster_ref, out_ref, order, pad,
):
    users, slab = shard_ref.shape
    m = bits_for(n) - 1
    sub = lax.broadcasted_iota(jnp.int32, (SUB, LANES), 0)
    lane = lax.broadcasted_iota(jnp.int32, (SUB, LANES), 1)
    me = scalars_ref[users]
    length = jnp.zeros((SUB, LANES), jnp.int32)
    live_total = jnp.int32(0)
    for u in range(users):
        length = jnp.where(sub == u, scalars_ref[u], length)
        live_total += jnp.clip(scalars_ref[u] - me * slab, 0, slab)
    length = length - me * slab

    base = jnp.zeros((SUB, LANES), jnp.int32)
    in_chain = jnp.zeros((SUB, LANES), jnp.int32)
    chain_size = jnp.zeros((SUB, LANES), jnp.int32)
    chain_at = []
    for lo, size in chains:
        inside = (sub >= lo) & (sub < lo + size)
        base = jnp.where(inside, lo * (K // 2), base)
        in_chain = jnp.where(inside, sub - lo, in_chain)
        chain_size = jnp.where(inside, size, chain_size)
        chain_at.append(inside)

    owner_shift = bits_for(owned)
    tiles = []
    hot_owner = [[] for _ in range(count_rows)]
    hot_slot = [[] for _ in range(count_rows)]
    per_row = LANES // owned
    owner_iota = lax.broadcasted_iota(jnp.int32, (n, LANES), 0)
    slot_iota = lax.broadcasted_iota(jnp.int32, (LANES, LANES), 0)
    for j in range(slab // LANES):
        at = pl.ds(j * LANES, LANES)
        shard, row, cluster = shard_ref[:, at], row_ref[:, at], cluster_ref[:, at]
        owner = lax.shift_right_logical(cluster, owner_shift)
        low = cluster & (owned - 1)
        live = lane + j * LANES < length
        dest = (shard & ~1) | (owner & 1)
        away = lax.shift_right_logical(owner ^ dest, 1)
        spread = jnp.zeros((SUB, LANES), jnp.int32)
        for g in range(len(chains)):
            turned = jnp.zeros((SUB, LANES), jnp.int32)
            for k in range(m):
                turned = turned * 2 + ((away >> ((g + k) % m)) & 1)
            spread = jnp.where(chain_at[g], turned, spread)
        cell = base + ((spread * chain_size + in_chain) << owner_shift) + low
        there = ((shard ^ owner) & 1) * table_rows + row
        key = (dest << dest_shift) | (there << cell_bits) | cell
        tiles.append(jnp.where(live, key, NONE))
        live_owner = jnp.where(live, owner, -1)
        for u in range(users):
            r = u // per_row
            hot_owner[r].append((owner_iota == live_owner[u : u + 1, :]).astype(jnp.bfloat16))
            target = low[u : u + 1, :] + (u % per_row) * owned
            hot_slot[r].append((slot_iota == target).astype(jnp.bfloat16))

    for r in range(count_rows):
        counts = jnp.zeros((n, LANES), jnp.float32)
        for a, b in zip(hot_owner[r], hot_slot[r]):
            counts += lax.dot_general(
                a, b, (((1,), (1,)), ((), ())), preferred_element_type=jnp.float32
            )
        counts = counts.astype(jnp.int32)
        for d in range(n):
            out_ref[d, pl.ds(cap_rows + r, 1), :] = counts[d : d + 1, :]

    ends = []
    for d in range(n - 1):
        below = jnp.zeros((SUB, LANES), jnp.float32)
        for x in tiles:
            below += (x < ((d + 1) << dest_shift)).astype(jnp.float32)
        ends.append(jnp.sum(below).astype(jnp.int32))
    ends.append(live_total)

    empty = jnp.full((SUB, LANES), NONE, jnp.int32)
    tiles = sort_tiles(tiles + [empty] * ((1 << bits_for(len(tiles))) - len(tiles)))
    count = len(tiles)
    for t, x in enumerate(tiles):
        order[pl.ds(t * SUB, SUB), :] = x
    lines = [order[pl.ds(s, count, stride=SUB), :] for s in range(SUB)]
    straight = jnp.concatenate(lines, axis=0).T
    pad[0:LANES, :] = straight
    pad[LANES:, :] = jnp.full((pad.shape[0] - LANES, LANES), NONE, jnp.int32)

    lane = lax.broadcasted_iota(jnp.int32, (cap_rows, LANES), 1)
    slot = lax.broadcasted_iota(jnp.int32, (cap_rows, LANES), 0) * LANES + lane
    in_group = lane % GROUP
    start = jnp.int32(0)
    for d in range(n):
        count = ends[d] - start
        first = lax.shift_right_logical(start, 7)
        off = start & (LANES - 1)
        block = pad[pl.ds(first, cap_rows + 1), :]
        turned = pltpu.roll(block, (LANES - off) & (LANES - 1), axis=1)
        mine = jnp.where(lane < LANES - off, turned[:cap_rows], turned[1:])
        cell = mine & ((1 << cell_bits) - 1)
        there = lax.shift_right_logical(mine, cell_bits) & (2 * table_rows - 1)
        code = jnp.where(slot < count, (there << (cell_bits + 1)) | cell, dummy)
        cell = code & ((2 << cell_bits) - 1)
        twice = jnp.zeros((cap_rows, LANES), jnp.int32)
        for back in range(1, GROUP):
            same = (pltpu.roll(cell, back, axis=1) == cell) & (in_group >= back)
            twice = jnp.where(same, 1, twice)
        twice = jnp.where(code == dummy, 0, twice)
        step = 1
        while step < GROUP:
            twice = twice | pltpu.roll(twice, LANES - step, axis=1)
            step *= 2
        flagged = (in_group == 0) & (twice > 0)
        out_ref[d, pl.ds(0, cap_rows), :] = jnp.where(flagged, code | FLAG, code)
        start = ends[d]


def add_kernel(n, cap_rows, cell_bits, dummy, cuts, request_ref, own_ref, other_ref, *rest):
    out_refs = rest[: len(cuts)]
    table, sums, lists, list_sems, sems = rest[len(cuts) :]
    rows = own_ref.shape[0]
    block = 128

    def read(s):
        slot = lax.rem(s, SLOTS)
        return pltpu.make_async_copy(
            request_ref.at[s, pl.ds(0, cap_rows), :], lists.at[slot], list_sems.at[slot]
        )

    for s in range(SLOTS - 1):
        read(s).start()

    def widen(i, _):
        for part, ref in enumerate((own_ref, other_ref)):
            x = ref[pl.ds(i * block, block), :].astype(jnp.float32)
            at = pl.ds(part * rows + i * block, block)
            table[at, 0, :] = x[:, :LANES]
            table[at, 1, :] = x[:, LANES:]
        return 0

    lax.fori_loop(0, rows // block, widen, 0)

    def clear(i, _):
        sums[pl.ds(i * 128, 128)] = jnp.zeros((128, 2, LANES), jnp.float32)
        return 0

    lax.fori_loop(0, sums.shape[0] // 128, clear, 0)
    low = (2 << cell_bits) - 1

    def place(code, first):
        if first:
            code = code & (FLAG - 1)
        return code & low, lax.shift_right_logical(code, cell_bits + 1)

    steps_per_row = LANES // GROUP

    def source(s, _):
        slot = lax.rem(s, SLOTS)

        @pl.when(s + SLOTS - 1 < n)
        def _():
            read(s + SLOTS - 1).start()

        read(s).wait()

        def head(i):
            i = jnp.minimum(i, cap_rows * steps_per_row - 1)
            return lists[slot, lax.shift_right_logical(i, 3), (i & 7) * GROUP]

        def more(i):
            return (i < cap_rows * steps_per_row) & (head(i) != dummy)

        def step(i):
            r = lax.shift_right_logical(i, 3)
            at = (i & 7) * GROUP
            codes = [lists[slot, r, at + k] for k in range(GROUP)]
            places = [place(c, k == 0) for k, c in enumerate(codes)]

            @pl.when(codes[0] < FLAG)
            def _():
                new = [sums[c] + table[r] for c, r in places]
                for (c, _), v in zip(places, new):
                    sums[c] = v

            @pl.when(codes[0] >= FLAG)
            def _():
                for c, r in places:
                    sums[c] = sums[c] + table[r]

            return i + 1

        lax.while_loop(more, step, jnp.int32(0))
        return 0

    lax.fori_loop(0, n, source, 0)
    copies = [
        pltpu.make_async_copy(sums.at[pl.ds(at, size)], ref, sems.at[k])
        for k, ((at, size), ref) in enumerate(zip(cuts, out_refs))
    ]
    for copy in copies:
        copy.start()
    for copy in copies:
        copy.wait()


def per_device(item_table, item_shard, item_row, cluster_id, lengths):
    n = lax.axis_size("tm")
    me = lax.axis_index("tm")
    users, slab = item_row.shape[1:]
    rows, width = item_table.shape
    total = users * slab
    owned = K // n
    m = bits_for(n) - 1
    cells = users * K // 2
    cell_bits = bits_for(cells)
    dest_shift = cell_bits + bits_for(2 * rows)
    cap_rows = -(-4 * total // n // LANES)
    count_rows = users * owned // LANES
    block_rows = -(-(cap_rows + count_rows) // SUB) * SUB
    chains = user_chains(users)
    dummy = cells

    other = lax.ppermute(item_table, "tm", [(i, i ^ 1) for i in range(n)])
    scalars = jnp.concatenate([lengths, me.astype(jnp.int32).reshape(1)])
    buckets = pl.pallas_call(
        functools.partial(
            prepare_kernel, n, owned, rows, dest_shift, cell_bits, cap_rows, count_rows, dummy,
            chains,
        ),
        out_shape=jax.ShapeDtypeStruct((n, block_rows, LANES), jnp.int32),
        in_specs=[pl.BlockSpec(memory_space=pltpu.SMEM)]
        + [pl.BlockSpec(memory_space=pltpu.VMEM)] * 3,
        out_specs=pl.BlockSpec(memory_space=pltpu.VMEM),
        scratch_shapes=[
            pltpu.VMEM((LANES, LANES), jnp.int32),
            pltpu.VMEM((LANES + -(-(cap_rows + 1) // SUB) * SUB, LANES), jnp.int32),
        ],
    )(
        scalars,
        item_shard.reshape(users, slab),
        item_row.reshape(users, slab),
        cluster_id.reshape(users, slab),
    )
    requests = lax.all_to_all(buckets, "tm", split_axis=0, concat_axis=0, tiled=True)
    counts = jnp.sum(requests[:, cap_rows : cap_rows + count_rows, :], axis=0)
    counts = counts.reshape(users, owned).astype(jnp.float32)

    cuts = []
    for lo, size in chains:
        half = size * (K // 4)
        cuts += [(lo * K // 2, half), (lo * K // 2 + half, half)]
    sums_rows = -(-(cells + 1) // 128) * 128
    partials = pl.pallas_call(
        functools.partial(add_kernel, n, cap_rows, cell_bits, dummy, cuts),
        out_shape=[jax.ShapeDtypeStruct((size, 2, LANES), jnp.float32) for _, size in cuts],
        in_specs=[
            pl.BlockSpec(memory_space=pl.ANY),
            pl.BlockSpec(memory_space=pltpu.VMEM),
            pl.BlockSpec(memory_space=pltpu.VMEM),
        ],
        out_specs=[pl.BlockSpec(memory_space=pl.ANY)] * len(cuts),
        scratch_shapes=[
            pltpu.VMEM((rows * 2, 2, LANES), jnp.float32),
            pltpu.VMEM((sums_rows, 2, LANES), jnp.float32),
            pltpu.SMEM((SLOTS, cap_rows, LANES), jnp.int32),
            pltpu.SemaphoreType.DMA((SLOTS,)),
            pltpu.SemaphoreType.DMA((len(cuts),)),
        ],
        compiler_params=pltpu.CompilerParams(vmem_limit_bytes=40 * 1024 * 1024),
    )(requests, item_table, other)

    keep = list(partials[0::2])
    send = list(partials[1::2])
    for stage in range(m):
        got = []
        for g in range(len(chains)):
            bit = 2 << ((g + stage) % m)
            got.append(lax.ppermute(send[g], "tm", [(i, i ^ bit) for i in range(n)]))
        for g in range(len(chains)):
            half = keep[g].shape[0] // 2
            if stage < m - 1:
                send[g] = keep[g][half:] + got[g][half:]
                keep[g] = keep[g][:half] + got[g][:half]
            else:
                keep[g] = keep[g] + got[g]
    sums = jnp.concatenate(
        [part.reshape(size, owned, width) for part, (_, size) in zip(keep, chains)], axis=0
    )
    return sums / jnp.maximum(counts, 1.0)[..., None]


def solution(mesh):
    return jax.shard_map(
        per_device,
        mesh=mesh,
        in_specs=(
            P("tm", None),
            P("tm", ("groups", "users"), None, None),
            P("tm", ("groups", "users"), None),
            P("tm", ("groups", "users"), None),
            P(("groups", "users")),
        ),
        out_specs=P(("groups", "users"), "tm", None),
        check_vma=False,
    )
```

```python
import functools

import jax
import jax.numpy as jnp
from jax import lax
from jax.experimental import pallas as pl
from jax.experimental.pallas import tpu as pltpu
from jax.sharding import PartitionSpec as P

K = 1024
LANES = 128
SUB = 8
GROUP = 16
FLAG = 1 << 30
NONE = 2**31 - 1
SLOTS = 4


def bits_for(count):
    return (count - 1).bit_length()


def user_chains(users):
    third = -(-users * 3 // 8)
    cuts = sorted({0, min(third, users), min(2 * third, users), users})
    return [(lo, hi - lo) for lo, hi in zip(cuts[:-1], cuts[1:])]


def sort_tiles(tiles):
    count = len(tiles)
    tile_bits = bits_for(count)
    sub = lax.broadcasted_iota(jnp.int32, (SUB, LANES), 0)
    lane = lax.broadcasted_iota(jnp.int32, (SUB, LANES), 1)
    total_bits = tile_bits + 3 + 7

    def bit_mask(bit):
        if bit < tile_bits + 3:
            return ((sub >> (bit - tile_bits)) & 1) == 1
        return ((lane >> (bit - tile_bits - 3)) & 1) == 1

    masks = {b: bit_mask(b) for b in range(tile_bits, total_bits)}
    flips = {b: jnp.where(masks[b], -1, 0) for b in masks}

    def flip(t, phase):
        if phase >= total_bits:
            return 0
        if phase < tile_bits:
            return -1 if (t >> phase) & 1 else 0
        return flips[phase]

    for phase in range(1, total_bits + 1):
        changed = []
        for t in range(count):
            old = flip(t, phase - 1) if phase > 1 else 0
            new = flip(t, phase)
            if isinstance(old, int) and isinstance(new, int):
                turn = old ^ new
                changed.append(tiles[t] if turn == 0 else ~tiles[t])
            else:
                changed.append(tiles[t] ^ (old ^ new))
        tiles = changed
        for bit in reversed(range(phase)):
            if bit < tile_bits:
                step = 1 << bit
                tiles = list(tiles)
                for t in range(count):
                    if not t & step:
                        a, b = tiles[t], tiles[t | step]
                        tiles[t], tiles[t | step] = jnp.minimum(a, b), jnp.maximum(a, b)
                continue
            if bit < tile_bits + 3:
                axis, step, size = 0, 1 << (bit - tile_bits), SUB
            else:
                axis, step, size = 1, 1 << (bit - tile_bits - 3), LANES
            upper = masks[bit]
            moved = []
            for x in tiles:
                down = pltpu.roll(x, step, axis=axis)
                if 2 * step == size:
                    other = down
                else:
                    other = jnp.where(upper, down, pltpu.roll(x, size - step, axis=axis))
                moved.append(
                    jnp.where(upper, jnp.maximum(x, other), jnp.minimum(x, other))
                )
            tiles = moved
    return tiles


def prepare_kernel(
    n, owned, table_rows, dest_shift, row_bits, cell_bits, cap_rows, count_rows, dummy, chains,
    scalars_ref, shard_ref, row_ref, cluster_ref, out_ref, order, pad,
):
    users, slab = shard_ref.shape
    m = bits_for(n) - 1
    sub = lax.broadcasted_iota(jnp.int32, (SUB, LANES), 0)
    lane = lax.broadcasted_iota(jnp.int32, (SUB, LANES), 1)
    me = scalars_ref[users]
    length = jnp.zeros((SUB, LANES), jnp.int32)
    live_total = jnp.int32(0)
    for u in range(users):
        length = jnp.where(sub == u, scalars_ref[u], length)
        live_total += jnp.clip(scalars_ref[u] - me * slab, 0, slab)
    length = length - me * slab

    base = jnp.zeros((SUB, LANES), jnp.int32)
    in_chain = jnp.zeros((SUB, LANES), jnp.int32)
    chain_size = jnp.zeros((SUB, LANES), jnp.int32)
    chain_at = []
    for lo, size in chains:
        inside = (sub >= lo) & (sub < lo + size)
        base = jnp.where(inside, lo * (K // 2), base)
        in_chain = jnp.where(inside, sub - lo, in_chain)
        chain_size = jnp.where(inside, size, chain_size)
        chain_at.append(inside)

    owner_shift = bits_for(owned)
    tiles = []
    hot_owner = [[] for _ in range(count_rows)]
    hot_slot = [[] for _ in range(count_rows)]
    per_row = LANES // owned
    owner_iota = lax.broadcasted_iota(jnp.int32, (n, LANES), 0)
    slot_iota = lax.broadcasted_iota(jnp.int32, (LANES, LANES), 0)
    for j in range(slab // LANES):
        at = pl.ds(j * LANES, LANES)
        shard, row, cluster = shard_ref[:, at], row_ref[:, at], cluster_ref[:, at]
        owner = lax.shift_right_logical(cluster, owner_shift)
        low = cluster & (owned - 1)
        live = lane + j * LANES < length
        dest = (shard & ~1) | (owner & 1)
        away = lax.shift_right_logical(owner ^ dest, 1)
        spread = jnp.zeros((SUB, LANES), jnp.int32)
        for g in range(len(chains)):
            turned = jnp.zeros((SUB, LANES), jnp.int32)
            for k in range(m):
                turned = turned * 2 + ((away >> ((g + k) % m)) & 1)
            spread = jnp.where(chain_at[g], turned, spread)
        cell = base + ((spread * chain_size + in_chain) << owner_shift) + low
        there = ((shard ^ owner) & 1) * table_rows + row
        key = (dest << dest_shift) | (cell << row_bits) | there
        tiles.append(jnp.where(live, key, NONE))
        live_owner = jnp.where(live, owner, -1)
        for u in range(users):
            r = u // per_row
            hot_owner[r].append((owner_iota == live_owner[u : u + 1, :]).astype(jnp.bfloat16))
            target = low[u : u + 1, :] + (u % per_row) * owned
            hot_slot[r].append((slot_iota == target).astype(jnp.bfloat16))

    for r in range(count_rows):
        counts = jnp.zeros((n, LANES), jnp.float32)
        for a, b in zip(hot_owner[r], hot_slot[r]):
            counts += lax.dot_general(
                a, b, (((1,), (1,)), ((), ())), preferred_element_type=jnp.float32
            )
        counts = counts.astype(jnp.int32)
        for d in range(n):
            out_ref[d, pl.ds(1 + cap_rows + r, 1), :] = counts[d : d + 1, :]

    ends = []
    for d in range(n - 1):
        below = jnp.zeros((SUB, LANES), jnp.float32)
        for x in tiles:
            below += (x < ((d + 1) << dest_shift)).astype(jnp.float32)
        ends.append(jnp.sum(below).astype(jnp.int32))
    ends.append(live_total)

    empty = jnp.full((SUB, LANES), NONE, jnp.int32)
    tiles = sort_tiles(tiles + [empty] * ((1 << bits_for(len(tiles))) - len(tiles)))
    count = len(tiles)
    for t, x in enumerate(tiles):
        order[pl.ds(t * SUB, SUB), :] = x
    lines = [order[pl.ds(s, count, stride=SUB), :] for s in range(SUB)]
    straight = jnp.concatenate(lines, axis=0).T
    pad[0:LANES, :] = straight
    pad[LANES:, :] = jnp.full((pad.shape[0] - LANES, LANES), NONE, jnp.int32)

    lane = lax.broadcasted_iota(jnp.int32, (cap_rows, LANES), 1)
    slot = lax.broadcasted_iota(jnp.int32, (cap_rows, LANES), 0) * LANES + lane
    nothing = jnp.full((1, LANES), dummy, jnp.int32)

    def ahead(x, by):
        turned = pltpu.roll(x, (LANES - by) & (LANES - 1), axis=1)
        return jnp.where(lane < LANES - by, turned[:cap_rows], turned[1:])

    start = jnp.int32(0)
    for d in range(n):
        count = ends[d] - start
        steps = lax.shift_right_logical(count + GROUP - 1, bits_for(GROUP))
        first = lax.shift_right_logical(start, bits_for(LANES))
        mine = ahead(pad[pl.ds(first, cap_rows + 1), :], start & (LANES - 1))
        there = mine & (2 * table_rows - 1)
        cell = lax.shift_right_logical(mine, row_bits) & ((1 << cell_bits) - 1)
        code = jnp.where(slot < count, (there << (cell_bits + 3)) | (cell << 1), dummy)
        cell = jnp.where(slot < count, cell, -1)
        later = ahead(jnp.concatenate([cell, nothing], axis=0), steps)
        twice = jnp.max(jnp.where((cell == later) & (cell >= 0), 1.0, 0.0))
        out_ref[d, pl.ds(1, cap_rows), :] = code
        head = steps | jnp.where(twice > 0, FLAG, 0)
        out_ref[d, pl.ds(0, 1), :] = jnp.full((1, LANES), head, jnp.int32)
        start = ends[d]


def add_kernel(n, stride, cell_bits, cuts, request_ref, own_ref, other_ref, *rest):
    out_refs = rest[: len(cuts)]
    table, sums, lists, list_sems, sems = rest[len(cuts) :]
    rows = own_ref.shape[0]
    block = 128

    def read(s):
        slot = lax.rem(s, SLOTS)
        return pltpu.make_async_copy(
            request_ref.at[pl.ds(pl.multiple_of(s * stride, stride), stride)],
            lists.at[pl.ds(pl.multiple_of(slot * stride, stride), stride)],
            list_sems.at[slot],
        )

    for s in range(SLOTS - 1):
        read(s).start()

    def widen(i, _):
        for part, ref in enumerate((own_ref, other_ref)):
            x = ref[pl.ds(i * block, block), :].astype(jnp.float32)
            at = (part * rows + i * block) * 2
            table[pl.ds(at, block, stride=2), :] = x[:, :LANES]
            table[pl.ds(at + 1, block, stride=2), :] = x[:, LANES:]
        return 0

    lax.fori_loop(0, rows // block, widen, 0)

    def clear(i, _):
        sums[pl.ds(i * 256, 256), :] = jnp.zeros((256, LANES), jnp.float32)
        return 0

    lax.fori_loop(0, sums.shape[0] // 256, clear, 0)
    low = (4 << cell_bits) - 1

    def cell_at(code):
        return pl.ds(pl.multiple_of(code & low, 2), 2)

    def row_at(code):
        return pl.ds(pl.multiple_of(lax.shift_right_logical(code, cell_bits + 2), 2), 2)

    def source(s, _):
        slot = lax.rem(s, SLOTS)

        @pl.when(s + SLOTS - 1 < n)
        def _():
            read(s + SLOTS - 1).start()

        read(s).wait()
        head = lists[slot * stride]
        steps = head & (FLAG - 1)
        begin = slot * stride + LANES

        @pl.when(head < FLAG)
        def _():
            def step(i, _):
                at = begin + i
                new = []
                for k in range(GROUP):
                    code = lists[at]
                    new.append((code, sums[cell_at(code), :] + table[row_at(code), :]))
                    at = at + steps
                for code, value in new:
                    sums[cell_at(code), :] = value
                return 0

            lax.fori_loop(0, steps, step, 0)

        @pl.when(head >= FLAG)
        def _():
            def step(i, _):
                code = lists[begin + i]
                sums[cell_at(code), :] = sums[cell_at(code), :] + table[row_at(code), :]
                return 0

            lax.fori_loop(0, steps * GROUP, step, 0)

        return 0

    lax.fori_loop(0, n, source, 0)
    copies = [
        pltpu.make_async_copy(sums.at[pl.ds(at, size), :], ref, sems.at[k])
        for k, ((at, size), ref) in enumerate(zip(cuts, out_refs))
    ]
    for copy in copies:
        copy.start()
    for copy in copies:
        copy.wait()


def per_device(item_table, item_shard, item_row, cluster_id, lengths):
    n = lax.axis_size("tm")
    me = lax.axis_index("tm")
    users, slab = item_row.shape[1:]
    rows, width = item_table.shape
    total = users * slab
    owned = K // n
    m = bits_for(n) - 1
    cells = users * K // 2
    cell_bits = bits_for(cells)
    row_bits = bits_for(2 * rows)
    dest_shift = cell_bits + row_bits
    cap_rows = -(-4 * total // n // LANES)
    count_rows = users * owned // LANES
    block_rows = -(-(1 + cap_rows + count_rows) // SUB) * SUB
    chains = user_chains(users)
    dummy = cells * 2

    other = lax.ppermute(item_table, "tm", [(i, i ^ 1) for i in range(n)])
    scalars = jnp.concatenate([lengths, me.astype(jnp.int32).reshape(1)])
    buckets = pl.pallas_call(
        functools.partial(
            prepare_kernel, n, owned, rows, dest_shift, row_bits, cell_bits, cap_rows, count_rows, dummy,
            chains,
        ),
        out_shape=jax.ShapeDtypeStruct((n, block_rows, LANES), jnp.int32),
        in_specs=[pl.BlockSpec(memory_space=pltpu.SMEM)]
        + [pl.BlockSpec(memory_space=pltpu.VMEM)] * 3,
        out_specs=pl.BlockSpec(memory_space=pltpu.VMEM),
        scratch_shapes=[
            pltpu.VMEM((LANES, LANES), jnp.int32),
            pltpu.VMEM((LANES + -(-(cap_rows + 1) // SUB) * SUB, LANES), jnp.int32),
        ],
    )(
        scalars,
        item_shard.reshape(users, slab),
        item_row.reshape(users, slab),
        cluster_id.reshape(users, slab),
    )
    requests = lax.all_to_all(buckets, "tm", split_axis=0, concat_axis=0, tiled=True)
    counts = jnp.sum(requests[:, 1 + cap_rows : 1 + cap_rows + count_rows, :], axis=0)
    counts = counts.reshape(users, owned).astype(jnp.float32)

    cuts = []
    for lo, size in chains:
        half = size * (K // 2)
        cuts += [(lo * K, half), (lo * K + half, half)]
    sums_rows = -(-(cells + 1) * 2 // 256) * 256
    partials = pl.pallas_call(
        functools.partial(add_kernel, n, block_rows * LANES, cell_bits, cuts),
        out_shape=[jax.ShapeDtypeStruct((size, LANES), jnp.float32) for _, size in cuts],
        in_specs=[
            pl.BlockSpec(memory_space=pl.ANY),
            pl.BlockSpec(memory_space=pltpu.VMEM),
            pl.BlockSpec(memory_space=pltpu.VMEM),
        ],
        out_specs=[pl.BlockSpec(memory_space=pl.ANY)] * len(cuts),
        scratch_shapes=[
            pltpu.VMEM((rows * 4, LANES), jnp.float32),
            pltpu.VMEM((sums_rows, LANES), jnp.float32),
            pltpu.SMEM((SLOTS * block_rows * LANES,), jnp.int32),
            pltpu.SemaphoreType.DMA((SLOTS,)),
            pltpu.SemaphoreType.DMA((len(cuts),)),
        ],
        compiler_params=pltpu.CompilerParams(vmem_limit_bytes=40 * 1024 * 1024),
    )(requests.reshape(-1), item_table, other)

    keep = list(partials[0::2])
    send = list(partials[1::2])
    for stage in range(m):
        got = []
        for g in range(len(chains)):
            bit = 2 << ((g + stage) % m)
            got.append(lax.ppermute(send[g], "tm", [(i, i ^ bit) for i in range(n)]))
        for g in range(len(chains)):
            half = keep[g].shape[0] // 2
            if stage < m - 1:
                send[g] = keep[g][half:] + got[g][half:]
                keep[g] = keep[g][:half] + got[g][:half]
            else:
                keep[g] = keep[g] + got[g]
    sums = jnp.concatenate(
        [part.reshape(size, owned, width) for part, (_, size) in zip(keep, chains)], axis=0
    )
    return sums / jnp.maximum(counts, 1.0)[..., None]


def solution(mesh):
    return jax.shard_map(
        per_device,
        mesh=mesh,
        in_specs=(
            P("tm", None),
            P("tm", ("groups", "users"), None, None),
            P("tm", ("groups", "users"), None),
            P("tm", ("groups", "users"), None),
            P(("groups", "users")),
        ),
        out_specs=P(("groups", "users"), "tm", None),
        check_vma=False,
    )
```

```python
import functools

import jax
import jax.numpy as jnp
from jax import lax
from jax.experimental import pallas as pl
from jax.experimental.pallas import tpu as pltpu
from jax.sharding import PartitionSpec as P

K = 1024
LANES = 128
SUB = 8
GROUP = 16
FLAG = 1 << 30
NONE = 2**31 - 1
SLOTS = 4
NEAR = 512


def bits_for(count):
    return (count - 1).bit_length()


def user_groups(users, m):
    turn = lambda k: tuple((k + i) % m for i in range(m))
    if users < 8:
        return [[(0, users, turn(0))]]
    more = users - 8
    return [
        [(0, 2, turn(0)), (2, 1, turn(1))],
        [(3, 2, turn(2)), (5, 1, turn(0))],
        [(6, 1, turn(1)), (7, 1 + more, turn(2))],
    ]


def stages_of(bits):
    return [[bit] for bit in bits[:-2]] + [list(bits[-2:])]


def sort_tiles(tiles):
    count = len(tiles)
    tile_bits = bits_for(count)
    sub = lax.broadcasted_iota(jnp.int32, (SUB, LANES), 0)
    lane = lax.broadcasted_iota(jnp.int32, (SUB, LANES), 1)
    total_bits = tile_bits + 3 + 7

    def bit_mask(bit):
        if bit < tile_bits + 3:
            return ((sub >> (bit - tile_bits)) & 1) == 1
        return ((lane >> (bit - tile_bits - 3)) & 1) == 1

    masks = {b: bit_mask(b) for b in range(tile_bits, total_bits)}
    flips = {b: jnp.where(masks[b], -1, 0) for b in masks}

    def flip(t, phase):
        if phase >= total_bits:
            return 0
        if phase < tile_bits:
            return -1 if (t >> phase) & 1 else 0
        return flips[phase]

    for phase in range(1, total_bits + 1):
        changed = []
        for t in range(count):
            old = flip(t, phase - 1) if phase > 1 else 0
            new = flip(t, phase)
            if isinstance(old, int) and isinstance(new, int):
                turn = old ^ new
                changed.append(tiles[t] if turn == 0 else ~tiles[t])
            else:
                changed.append(tiles[t] ^ (old ^ new))
        tiles = changed
        for bit in reversed(range(phase)):
            if bit < tile_bits:
                step = 1 << bit
                tiles = list(tiles)
                for t in range(count):
                    if not t & step:
                        a, b = tiles[t], tiles[t | step]
                        tiles[t], tiles[t | step] = jnp.minimum(a, b), jnp.maximum(a, b)
                continue
            if bit < tile_bits + 3:
                axis, step, size = 0, 1 << (bit - tile_bits), SUB
            else:
                axis, step, size = 1, 1 << (bit - tile_bits - 3), LANES
            upper = masks[bit]
            moved = []
            for x in tiles:
                down = pltpu.roll(x, step, axis=axis)
                if 2 * step == size:
                    other = down
                else:
                    other = jnp.where(upper, down, pltpu.roll(x, size - step, axis=axis))
                moved.append(
                    jnp.where(upper, jnp.maximum(x, other), jnp.minimum(x, other))
                )
            tiles = moved
    return tiles


def prepare_kernel(
    n, owned, table_rows, dest_shift, row_bits, cell_bits, req_rows, count_rows, dummy, groups,
    scalars_ref, shard_ref, row_ref, cluster_ref, out_ref, order, pad,
):
    users, slab = shard_ref.shape
    sub = lax.broadcasted_iota(jnp.int32, (SUB, LANES), 0)
    lane = lax.broadcasted_iota(jnp.int32, (SUB, LANES), 1)
    me = scalars_ref[users]
    length = jnp.zeros((SUB, LANES), jnp.int32)
    live_total = jnp.int32(0)
    for u in range(users):
        length = jnp.where(sub == u, scalars_ref[u], length)
        live_total += jnp.clip(scalars_ref[u] - me * slab, 0, slab)
    length = length - me * slab

    base = jnp.zeros((SUB, LANES), jnp.int32)
    in_chain = jnp.zeros((SUB, LANES), jnp.int32)
    chain_size = jnp.zeros((SUB, LANES), jnp.int32)
    chain_at = []
    chains = [chain for group in groups for chain in group]
    for lo, size, _ in chains:
        inside = (sub >= lo) & (sub < lo + size)
        base = jnp.where(inside, lo * (K // 2), base)
        in_chain = jnp.where(inside, sub - lo, in_chain)
        chain_size = jnp.where(inside, size, chain_size)
        chain_at.append(inside)

    owner_shift = bits_for(owned)
    tiles = []
    hot_owner = [[] for _ in range(count_rows)]
    hot_slot = [[] for _ in range(count_rows)]
    per_row = LANES // owned
    owner_iota = lax.broadcasted_iota(jnp.int32, (n, LANES), 0)
    slot_iota = lax.broadcasted_iota(jnp.int32, (LANES, LANES), 0)
    for j in range(slab // LANES):
        at = pl.ds(j * LANES, LANES)
        shard, row, cluster = shard_ref[:, at], row_ref[:, at], cluster_ref[:, at]
        owner = lax.shift_right_logical(cluster, owner_shift)
        low = cluster & (owned - 1)
        live = lane + j * LANES < length
        dest = (shard & ~1) | (owner & 1)
        away = lax.shift_right_logical(owner ^ dest, 1)
        spread = jnp.zeros((SUB, LANES), jnp.int32)
        by_order = {}
        for (_, _, bits), inside in zip(chains, chain_at):
            if bits not in by_order:
                turned = jnp.zeros((SUB, LANES), jnp.int32)
                for bit in bits:
                    turned = turned * 2 + ((away >> bit) & 1)
                by_order[bits] = turned
            spread = jnp.where(inside, by_order[bits], spread)
        cell = base + ((spread * chain_size + in_chain) << owner_shift) + low
        there = ((shard ^ owner) & 1) * table_rows + row
        key = (dest << dest_shift) | (cell << row_bits) | there
        tiles.append(jnp.where(live, key, NONE))
        live_owner = jnp.where(live, owner, -1)
        for u in range(users):
            r = u // per_row
            hot_owner[r].append((owner_iota == live_owner[u : u + 1, :]).astype(jnp.bfloat16))
            target = low[u : u + 1, :] + (u % per_row) * owned
            hot_slot[r].append((slot_iota == target).astype(jnp.bfloat16))

    for r in range(count_rows):
        counts = jnp.zeros((n, LANES), jnp.float32)
        for a, b in zip(hot_owner[r], hot_slot[r]):
            counts += lax.dot_general(
                a, b, (((1,), (1,)), ((), ())), preferred_element_type=jnp.float32
            )
        counts = counts.astype(jnp.int32)
        for d in range(n):
            out_ref[d, pl.ds(1 + req_rows + r, 1), :] = counts[d : d + 1, :]

    ends = []
    for d in range(n):
        for g in range(len(groups)):
            if g + 1 < len(groups):
                limit = (d << dest_shift) + ((groups[g + 1][0][0] * (K // 2)) << row_bits)
            elif d + 1 < n:
                limit = (d + 1) << dest_shift
            else:
                ends.append(live_total)
                continue
            below = jnp.zeros((SUB, LANES), jnp.float32)
            for x in tiles:
                below += (x < limit).astype(jnp.float32)
            ends.append(jnp.sum(below).astype(jnp.int32))

    empty = jnp.full((SUB, LANES), NONE, jnp.int32)
    tiles = sort_tiles(tiles + [empty] * ((1 << bits_for(len(tiles))) - len(tiles)))
    count = len(tiles)
    for t, x in enumerate(tiles):
        order[pl.ds(t * SUB, SUB), :] = x
    lines = [order[pl.ds(s, count, stride=SUB), :] for s in range(SUB)]
    straight = jnp.concatenate(lines, axis=0).T
    pad[0:LANES, :] = straight
    pad[LANES:, :] = jnp.full((pad.shape[0] - LANES, LANES), NONE, jnp.int32)

    lane = lax.broadcasted_iota(jnp.int32, (req_rows, LANES), 1)
    slot = lax.broadcasted_iota(jnp.int32, (req_rows, LANES), 0) * LANES + lane
    head_lane = lax.broadcasted_iota(jnp.int32, (1, LANES), 1)
    nothing = jnp.full((1, LANES), -1, jnp.int32)

    def ahead(x, by):
        turned = pltpu.roll(x, (LANES - by) & (LANES - 1), axis=1)
        return jnp.where(lane < LANES - by, turned[:req_rows], turned[1:])

    start = jnp.int32(0)
    for d in range(n):
        mine_ends = ends[d * len(groups) : (d + 1) * len(groups)]
        count = mine_ends[-1] - start
        first = lax.shift_right_logical(start, bits_for(LANES))
        mine = ahead(pad[pl.ds(first, req_rows + 1), :], start & (LANES - 1))
        there = mine & (2 * table_rows - 1)
        cell = lax.shift_right_logical(mine, row_bits) & ((1 << cell_bits) - 1)
        code = jnp.where(slot < count, (there << (cell_bits + 3)) | (cell << 1), dummy)
        cell = jnp.where(slot < count, cell, -1)
        out_ref[d, pl.ds(1, req_rows), :] = code
        cells = jnp.concatenate([cell, nothing], axis=0)
        head = jnp.zeros((1, LANES), jnp.int32)
        begin = jnp.int32(0)
        for g, end in enumerate(mine_ends):
            end = end - start
            steps = lax.shift_right_logical(end - begin + GROUP - 1, bits_for(GROUP))
            same = (cell == ahead(cells, steps)) & (slot >= begin) & (slot < end)
            twice = jnp.max(same.astype(jnp.float32))
            head = jnp.where(head_lane == 2 * g, begin, head)
            head = jnp.where(
                head_lane == 2 * g + 1, steps | jnp.where(twice > 0, FLAG, 0), head
            )
            begin = end
        out_ref[d, pl.ds(0, 1), :] = head
        start = mine_ends[-1]


def widen_kernel(own_ref, other_ref, table):
    rows = own_ref.shape[0]
    block = 128

    def widen(i, _):
        for part, ref in enumerate((own_ref, other_ref)):
            x = ref[pl.ds(i * block, block), :].astype(jnp.float32)
            at = (part * rows + i * block) * 2
            table[pl.ds(at, block, stride=2), :] = x[:, :LANES]
            table[pl.ds(at + 1, block, stride=2), :] = x[:, LANES:]
        return 0

    lax.fori_loop(0, rows // block, widen, 0)


def add_kernel(n, stride, cell_bits, group, cuts, request_ref, table, _, *rest):
    out_refs = rest[: len(cuts)]
    sums, lists, near_sems, far_sems, sems = rest[len(cuts) :]
    near = min(NEAR, stride)

    def read(s, at, size, read_sems):
        slot = lax.rem(s, SLOTS)
        return pltpu.make_async_copy(
            request_ref.at[pl.ds(pl.multiple_of(s * stride + at, LANES), size)],
            lists.at[pl.ds(pl.multiple_of(slot * stride + at, LANES), size)],
            read_sems.at[slot],
        )

    def read_near(s):
        return read(s, 0, near, near_sems)

    def read_far(s):
        return read(s, near, stride - near, far_sems)

    def heads(s):
        at = lax.rem(s, SLOTS) * stride
        begin, head = lists[at + 2 * group], lists[at + 2 * group + 1]
        steps = head & (FLAG - 1)
        return at + LANES + begin, head, steps, LANES + begin + steps * GROUP > near

    for s in range(SLOTS - 1):
        read_near(s).start()

    first = min(at for at, _ in cuts)
    cleared = sum(size for _, size in cuts)

    def clear(i, _):
        sums[pl.ds(first + i * 256, 256), :] = jnp.zeros((256, LANES), jnp.float32)
        return 0

    lax.fori_loop(0, cleared // 256, clear, 0)
    low = (4 << cell_bits) - 1

    def cell_at(code):
        return pl.ds(pl.multiple_of(code & low, 2), 2)

    def row_at(code):
        return pl.ds(pl.multiple_of(lax.shift_right_logical(code, cell_bits + 2), 2), 2)

    def arrive(s):
        read_near(s).wait()

        @pl.when(heads(s)[3])
        def _():
            read_far(s).start()

    arrive(0)

    def source(s, _):
        @pl.when(s + SLOTS - 1 < n)
        def _():
            read_near(s + SLOTS - 1).start()

        @pl.when(s + 1 < n)
        def _():
            arrive(s + 1)

        begin, head, steps, far = heads(s)

        @pl.when(far)
        def _():
            read_far(s).wait()

        @pl.when(head < FLAG)
        def _():
            def step(i, _):
                at = begin + i
                new = []
                for k in range(GROUP):
                    code = lists[at]
                    new.append((code, sums[cell_at(code), :] + table[row_at(code), :]))
                    at = at + steps
                for code, value in new:
                    sums[cell_at(code), :] = value
                return 0

            lax.fori_loop(0, steps, step, 0)

        @pl.when(head >= FLAG)
        def _():
            def step(i, _):
                code = lists[begin + i]
                sums[cell_at(code), :] = sums[cell_at(code), :] + table[row_at(code), :]
                return 0

            lax.fori_loop(0, steps * GROUP, step, 0)

        return 0

    lax.fori_loop(0, n, source, 0)
    copies = [
        pltpu.make_async_copy(sums.at[pl.ds(at, size), :], ref, sems.at[k])
        for k, ((at, size), ref) in enumerate(zip(cuts, out_refs))
    ]
    for copy in copies:
        copy.start()
    for copy in copies:
        copy.wait()


def merge_kernel(plan, *refs):
    refs = list(refs)
    outs = refs[sum(1 + arrived for arrived, _ in plan) + 1 :]
    for arrived, blocks in plan:
        sources = [refs.pop(0) for _ in range(1 + arrived)]
        size = sources[0].shape[0] // blocks
        for p in range(blocks):
            at = pl.ds(p * size, size)
            total = sources[0][at, :]
            for ref in sources[1:]:
                total = total + ref[at, :]
            outs.pop(0)[...] = total


def merge(chains, after):
    operands, plan, shapes = [], [], []
    for kept, arrived, stages in chains:
        operands += [kept, *arrived]
        blocks = 1 << len(stages[0]) if stages else 1
        plan.append((len(arrived), blocks))
        shapes += [jax.ShapeDtypeStruct((kept.shape[0] // blocks, LANES), kept.dtype)] * blocks
    outs = pl.pallas_call(
        functools.partial(merge_kernel, plan),
        out_shape=shapes,
        in_specs=[pl.BlockSpec(memory_space=pltpu.VMEM)] * len(operands)
        + [pl.BlockSpec(memory_space=pl.ANY)],
        out_specs=[pl.BlockSpec(memory_space=pltpu.VMEM)] * len(shapes),
        compiler_params=pltpu.CompilerParams(vmem_limit_bytes=16 * 1024 * 1024),
    )(*operands, after)
    outs = list(outs)
    result = []
    for (_, blocks), (_, _, stages) in zip(plan, chains):
        mine = [outs.pop(0) for _ in range(blocks)]
        result.append((mine[0], mine[1:], stages))
    return result


def exchange(chain, n):
    kept, sends, stages = chain
    if not stages:
        return chain
    bits = stages[0]
    arrived = []
    for p, block in enumerate(sends, 1):
        flip = sum(2 << bit for k, bit in enumerate(reversed(bits)) if (p >> k) & 1)
        arrived.append(lax.ppermute(block, "tm", [(i, i ^ flip) for i in range(n)]))
    return (kept, arrived, stages[1:])


def per_device(item_table, item_shard, item_row, cluster_id, lengths):
    n = lax.axis_size("tm")
    me = lax.axis_index("tm")
    users, slab = item_row.shape[1:]
    rows, width = item_table.shape
    total = users * slab
    owned = K // n
    m = bits_for(n) - 1
    cells = users * K // 2
    cell_bits = bits_for(cells)
    row_bits = bits_for(2 * rows)
    dest_shift = cell_bits + row_bits
    cap_rows = -(-4 * total // n // LANES)
    count_rows = users * owned // LANES
    req_rows = cap_rows + 1
    block_rows = -(-(1 + req_rows + count_rows) // SUB) * SUB
    groups = user_groups(users, m)
    dummy = cells * 2

    other = lax.ppermute(item_table, "tm", [(i, i ^ 1) for i in range(n)])
    scalars = jnp.concatenate([lengths, me.astype(jnp.int32).reshape(1)])
    buckets = pl.pallas_call(
        functools.partial(
            prepare_kernel, n, owned, rows, dest_shift, row_bits, cell_bits, req_rows, count_rows,
            dummy, groups,
        ),
        out_shape=jax.ShapeDtypeStruct((n, block_rows, LANES), jnp.int32),
        in_specs=[pl.BlockSpec(memory_space=pltpu.SMEM)]
        + [pl.BlockSpec(memory_space=pltpu.VMEM)] * 3,
        out_specs=pl.BlockSpec(memory_space=pltpu.VMEM),
        scratch_shapes=[
            pltpu.VMEM((LANES, LANES), jnp.int32),
            pltpu.VMEM((LANES + -(-(req_rows + 1) // SUB) * SUB, LANES), jnp.int32),
        ],
    )(
        scalars,
        item_shard.reshape(users, slab),
        item_row.reshape(users, slab),
        cluster_id.reshape(users, slab),
    )
    requests = lax.all_to_all(buckets, "tm", split_axis=0, concat_axis=0, tiled=True)
    counts = jnp.sum(requests[:, 1 + req_rows : 1 + req_rows + count_rows, :], axis=0)
    counts = counts.reshape(users, owned).astype(jnp.float32)

    table = pl.pallas_call(
        widen_kernel,
        out_shape=jax.ShapeDtypeStruct((rows * 4, LANES), jnp.float32),
        in_specs=[pl.BlockSpec(memory_space=pltpu.VMEM)] * 2,
        out_specs=pl.BlockSpec(memory_space=pltpu.VMEM),
        compiler_params=pltpu.CompilerParams(vmem_limit_bytes=16 * 1024 * 1024),
    )(item_table, other)
    requests = requests.reshape(-1)

    sums_rows = -(-(cells + 1) * 2 // 256) * 256

    def add(g, after):
        cuts = []
        for lo, size, _ in groups[g]:
            half = size * (K // 2)
            cuts += [(lo * K, half), (lo * K + half, half)]
        group_users = sum(size for _, size, _ in groups[g])
        parts = pl.pallas_call(
            functools.partial(add_kernel, n, block_rows * LANES, cell_bits, g, cuts),
            out_shape=[jax.ShapeDtypeStruct((size, LANES), jnp.float32) for _, size in cuts],
            in_specs=[
                pl.BlockSpec(memory_space=pl.ANY),
                pl.BlockSpec(memory_space=pltpu.VMEM),
                pl.BlockSpec(memory_space=pl.ANY),
            ],
            out_specs=[pl.BlockSpec(memory_space=pl.ANY)] * len(cuts),
            scratch_shapes=[
                pltpu.VMEM((sums_rows, LANES), jnp.float32),
                pltpu.SMEM((SLOTS * block_rows * LANES,), jnp.int32),
                pltpu.SemaphoreType.DMA((SLOTS,)),
                pltpu.SemaphoreType.DMA((SLOTS,)),
                pltpu.SemaphoreType.DMA((len(cuts),)),
            ],
            compiler_params=pltpu.CompilerParams(vmem_limit_bytes=16 * 1024 * 1024),
            cost_estimate=pl.CostEstimate(
                flops=group_users * slab * width,
                bytes_accessed=group_users * 12 * 1024 * 1024,
                transcendentals=0,
            ),
        )(requests, table, after)
        return [
            (kept, [sent], stages_of(bits))
            for kept, sent, (_, _, bits) in zip(parts[0::2], parts[1::2], groups[g])
        ]

    names = [chain for group in groups for chain in group]
    under_way, finished = {}, {}
    after = scalars
    g = 0
    while g < len(groups) or under_way:
        new = {}
        if g < len(groups):
            new = dict(zip(groups[g], add(g, after)))
            after = new[groups[g][0]][0]
            g += 1
        if under_way:
            merged = dict(zip(under_way, merge(list(under_way.values()), after)))
            after = next(iter(merged.values()))[0]
            finished.update({name: c[0] for name, c in merged.items() if not c[1]})
            under_way = {name: c for name, c in merged.items() if c[1]}
        under_way = {
            name: exchange(chain, n) for name, chain in {**under_way, **new}.items()
        }
    done = [finished[name].reshape(name[1], owned, width) for name in names]
    return jnp.concatenate(done, axis=0) / jnp.maximum(counts, 1.0)[..., None]


def solution(mesh):
    return jax.shard_map(
        per_device,
        mesh=mesh,
        in_specs=(
            P("tm", None),
            P("tm", ("groups", "users"), None, None),
            P("tm", ("groups", "users"), None),
            P("tm", ("groups", "users"), None),
            P(("groups", "users")),
        ),
        out_specs=P(("groups", "users"), "tm", None),
        check_vma=False,
    )
```

```python
import functools

import jax
import jax.numpy as jnp
from jax import lax
from jax.experimental import pallas as pl
from jax.experimental.pallas import tpu as pltpu
from jax.sharding import PartitionSpec as P

K = 1024
LANES = 128
SUB = 8
GROUP = 16
FLAG = 1 << 30
NONE = 2**31 - 1
NEAR = 512


def bits_for(count):
    return (count - 1).bit_length()


def user_groups(users, m):
    orders = [(0, 2, 1, 3), (2, 1, 0, 3), (1, 0, 3, 2)] if m == 4 else [range(m)] * 3
    sizes = [-(-users * 3 // 8), users * 3 // 8]
    sizes.append(users - sum(sizes))
    chains, lo = [], 0
    for size, order in zip(sizes, orders):
        if size:
            chains.append((lo, size, tuple(order)))
        lo += size
    return [chains]


def stages_of(bits):
    return [[bit] for bit in bits]


def sort_tiles(tiles):
    count = len(tiles)
    tile_bits = bits_for(count)
    sub = lax.broadcasted_iota(jnp.int32, (SUB, LANES), 0)
    lane = lax.broadcasted_iota(jnp.int32, (SUB, LANES), 1)
    total_bits = tile_bits + 3 + 7

    def bit_mask(bit):
        if bit < tile_bits + 3:
            return ((sub >> (bit - tile_bits)) & 1) == 1
        return ((lane >> (bit - tile_bits - 3)) & 1) == 1

    masks = {b: bit_mask(b) for b in range(tile_bits, total_bits)}
    flips = {b: jnp.where(masks[b], -1, 0) for b in masks}

    def flip(t, phase):
        if phase >= total_bits:
            return 0
        if phase < tile_bits:
            return -1 if (t >> phase) & 1 else 0
        return flips[phase]

    for phase in range(1, total_bits + 1):
        changed = []
        for t in range(count):
            old = flip(t, phase - 1) if phase > 1 else 0
            new = flip(t, phase)
            if isinstance(old, int) and isinstance(new, int):
                turn = old ^ new
                changed.append(tiles[t] if turn == 0 else ~tiles[t])
            else:
                changed.append(tiles[t] ^ (old ^ new))
        tiles = changed
        for bit in reversed(range(phase)):
            if bit < tile_bits:
                step = 1 << bit
                tiles = list(tiles)
                for t in range(count):
                    if not t & step:
                        a, b = tiles[t], tiles[t | step]
                        tiles[t], tiles[t | step] = jnp.minimum(a, b), jnp.maximum(a, b)
                continue
            if bit < tile_bits + 3:
                axis, step, size = 0, 1 << (bit - tile_bits), SUB
            else:
                axis, step, size = 1, 1 << (bit - tile_bits - 3), LANES
            upper = masks[bit]
            moved = []
            for x in tiles:
                down = pltpu.roll(x, step, axis=axis)
                if 2 * step == size:
                    other = down
                else:
                    other = jnp.where(upper, down, pltpu.roll(x, size - step, axis=axis))
                moved.append(
                    jnp.where(upper, jnp.maximum(x, other), jnp.minimum(x, other))
                )
            tiles = moved
    return tiles


def prepare_kernel(
    n, owned, table_rows, dest_shift, row_bits, cell_bits, req_rows, count_rows, dummy, groups,
    scalars_ref, shard_ref, row_ref, cluster_ref, out_ref, order, pad,
):
    users, slab = shard_ref.shape
    sub = lax.broadcasted_iota(jnp.int32, (SUB, LANES), 0)
    lane = lax.broadcasted_iota(jnp.int32, (SUB, LANES), 1)
    me = scalars_ref[users]
    length = jnp.zeros((SUB, LANES), jnp.int32)
    live_total = jnp.int32(0)
    for u in range(users):
        length = jnp.where(sub == u, scalars_ref[u], length)
        live_total += jnp.clip(scalars_ref[u] - me * slab, 0, slab)
    length = length - me * slab

    base = jnp.zeros((SUB, LANES), jnp.int32)
    in_chain = jnp.zeros((SUB, LANES), jnp.int32)
    chain_size = jnp.zeros((SUB, LANES), jnp.int32)
    chain_at = []
    chains = [chain for group in groups for chain in group]
    for lo, size, _ in chains:
        inside = (sub >= lo) & (sub < lo + size)
        base = jnp.where(inside, lo * (K // 2), base)
        in_chain = jnp.where(inside, sub - lo, in_chain)
        chain_size = jnp.where(inside, size, chain_size)
        chain_at.append(inside)

    owner_shift = bits_for(owned)
    tiles = []
    hot_owner = [[] for _ in range(count_rows)]
    hot_slot = [[] for _ in range(count_rows)]
    per_row = LANES // owned
    owner_iota = lax.broadcasted_iota(jnp.int32, (n, LANES), 0)
    slot_iota = lax.broadcasted_iota(jnp.int32, (LANES, LANES), 0)
    for j in range(slab // LANES):
        at = pl.ds(j * LANES, LANES)
        shard, row, cluster = shard_ref[:, at], row_ref[:, at], cluster_ref[:, at]
        owner = lax.shift_right_logical(cluster, owner_shift)
        low = cluster & (owned - 1)
        live = lane + j * LANES < length
        dest = (shard & ~1) | (owner & 1)
        away = lax.shift_right_logical(owner ^ dest, 1)
        spread = jnp.zeros((SUB, LANES), jnp.int32)
        by_order = {}
        for (_, _, bits), inside in zip(chains, chain_at):
            if bits not in by_order:
                turned = jnp.zeros((SUB, LANES), jnp.int32)
                for bit in bits:
                    turned = turned * 2 + ((away >> bit) & 1)
                by_order[bits] = turned
            spread = jnp.where(inside, by_order[bits], spread)
        cell = base + ((spread * chain_size + in_chain) << owner_shift) + low
        there = ((shard ^ owner) & 1) * table_rows + row
        key = (dest << dest_shift) | (cell << row_bits) | there
        tiles.append(jnp.where(live, key, NONE))
        live_owner = jnp.where(live, owner, -1)
        for u in range(users):
            r = u // per_row
            hot_owner[r].append((owner_iota == live_owner[u : u + 1, :]).astype(jnp.bfloat16))
            target = low[u : u + 1, :] + (u % per_row) * owned
            hot_slot[r].append((slot_iota == target).astype(jnp.bfloat16))

    for r in range(count_rows):
        counts = jnp.zeros((n, LANES), jnp.float32)
        for a, b in zip(hot_owner[r], hot_slot[r]):
            counts += lax.dot_general(
                a, b, (((1,), (1,)), ((), ())), preferred_element_type=jnp.float32
            )
        counts = counts.astype(jnp.int32)
        for d in range(n):
            out_ref[d, pl.ds(1 + req_rows + r, 1), :] = counts[d : d + 1, :]

    ends = []
    for d in range(n):
        for g in range(len(groups)):
            if g + 1 < len(groups):
                limit = (d << dest_shift) + ((groups[g + 1][0][0] * (K // 2)) << row_bits)
            elif d + 1 < n:
                limit = (d + 1) << dest_shift
            else:
                ends.append(live_total)
                continue
            below = jnp.zeros((SUB, LANES), jnp.float32)
            for x in tiles:
                below += (x < limit).astype(jnp.float32)
            ends.append(jnp.sum(below).astype(jnp.int32))

    empty = jnp.full((SUB, LANES), NONE, jnp.int32)
    tiles = sort_tiles(tiles + [empty] * ((1 << bits_for(len(tiles))) - len(tiles)))
    count = len(tiles)
    for t, x in enumerate(tiles):
        order[pl.ds(t * SUB, SUB), :] = x
    lines = [order[pl.ds(s, count, stride=SUB), :] for s in range(SUB)]
    straight = jnp.concatenate(lines, axis=0).T
    pad[0:LANES, :] = straight
    pad[LANES:, :] = jnp.full((pad.shape[0] - LANES, LANES), NONE, jnp.int32)

    lane = lax.broadcasted_iota(jnp.int32, (req_rows, LANES), 1)
    slot = lax.broadcasted_iota(jnp.int32, (req_rows, LANES), 0) * LANES + lane
    head_lane = lax.broadcasted_iota(jnp.int32, (1, LANES), 1)
    nothing = jnp.full((1, LANES), -1, jnp.int32)

    def ahead(x, by):
        turned = pltpu.roll(x, (LANES - by) & (LANES - 1), axis=1)
        return jnp.where(lane < LANES - by, turned[:req_rows], turned[1:])

    start = jnp.int32(0)
    for d in range(n):
        mine_ends = ends[d * len(groups) : (d + 1) * len(groups)]
        count = mine_ends[-1] - start
        first = lax.shift_right_logical(start, bits_for(LANES))
        mine = ahead(pad[pl.ds(first, req_rows + 1), :], start & (LANES - 1))
        there = mine & (2 * table_rows - 1)
        cell = lax.shift_right_logical(mine, row_bits) & ((1 << cell_bits) - 1)
        code = jnp.where(slot < count, (there << (cell_bits + 3)) | (cell << 1), dummy)
        cell = jnp.where(slot < count, cell, -1)
        out_ref[d, pl.ds(1, req_rows), :] = code
        cells = jnp.concatenate([cell, nothing], axis=0)
        head = jnp.zeros((1, LANES), jnp.int32)
        begin = jnp.int32(0)
        for g, end in enumerate(mine_ends):
            end = end - start
            steps = lax.shift_right_logical(end - begin + GROUP - 1, bits_for(GROUP))
            same = (cell == ahead(cells, steps)) & (slot >= begin) & (slot < end)
            twice = jnp.max(same.astype(jnp.float32))
            head = jnp.where(head_lane == 2 * g, begin, head)
            head = jnp.where(
                head_lane == 2 * g + 1, steps | jnp.where(twice > 0, FLAG, 0), head
            )
            begin = end
        out_ref[d, pl.ds(0, 1), :] = head
        start = mine_ends[-1]


def widen_kernel(own_ref, other_ref, table):
    rows = own_ref.shape[0]
    block = 128

    def widen(i, _):
        for part, ref in enumerate((own_ref, other_ref)):
            x = ref[pl.ds(i * block, block), :].astype(jnp.float32)
            at = (part * rows + i * block) * 2
            table[pl.ds(at, block, stride=2), :] = x[:, :LANES]
            table[pl.ds(at + 1, block, stride=2), :] = x[:, LANES:]
        return 0

    lax.fori_loop(0, rows // block, widen, 0)


def add_kernel(n, stride, cell_bits, group, cuts, request_ref, table, _, *rest):
    out_refs = rest[: len(cuts)]
    sums, lists, near_sems, far_sems, sems = rest[len(cuts) :]
    near = min(NEAR, stride)

    def read(s, at, size, read_sems):
        at = pl.ds(pl.multiple_of(s * stride + at, LANES), size)
        return pltpu.make_async_copy(request_ref.at[at], lists.at[at], read_sems.at[s])

    def read_near(s):
        return read(s, 0, near, near_sems)

    def read_far(s):
        return read(s, near, stride - near, far_sems)

    def heads(s):
        at = s * stride
        begin, head = lists[at + 2 * group], lists[at + 2 * group + 1]
        steps = head & (FLAG - 1)
        return at + LANES + begin, head, steps, LANES + begin + steps * GROUP > near

    def start_near(s, _):
        read_near(s).start()
        return 0

    lax.fori_loop(0, n, start_near, 0)

    first = min(at for at, _ in cuts)
    cleared = sum(size for _, size in cuts)

    def clear(i, _):
        sums[pl.ds(first + i * 256, 256), :] = jnp.zeros((256, LANES), jnp.float32)
        return 0

    lax.fori_loop(0, cleared // 256, clear, 0)
    low = (4 << cell_bits) - 1

    def cell_at(code):
        return pl.ds(pl.multiple_of(code & low, 2), 2)

    def row_at(code):
        return pl.ds(pl.multiple_of(lax.shift_right_logical(code, cell_bits + 2), 2), 2)

    def arrive(s, _):
        read_near(s).wait()

        @pl.when(heads(s)[3])
        def _():
            read_far(s).start()

        return 0

    lax.fori_loop(0, n, arrive, 0)

    def source(s, _):
        begin, head, steps, far = heads(s)

        @pl.when(far)
        def _():
            read_far(s).wait()

        @pl.when(head < FLAG)
        def _():
            def step(i, _):
                at = begin + i
                new = []
                for k in range(GROUP):
                    code = lists[at]
                    new.append((code, sums[cell_at(code), :] + table[row_at(code), :]))
                    at = at + steps
                for code, value in new:
                    sums[cell_at(code), :] = value
                return 0

            lax.fori_loop(0, steps, step, 0)

        @pl.when(head >= FLAG)
        def _():
            def step(i, _):
                code = lists[begin + i]
                sums[cell_at(code), :] = sums[cell_at(code), :] + table[row_at(code), :]
                return 0

            lax.fori_loop(0, steps * GROUP, step, 0)

        return 0

    lax.fori_loop(0, n, source, 0)
    copies = [
        pltpu.make_async_copy(sums.at[pl.ds(at, size), :], ref, sems.at[k])
        for k, ((at, size), ref) in enumerate(zip(cuts, out_refs))
    ]
    for copy in copies:
        copy.start()
    for copy in copies:
        copy.wait()


def merge_kernel(plan, *refs):
    refs = list(refs)
    outs = refs[sum(1 + arrived for arrived, _ in plan) + 1 :]
    for arrived, blocks in plan:
        sources = [refs.pop(0) for _ in range(1 + arrived)]
        size = sources[0].shape[0] // blocks
        for p in range(blocks):
            at = pl.ds(p * size, size)
            total = sources[0][at, :]
            for ref in sources[1:]:
                total = total + ref[at, :]
            outs.pop(0)[...] = total


def merge(chains, after):
    operands, plan, shapes = [], [], []
    for kept, arrived, stages in chains:
        operands += [kept, *arrived]
        blocks = 1 << len(stages[0]) if stages else 1
        plan.append((len(arrived), blocks))
        shapes += [jax.ShapeDtypeStruct((kept.shape[0] // blocks, LANES), kept.dtype)] * blocks
    outs = pl.pallas_call(
        functools.partial(merge_kernel, plan),
        out_shape=shapes,
        in_specs=[pl.BlockSpec(memory_space=pltpu.VMEM)] * len(operands)
        + [pl.BlockSpec(memory_space=pl.ANY)],
        out_specs=[pl.BlockSpec(memory_space=pltpu.VMEM)] * len(shapes),
        compiler_params=pltpu.CompilerParams(vmem_limit_bytes=16 * 1024 * 1024),
    )(*operands, after)
    outs = list(outs)
    result = []
    for (_, blocks), (_, _, stages) in zip(plan, chains):
        mine = [outs.pop(0) for _ in range(blocks)]
        result.append((mine[0], mine[1:], stages))
    return result


def exchange(chain, n):
    kept, sends, stages = chain
    if not stages:
        return chain
    bits = stages[0]
    arrived = []
    for p, block in enumerate(sends, 1):
        flip = sum(2 << bit for k, bit in enumerate(reversed(bits)) if (p >> k) & 1)
        arrived.append(lax.ppermute(block, "tm", [(i, i ^ flip) for i in range(n)]))
    return (kept, arrived, stages[1:])


def per_device(item_table, item_shard, item_row, cluster_id, lengths):
    n = lax.axis_size("tm")
    me = lax.axis_index("tm")
    users, slab = item_row.shape[1:]
    rows, width = item_table.shape
    total = users * slab
    owned = K // n
    m = bits_for(n) - 1
    cells = users * K // 2
    cell_bits = bits_for(cells)
    row_bits = bits_for(2 * rows)
    dest_shift = cell_bits + row_bits
    cap_rows = -(-4 * total // n // LANES)
    count_rows = users * owned // LANES
    req_rows = cap_rows + 1
    block_rows = -(-(1 + req_rows + count_rows) // SUB) * SUB
    groups = user_groups(users, m)
    dummy = cells * 2

    other = lax.ppermute(item_table, "tm", [(i, i ^ 1) for i in range(n)])
    scalars = jnp.concatenate([lengths, me.astype(jnp.int32).reshape(1)])
    buckets = pl.pallas_call(
        functools.partial(
            prepare_kernel, n, owned, rows, dest_shift, row_bits, cell_bits, req_rows, count_rows,
            dummy, groups,
        ),
        out_shape=jax.ShapeDtypeStruct((n, block_rows, LANES), jnp.int32),
        in_specs=[pl.BlockSpec(memory_space=pltpu.SMEM)]
        + [pl.BlockSpec(memory_space=pltpu.VMEM)] * 3,
        out_specs=pl.BlockSpec(memory_space=pltpu.VMEM),
        scratch_shapes=[
            pltpu.VMEM((LANES, LANES), jnp.int32),
            pltpu.VMEM((LANES + -(-(req_rows + 1) // SUB) * SUB, LANES), jnp.int32),
        ],
    )(
        scalars,
        item_shard.reshape(users, slab),
        item_row.reshape(users, slab),
        cluster_id.reshape(users, slab),
    )
    requests = lax.all_to_all(buckets, "tm", split_axis=0, concat_axis=0, tiled=True)
    counts = jnp.sum(requests[:, 1 + req_rows : 1 + req_rows + count_rows, :], axis=0)
    counts = counts.reshape(users, owned).astype(jnp.float32)

    table = pl.pallas_call(
        widen_kernel,
        out_shape=jax.ShapeDtypeStruct((rows * 4, LANES), jnp.float32),
        in_specs=[pl.BlockSpec(memory_space=pltpu.VMEM)] * 2,
        out_specs=pl.BlockSpec(memory_space=pltpu.VMEM),
        compiler_params=pltpu.CompilerParams(vmem_limit_bytes=16 * 1024 * 1024),
    )(item_table, other)
    requests = requests.reshape(-1)

    sums_rows = -(-(cells + 1) * 2 // 256) * 256

    def add(g, after):
        cuts = []
        for lo, size, _ in groups[g]:
            half = size * (K // 2)
            cuts += [(lo * K, half), (lo * K + half, half)]
        group_users = sum(size for _, size, _ in groups[g])
        parts = pl.pallas_call(
            functools.partial(add_kernel, n, block_rows * LANES, cell_bits, g, cuts),
            out_shape=[jax.ShapeDtypeStruct((size, LANES), jnp.float32) for _, size in cuts],
            in_specs=[
                pl.BlockSpec(memory_space=pltpu.VMEM),
                pl.BlockSpec(memory_space=pltpu.VMEM),
                pl.BlockSpec(memory_space=pl.ANY),
            ],
            out_specs=[pl.BlockSpec(memory_space=pl.ANY)] * len(cuts),
            scratch_shapes=[
                pltpu.VMEM((sums_rows, LANES), jnp.float32),
                pltpu.SMEM((n * block_rows * LANES,), jnp.int32),
                pltpu.SemaphoreType.DMA((n,)),
                pltpu.SemaphoreType.DMA((n,)),
                pltpu.SemaphoreType.DMA((len(cuts),)),
            ],
            compiler_params=pltpu.CompilerParams(vmem_limit_bytes=16 * 1024 * 1024),
            cost_estimate=pl.CostEstimate(
                flops=group_users * slab * width,
                bytes_accessed=group_users * 12 * 1024 * 1024,
                transcendentals=0,
            ),
        )(requests, table, after)
        return [
            (kept, [sent], stages_of(bits))
            for kept, sent, (_, _, bits) in zip(parts[0::2], parts[1::2], groups[g])
        ]

    names = [chain for group in groups for chain in group]
    under_way, finished = {}, {}
    after = scalars
    g = 0
    while g < len(groups) or under_way:
        new = {}
        if g < len(groups):
            new = dict(zip(groups[g], add(g, after)))
            after = new[groups[g][0]][0]
            g += 1
        if under_way:
            merged = dict(zip(under_way, merge(list(under_way.values()), after)))
            after = next(iter(merged.values()))[0]
            finished.update({name: c[0] for name, c in merged.items() if not c[1]})
            under_way = {name: c for name, c in merged.items() if c[1]}
        under_way = {
            name: exchange(chain, n) for name, chain in {**under_way, **new}.items()
        }
    done = [finished[name].reshape(name[1], owned, width) for name in names]
    return jnp.concatenate(done, axis=0) / jnp.maximum(counts, 1.0)[..., None]


def solution(mesh):
    return jax.shard_map(
        per_device,
        mesh=mesh,
        in_specs=(
            P("tm", None),
            P("tm", ("groups", "users"), None, None),
            P("tm", ("groups", "users"), None),
            P("tm", ("groups", "users"), None),
            P(("groups", "users")),
        ),
        out_specs=P(("groups", "users"), "tm", None),
        check_vma=False,
    )
```

```python
import functools
import math

import jax
import jax.numpy as jnp
from jax import lax
from jax.experimental import pallas as pl
from jax.experimental.pallas import tpu as pltpu
from jax.sharding import PartitionSpec as P

K = 1024
LANES = 128
SUB = 8
GROUP = 16
FLAG = 1 << 30
NONE = 2**31 - 1
CODE_TOP = 32766.0
NEAR = 512


def bits_for(count):
    return (count - 1).bit_length()


def user_chains(users, m):
    orders = [(0, 2, 1, 3), (2, 1, 0, 3), (1, 0, 3, 2)] if m == 4 else [tuple(range(m))] * 3
    sizes = [-(-users * 3 // 8), users * 3 // 8]
    sizes.append(users - sum(sizes))
    chains, lo = [], 0
    for size, order in zip(sizes, orders):
        if size:
            chains.append((lo, size, order))
        lo += size
    return chains


def packets_of(chains, stage, rows):
    if stage == len(chains[0][2]):
        return []
    bits = {}
    for c, (_, _, order) in enumerate(chains):
        bits.setdefault(order[stage], []).append(c)
    return [
        (bit, [(c, rows[c]) for c in members], all(rows[c] % LANES == 0 for c in members))
        for bit, members in bits.items()
    ]


def packet_shape(packet):
    _, members, coded = packet
    lines = sum(rows for _, rows in members)
    if not coded:
        return jax.ShapeDtypeStruct((lines, LANES), jnp.float32)
    return jax.ShapeDtypeStruct((lines + scale_lines(lines), LANES), jnp.int16)


def scale_lines(lines):
    return -(-lines // LANES // 16) * 16


def diagonal():
    at = (LANES, LANES)
    return lax.broadcasted_iota(jnp.int32, at, 0) == lax.broadcasted_iota(jnp.int32, at, 1)


def scale_of(exponent):
    return jnp.exp(exponent * (math.log(2.0) / 64.0))


def encode(packet, sources, out_ref, scales):
    done = 0
    for (_, rows), (ref, start) in zip(packet[1], sources):
        if not packet[2]:
            out_ref[pl.ds(done, rows), :] = ref[pl.ds(start, rows), :]
            done += rows
            continue

        def block(i, _, ref=ref, start=start, done=done):
            x = ref[pl.ds(start + i * LANES, LANES), :]
            top = jnp.maximum(jnp.max(jnp.abs(x), axis=1, keepdims=True), 1e-33)
            exponent = jnp.ceil(jnp.log(top) * (64.0 / math.log(2.0)))
            code = jnp.round(x * (CODE_TOP / scale_of(exponent)))
            code = jnp.clip(code, -32767.0, 32767.0).astype(jnp.int32).astype(jnp.int16)
            out_ref[pl.ds(pl.multiple_of(done + i * LANES, LANES), LANES), :] = code
            line = jnp.sum(jnp.where(diagonal(), exponent, 0.0), axis=0, keepdims=True)
            scales[pl.ds(done // LANES + i, 1), :] = line
            return 0

        lax.fori_loop(0, rows // LANES, block, 0)
        done += rows
    if packet[2]:
        out_ref[pl.ds(done, scale_lines(done)), :] = (
            scales[pl.ds(0, scale_lines(done)), :].astype(jnp.int32).astype(jnp.int16)
        )


def add_packet(packet, ref, sums, scales):
    if packet[2]:
        lines = sum(rows for _, rows in packet[1])
        scales[pl.ds(0, scale_lines(lines)), :] = ref[
            pl.ds(lines, scale_lines(lines)), :
        ].astype(jnp.float32)
    done = 0
    for c, rows in packet[1]:
        if not packet[2]:
            sums[c][...] = sums[c][...] + ref[pl.ds(done, rows), :]
            done += rows
            continue

        def block(i, _, c=c, done=done):
            line = scales[pl.ds(done // LANES + i, 1), :]
            exponent = jnp.sum(jnp.where(diagonal(), line, 0.0), axis=1, keepdims=True)
            code = ref[pl.ds(pl.multiple_of(done + i * LANES, LANES), LANES), :]
            at = pl.ds(pl.multiple_of(i * LANES, LANES), LANES)
            value = code.astype(jnp.float32) * (scale_of(exponent) * (1.0 / CODE_TOP))
            sums[c][at, :] = sums[c][at, :] + value
            return 0

        lax.fori_loop(0, rows // LANES, block, 0)
        done += rows


def sort_tiles(tiles):
    count = len(tiles)
    tile_bits = bits_for(count)
    sub = lax.broadcasted_iota(jnp.int32, (SUB, LANES), 0)
    lane = lax.broadcasted_iota(jnp.int32, (SUB, LANES), 1)
    total_bits = tile_bits + 3 + 7

    def bit_mask(bit):
        if bit < tile_bits + 3:
            return ((sub >> (bit - tile_bits)) & 1) == 1
        return ((lane >> (bit - tile_bits - 3)) & 1) == 1

    masks = {b: bit_mask(b) for b in range(tile_bits, total_bits)}
    flips = {b: jnp.where(masks[b], -1, 0) for b in masks}

    def flip(t, phase):
        if phase >= total_bits:
            return 0
        if phase < tile_bits:
            return -1 if (t >> phase) & 1 else 0
        return flips[phase]

    for phase in range(1, total_bits + 1):
        changed = []
        for t in range(count):
            old = flip(t, phase - 1) if phase > 1 else 0
            new = flip(t, phase)
            if isinstance(old, int) and isinstance(new, int):
                turn = old ^ new
                changed.append(tiles[t] if turn == 0 else ~tiles[t])
            else:
                changed.append(tiles[t] ^ (old ^ new))
        tiles = changed
        for bit in reversed(range(phase)):
            if bit < tile_bits:
                step = 1 << bit
                tiles = list(tiles)
                for t in range(count):
                    if not t & step:
                        a, b = tiles[t], tiles[t | step]
                        tiles[t], tiles[t | step] = jnp.minimum(a, b), jnp.maximum(a, b)
                continue
            if bit < tile_bits + 3:
                axis, step, size = 0, 1 << (bit - tile_bits), SUB
            else:
                axis, step, size = 1, 1 << (bit - tile_bits - 3), LANES
            upper = masks[bit]
            moved = []
            for x in tiles:
                down = pltpu.roll(x, step, axis=axis)
                if 2 * step == size:
                    other = down
                else:
                    other = jnp.where(upper, down, pltpu.roll(x, size - step, axis=axis))
                moved.append(
                    jnp.where(upper, jnp.maximum(x, other), jnp.minimum(x, other))
                )
            tiles = moved
    return tiles


def prepare_kernel(
    n, owned, table_rows, dest_shift, row_bits, cell_bits, req_rows, count_rows, dummy, chains,
    lengths_ref, shard_ref, row_ref, cluster_ref, out_ref, order, pad,
):
    users, slab = row_ref.shape
    sub = lax.broadcasted_iota(jnp.int32, (SUB, LANES), 0)
    lane = lax.broadcasted_iota(jnp.int32, (SUB, LANES), 1)
    me = lax.axis_index("tm")
    length = jnp.zeros((SUB, LANES), jnp.int32)
    live_total = jnp.int32(0)
    for u in range(users):
        length = jnp.where(sub == u, lengths_ref[u], length)
        live_total += jnp.clip(lengths_ref[u] - me * slab, 0, slab)
    length = length - me * slab

    base = jnp.zeros((SUB, LANES), jnp.int32)
    in_chain = jnp.zeros((SUB, LANES), jnp.int32)
    chain_size = jnp.zeros((SUB, LANES), jnp.int32)
    chain_at = []
    for lo, size, _ in chains:
        inside = (sub >= lo) & (sub < lo + size)
        base = jnp.where(inside, lo * (K // 2), base)
        in_chain = jnp.where(inside, sub - lo, in_chain)
        chain_size = jnp.where(inside, size, chain_size)
        chain_at.append(inside)

    owner_shift = bits_for(owned)
    tiles = []
    hot_owner = [[] for _ in range(count_rows)]
    hot_slot = [[] for _ in range(count_rows)]
    per_row = LANES // owned
    owner_iota = lax.broadcasted_iota(jnp.int32, (n, LANES), 0)
    slot_iota = lax.broadcasted_iota(jnp.int32, (LANES, LANES), 0)
    for j in range(slab // LANES):
        at = pl.ds(j * LANES, LANES)
        row, cluster = row_ref[:, at], cluster_ref[:, at]
        shard = shard_ref[pl.ds(j, users, stride=slab // LANES), :]
        owner = lax.shift_right_logical(cluster, owner_shift)
        low = cluster & (owned - 1)
        live = lane + j * LANES < length
        dest = (shard & ~1) | (owner & 1)
        away = lax.shift_right_logical(owner ^ dest, 1)
        spread = jnp.zeros((SUB, LANES), jnp.int32)
        by_order = {}
        for (_, _, bits), inside in zip(chains, chain_at):
            if bits not in by_order:
                turned = jnp.zeros((SUB, LANES), jnp.int32)
                for bit in bits:
                    turned = turned * 2 + ((away >> bit) & 1)
                by_order[bits] = turned
            spread = jnp.where(inside, by_order[bits], spread)
        cell = base + ((spread * chain_size + in_chain) << owner_shift) + low
        there = ((shard ^ owner) & 1) * table_rows + row
        key = (dest << dest_shift) | (cell << row_bits) | there
        tiles.append(jnp.where(live, key, NONE))
        live_owner = jnp.where(live, owner, -1)
        for u in range(users):
            r = u // per_row
            hot_owner[r].append((owner_iota == live_owner[u : u + 1, :]).astype(jnp.bfloat16))
            target = low[u : u + 1, :] + (u % per_row) * owned
            hot_slot[r].append((slot_iota == target).astype(jnp.bfloat16))

    for r in range(count_rows):
        counts = jnp.zeros((n, LANES), jnp.float32)
        for a, b in zip(hot_owner[r], hot_slot[r]):
            counts += lax.dot_general(
                a, b, (((1,), (1,)), ((), ())), preferred_element_type=jnp.float32
            )
        counts = counts.astype(jnp.int32)
        for d in range(n):
            out_ref[d, pl.ds(1 + req_rows + r, 1), :] = counts[d : d + 1, :]

    ends = []
    for d in range(n - 1):
        below = jnp.zeros((SUB, LANES), jnp.float32)
        for x in tiles:
            below += (x < ((d + 1) << dest_shift)).astype(jnp.float32)
        ends.append(jnp.sum(below).astype(jnp.int32))
    ends.append(live_total)

    empty = jnp.full((SUB, LANES), NONE, jnp.int32)
    tiles = sort_tiles(tiles + [empty] * ((1 << bits_for(len(tiles))) - len(tiles)))
    count = len(tiles)
    for t, x in enumerate(tiles):
        order[pl.ds(t * SUB, SUB), :] = x
    lines = [order[pl.ds(s, count, stride=SUB), :] for s in range(SUB)]
    straight = jnp.concatenate(lines, axis=0).T
    pad[0:LANES, :] = straight
    pad[LANES:, :] = jnp.full((pad.shape[0] - LANES, LANES), NONE, jnp.int32)

    lane = lax.broadcasted_iota(jnp.int32, (req_rows, LANES), 1)
    slot = lax.broadcasted_iota(jnp.int32, (req_rows, LANES), 0) * LANES + lane
    nothing = jnp.full((1, LANES), -1, jnp.int32)

    def ahead(x, by):
        turned = pltpu.roll(x, (LANES - by) & (LANES - 1), axis=1)
        return jnp.where(lane < LANES - by, turned[:req_rows], turned[1:])

    start = jnp.int32(0)
    for d in range(n):
        count = ends[d] - start
        steps = lax.shift_right_logical(count + GROUP - 1, bits_for(GROUP))
        first = lax.shift_right_logical(start, bits_for(LANES))
        mine = ahead(pad[pl.ds(first, req_rows + 1), :], start & (LANES - 1))
        there = mine & (2 * table_rows - 1)
        cell = lax.shift_right_logical(mine, row_bits) & ((1 << cell_bits) - 1)
        code = jnp.where(slot < count, (there << (cell_bits + 3)) | (cell << 1), dummy)
        cell = jnp.where(slot < count, cell, -1)
        later = ahead(jnp.concatenate([cell, nothing], axis=0), steps)
        twice = jnp.max(jnp.where((cell == later) & (cell >= 0), 1.0, 0.0))
        out_ref[d, pl.ds(1, req_rows), :] = code
        head = steps | jnp.where(twice > 0, FLAG, 0)
        out_ref[d, pl.ds(0, 1), :] = jnp.full((1, LANES), head, jnp.int32)
        start = ends[d]


def add_kernel(n, stride, cell_bits, chains, packets, request_ref, own_ref, other_ref, *rest):
    keep_refs = rest[: len(chains)]
    packet_refs = rest[len(chains) : len(chains) + len(packets)]
    narrow, table, sums, scales, lists, near_sems, far_sems, sems = rest[
        len(chains) + len(packets) :
    ]
    near = min(NEAR, stride)

    def read(s, at, size, read_sems):
        at = pl.ds(pl.multiple_of(s * stride + at, LANES), size)
        return pltpu.make_async_copy(request_ref.at[at], lists.at[at], read_sems.at[s])

    def read_near(s):
        return read(s, 0, near, near_sems)

    def read_far(s):
        return read(s, near, stride - near, far_sems)

    def start_near(s, _):
        read_near(s).start()
        return 0

    rows = own_ref.shape[0]
    tables = [
        pltpu.make_async_copy(ref, narrow.at[pl.ds(part * rows, rows), :], sems.at[part])
        for part, ref in enumerate((own_ref, other_ref))
    ]
    for copy in tables:
        copy.start()
    lax.fori_loop(0, n, start_near, 0)

    def clear(i, _):
        sums[pl.ds(i * 256, 256), :] = jnp.zeros((256, LANES), jnp.float32)
        return 0

    lax.fori_loop(0, sums.shape[0] // 256, clear, 0)

    def arrive(s, _):
        read_near(s).wait()

        @pl.when(LANES + (lists[s * stride] & (FLAG - 1)) * GROUP > near)
        def _():
            read_far(s).start()

        return 0

    lax.fori_loop(0, n, arrive, 0)
    for copy in tables:
        copy.wait()

    def widen(i, _):
        x = narrow[pl.ds(i * LANES, LANES), :].astype(jnp.float32)
        table[pl.ds(i * 2 * LANES, LANES, stride=2), :] = x[:, :LANES]
        table[pl.ds(i * 2 * LANES + 1, LANES, stride=2), :] = x[:, LANES:]
        return 0

    lax.fori_loop(0, 2 * rows // LANES, widen, 0)
    low = (4 << cell_bits) - 1

    def cell_at(code):
        return pl.ds(pl.multiple_of(code & low, 2), 2)

    def row_at(code):
        return pl.ds(pl.multiple_of(lax.shift_right_logical(code, cell_bits + 2), 2), 2)

    def source(s, _):
        head = lists[s * stride]
        steps = head & (FLAG - 1)
        begin = s * stride + LANES

        @pl.when(LANES + steps * GROUP > near)
        def _():
            read_far(s).wait()

        def step(at):
            new = []
            for k in range(GROUP):
                code = lists[at]
                new.append((code, sums[cell_at(code), :] + table[row_at(code), :]))
                at = at + steps
            for code, value in new:
                sums[cell_at(code), :] = value

        @pl.when(head < FLAG)
        def _():
            def two_steps(i, _):
                step(begin + 2 * i)
                step(begin + 2 * i + 1)
                return 0

            lax.fori_loop(0, lax.shift_right_logical(steps, 1), two_steps, 0)

            @pl.when((steps & 1) == 1)
            def _():
                step(begin + steps - 1)

        @pl.when(head >= FLAG)
        def _():
            def single(i, _):
                code = lists[begin + i]
                sums[cell_at(code), :] = sums[cell_at(code), :] + table[row_at(code), :]
                return 0

            lax.fori_loop(0, steps * GROUP, single, 0)

        return 0

    lax.fori_loop(0, n, source, 0)
    keeps = [
        pltpu.make_async_copy(
            sums.at[pl.ds(lo * K, size * (K // 2)), :], ref, sems.at[2 + c]
        )
        for c, ((lo, size, _), ref) in enumerate(zip(chains, keep_refs))
    ]
    for copy in keeps:
        copy.start()
    for packet, ref in zip(packets, packet_refs):
        sources = [(sums, chains[c][0] * K + rows) for c, rows in packet[1]]
        encode(packet, sources, ref, scales)
    for copy in keeps:
        copy.wait()


def merge_kernel(chains, arrived, packets, *refs):
    refs = list(refs)
    take = lambda k: [refs.pop(0) for _ in range(k)]
    kept, came = take(chains), take(len(arrived))
    keep_refs, packet_refs = take(chains), take(len(packets))
    sums, scales = refs[:chains], refs[chains]
    for ref, total in zip(kept, sums):
        total[...] = ref[...]
    for packet, ref in zip(arrived, came):
        add_packet(packet, ref, sums, scales)
    for total, ref in zip(sums, keep_refs):
        ref[...] = total[pl.ds(0, ref.shape[0]), :]
    for packet, ref in zip(packets, packet_refs):
        encode(packet, [(sums[c], rows) for c, rows in packet[1]], ref, scales)


def merge(kept, came, arrived, packets):
    last = not packets
    shapes = [
        jax.ShapeDtypeStruct((x.shape[0] if last else x.shape[0] // 2, LANES), x.dtype)
        for x in kept
    ] + [packet_shape(p) for p in packets]
    lines = max(x.shape[0] for x in came)
    outs = pl.pallas_call(
        functools.partial(merge_kernel, len(kept), arrived, packets),
        out_shape=shapes,
        in_specs=[pl.BlockSpec(memory_space=pltpu.VMEM)] * (len(kept) + len(came)),
        out_specs=[pl.BlockSpec(memory_space=pltpu.VMEM)] * len(shapes),
        scratch_shapes=[pltpu.VMEM(x.shape, x.dtype) for x in kept]
        + [pltpu.VMEM((scale_lines(lines) + 16, LANES), jnp.float32)],
        compiler_params=pltpu.CompilerParams(vmem_limit_bytes=16 * 1024 * 1024),
    )(*kept, *came)
    return list(outs[: len(kept)]), list(outs[len(kept) :])


def exchange(blocks, packets, n):
    return [
        lax.ppermute(block, "tm", [(i, i ^ (2 << packet[0])) for i in range(n)])
        for block, packet in zip(blocks, packets)
    ]


def per_device(item_table, item_shard, item_row, cluster_id, lengths):
    n = lax.axis_size("tm")
    users, slab = item_row.shape[1:]
    rows, width = item_table.shape
    total = users * slab
    owned = K // n
    m = bits_for(n) - 1
    cells = users * K // 2
    cell_bits = bits_for(cells)
    row_bits = bits_for(2 * rows)
    dest_shift = cell_bits + row_bits
    cap_rows = -(-4 * total // n // LANES)
    count_rows = users * owned // LANES
    req_rows = cap_rows + 1
    block_rows = -(-(1 + req_rows + count_rows) // SUB) * SUB
    chains = user_chains(users, m)
    dummy = cells * 2

    other = lax.ppermute(item_table, "tm", [(i, i ^ 1) for i in range(n)])
    buckets = pl.pallas_call(
        functools.partial(
            prepare_kernel, n, owned, rows, dest_shift, row_bits, cell_bits, req_rows, count_rows,
            dummy, chains,
        ),
        out_shape=jax.ShapeDtypeStruct((n, block_rows, LANES), jnp.int32),
        in_specs=[pl.BlockSpec(memory_space=pltpu.SMEM)]
        + [pl.BlockSpec(memory_space=pltpu.VMEM)] * 3,
        out_specs=pl.BlockSpec(memory_space=pltpu.VMEM),
        scratch_shapes=[
            pltpu.VMEM((LANES, LANES), jnp.int32),
            pltpu.VMEM((LANES + -(-(req_rows + 1) // SUB) * SUB, LANES), jnp.int32),
        ],
    )(
        lengths,
        item_shard.reshape(total // LANES, LANES),
        item_row.reshape(users, slab),
        cluster_id.reshape(users, slab),
    )
    requests = lax.all_to_all(buckets, "tm", split_axis=0, concat_axis=0, tiled=True)
    counts = jnp.sum(requests[:, 1 + req_rows : 1 + req_rows + count_rows, :], axis=0)
    counts = counts.reshape(users, owned).astype(jnp.float32)

    sums_rows = -(-(cells + 1) * 2 // 256) * 256
    lines = [size * (K // 2) for _, size, _ in chains]
    packets = packets_of(chains, 0, lines)
    parts = pl.pallas_call(
        functools.partial(add_kernel, n, block_rows * LANES, cell_bits, chains, packets),
        out_shape=[jax.ShapeDtypeStruct((r, LANES), jnp.float32) for r in lines]
        + [packet_shape(p) for p in packets],
        in_specs=[
            pl.BlockSpec(memory_space=pltpu.VMEM),
            pl.BlockSpec(memory_space=pl.ANY),
            pl.BlockSpec(memory_space=pl.ANY),
        ],
        out_specs=[pl.BlockSpec(memory_space=pl.ANY)] * len(chains)
        + [pl.BlockSpec(memory_space=pltpu.VMEM)] * len(packets),
        scratch_shapes=[
            pltpu.VMEM((rows * 2, width), jnp.bfloat16),
            pltpu.VMEM((rows * 4, LANES), jnp.float32),
            pltpu.VMEM((sums_rows, LANES), jnp.float32),
            pltpu.VMEM((scale_lines(cells * 2) + 16, LANES), jnp.float32),
            pltpu.SMEM((n * block_rows * LANES,), jnp.int32),
            pltpu.SemaphoreType.DMA((n,)),
            pltpu.SemaphoreType.DMA((n,)),
            pltpu.SemaphoreType.DMA((2 + len(chains),)),
        ],
        compiler_params=pltpu.CompilerParams(vmem_limit_bytes=32 * 1024 * 1024),
    )(requests.reshape(-1), item_table, other)
    kept, sent = list(parts[: len(chains)]), list(parts[len(chains) :])

    for stage in range(m):
        came = exchange(sent, packets, n)
        arrived = packets
        lines = [r // 2 for r in lines]
        packets = packets_of(chains, stage + 1, lines)
        kept, sent = merge(kept, came, arrived, packets)
    done = [x.reshape(size, owned, width) for x, (_, size, _) in zip(kept, chains)]
    return jnp.concatenate(done, axis=0) / jnp.maximum(counts, 1.0)[..., None]


def solution(mesh):
    return jax.shard_map(
        per_device,
        mesh=mesh,
        in_specs=(
            P("tm", None),
            P("tm", ("groups", "users"), None, None),
            P("tm", ("groups", "users"), None),
            P("tm", ("groups", "users"), None),
            P(("groups", "users")),
        ),
        out_specs=P(("groups", "users"), "tm", None),
        check_vma=False,
    )
```

```python
import functools
import math

import jax
import jax.numpy as jnp
from jax import lax
from jax.experimental import pallas as pl
from jax.experimental.pallas import tpu as pltpu
from jax.sharding import PartitionSpec as P

K = 1024
LANES = 128
SUB = 8
GROUP = 16
FLAG = 1 << 30
NONE = 2**31 - 1
CODE_TOP = 32766.0
NEAR = 512


def bits_for(count):
    return (count - 1).bit_length()


def user_chains(users, m):
    orders = [(0, 2, 1, 3), (2, 1, 0, 3), (1, 0, 3, 2)] if m == 4 else [tuple(range(m))] * 3
    sizes = [-(-users * 3 // 8), users * 3 // 8]
    sizes.append(users - sum(sizes))
    chains, lo = [], 0
    for size, order in zip(sizes, orders):
        if size:
            chains.append((lo, size, order))
        lo += size
    return chains


def packets_of(chains, stage, rows):
    if stage == len(chains[0][2]):
        return []
    bits = {}
    for c, (_, _, order) in enumerate(chains):
        bits.setdefault(order[stage], []).append(c)
    return [
        (bit, [(c, rows[c]) for c in members], all(rows[c] % LANES == 0 for c in members))
        for bit, members in bits.items()
    ]


def packet_shape(packet):
    _, members, coded = packet
    lines = sum(rows for _, rows in members)
    if not coded:
        return jax.ShapeDtypeStruct((lines, LANES), jnp.float32)
    return jax.ShapeDtypeStruct((lines + scale_lines(lines), LANES), jnp.int16)


def scale_lines(lines):
    return -(-lines // LANES // 16) * 16


def scale_of(exponent):
    return jnp.exp(exponent * (math.log(2.0) / 64.0))


def encode(packet, sources, out_ref, scales):
    done = 0
    for (_, rows), (ref, start) in zip(packet[1], sources):
        if not packet[2]:
            out_ref[pl.ds(done, rows), :] = ref[pl.ds(start, rows), :]
            done += rows
            continue

        def block(i, _, ref=ref, start=start, done=done):
            x = ref[pl.ds(start + i * LANES, LANES), :]
            top = jnp.maximum(jnp.max(jnp.abs(x), axis=0, keepdims=True), 1e-33)
            exponent = jnp.ceil(jnp.log(top) * (64.0 / math.log(2.0)))
            code = jnp.round(x * (CODE_TOP / scale_of(exponent)))
            code = code.astype(jnp.int32).astype(jnp.int16)
            out_ref[pl.ds(pl.multiple_of(done + i * LANES, LANES), LANES), :] = code
            scales[pl.ds(done // LANES + i, 1), :] = exponent
            return 0

        lax.fori_loop(0, rows // LANES, block, 0)
        done += rows
    if packet[2]:
        out_ref[pl.ds(done, scale_lines(done)), :] = (
            scales[pl.ds(0, scale_lines(done)), :].astype(jnp.int32).astype(jnp.int16)
        )


def add_packet(packet, ref, sums, scales):
    if packet[2]:
        lines = sum(rows for _, rows in packet[1])
        scales[pl.ds(0, scale_lines(lines)), :] = ref[
            pl.ds(lines, scale_lines(lines)), :
        ].astype(jnp.float32)
    done = 0
    for c, rows in packet[1]:
        if not packet[2]:
            sums[c][...] = sums[c][...] + ref[pl.ds(done, rows), :]
            done += rows
            continue

        def block(i, _, c=c, done=done):
            exponent = scales[pl.ds(done // LANES + i, 1), :]
            code = ref[pl.ds(pl.multiple_of(done + i * LANES, LANES), LANES), :]
            at = pl.ds(pl.multiple_of(i * LANES, LANES), LANES)
            value = code.astype(jnp.float32) * (scale_of(exponent) * (1.0 / CODE_TOP))
            sums[c][at, :] = sums[c][at, :] + value
            return 0

        lax.fori_loop(0, rows // LANES, block, 0)
        done += rows


def sort_tiles(tiles):
    count = len(tiles)
    tile_bits = bits_for(count)
    sub = lax.broadcasted_iota(jnp.int32, (SUB, LANES), 0)
    lane = lax.broadcasted_iota(jnp.int32, (SUB, LANES), 1)
    total_bits = tile_bits + 3 + 7

    def bit_mask(bit):
        if bit < tile_bits + 3:
            return ((sub >> (bit - tile_bits)) & 1) == 1
        return ((lane >> (bit - tile_bits - 3)) & 1) == 1

    masks = {b: bit_mask(b) for b in range(tile_bits, total_bits)}
    flips = {b: jnp.where(masks[b], -1, 0) for b in masks}

    def flip(t, phase):
        if phase >= total_bits:
            return 0
        if phase < tile_bits:
            return -1 if (t >> phase) & 1 else 0
        return flips[phase]

    for phase in range(1, total_bits + 1):
        changed = []
        for t in range(count):
            old = flip(t, phase - 1) if phase > 1 else 0
            new = flip(t, phase)
            if isinstance(old, int) and isinstance(new, int):
                turn = old ^ new
                changed.append(tiles[t] if turn == 0 else ~tiles[t])
            else:
                changed.append(tiles[t] ^ (old ^ new))
        tiles = changed
        for bit in reversed(range(phase)):
            if bit < tile_bits:
                step = 1 << bit
                tiles = list(tiles)
                for t in range(count):
                    if not t & step:
                        a, b = tiles[t], tiles[t | step]
                        tiles[t], tiles[t | step] = jnp.minimum(a, b), jnp.maximum(a, b)
                continue
            if bit < tile_bits + 3:
                axis, step, size = 0, 1 << (bit - tile_bits), SUB
            else:
                axis, step, size = 1, 1 << (bit - tile_bits - 3), LANES
            upper = masks[bit]
            moved = []
            for x in tiles:
                down = pltpu.roll(x, step, axis=axis)
                if 2 * step == size:
                    other = down
                else:
                    other = jnp.where(upper, down, pltpu.roll(x, size - step, axis=axis))
                moved.append(
                    jnp.where(upper, jnp.maximum(x, other), jnp.minimum(x, other))
                )
            tiles = moved
    return tiles


def prepare_kernel(
    n, owned, table_rows, dest_shift, row_bits, cell_bits, req_rows, count_rows, dummy, chains,
    lengths_ref, shard_ref, row_ref, cluster_ref, out_ref, order, pad,
):
    users, slab = row_ref.shape
    sub = lax.broadcasted_iota(jnp.int32, (SUB, LANES), 0)
    lane = lax.broadcasted_iota(jnp.int32, (SUB, LANES), 1)
    me = lax.axis_index("tm")
    length = jnp.zeros((SUB, LANES), jnp.int32)
    live_total = jnp.int32(0)
    for u in range(users):
        length = jnp.where(sub == u, lengths_ref[u], length)
        live_total += jnp.clip(lengths_ref[u] - me * slab, 0, slab)
    length = length - me * slab

    base = jnp.zeros((SUB, LANES), jnp.int32)
    in_chain = jnp.zeros((SUB, LANES), jnp.int32)
    chain_size = jnp.zeros((SUB, LANES), jnp.int32)
    chain_at = []
    for lo, size, _ in chains:
        inside = (sub >= lo) & (sub < lo + size)
        base = jnp.where(inside, lo * (K // 2), base)
        in_chain = jnp.where(inside, sub - lo, in_chain)
        chain_size = jnp.where(inside, size, chain_size)
        chain_at.append(inside)

    owner_shift = bits_for(owned)
    tiles = []
    hot_owner = [[] for _ in range(count_rows)]
    hot_slot = [[] for _ in range(count_rows)]
    per_row = LANES // owned
    owner_iota = lax.broadcasted_iota(jnp.int32, (n, LANES), 0)
    slot_iota = lax.broadcasted_iota(jnp.int32, (LANES, LANES), 0)
    for j in range(slab // LANES):
        at = pl.ds(j * LANES, LANES)
        row, cluster = row_ref[:, at], cluster_ref[:, at]
        shard = shard_ref[pl.ds(j, users, stride=slab // LANES), :]
        owner = lax.shift_right_logical(cluster, owner_shift)
        low = cluster & (owned - 1)
        live = lane + j * LANES < length
        dest = (shard & ~1) | (owner & 1)
        away = lax.shift_right_logical(owner ^ dest, 1)
        spread = jnp.zeros((SUB, LANES), jnp.int32)
        by_order = {}
        for (_, _, bits), inside in zip(chains, chain_at):
            if bits not in by_order:
                turned = jnp.zeros((SUB, LANES), jnp.int32)
                for bit in bits:
                    turned = turned * 2 + ((away >> bit) & 1)
                by_order[bits] = turned
            spread = jnp.where(inside, by_order[bits], spread)
        cell = base + ((spread * chain_size + in_chain) << owner_shift) + low
        there = ((shard ^ owner) & 1) * table_rows + row
        key = (dest << dest_shift) | (cell << row_bits) | there
        tiles.append(jnp.where(live, key, NONE))
        live_owner = jnp.where(live, owner, -1)
        for u in range(users):
            r = u // per_row
            hot_owner[r].append((owner_iota == live_owner[u : u + 1, :]).astype(jnp.bfloat16))
            target = low[u : u + 1, :] + (u % per_row) * owned
            hot_slot[r].append((slot_iota == target).astype(jnp.bfloat16))

    for r in range(count_rows):
        counts = jnp.zeros((n, LANES), jnp.float32)
        for a, b in zip(hot_owner[r], hot_slot[r]):
            counts += lax.dot_general(
                a, b, (((1,), (1,)), ((), ())), preferred_element_type=jnp.float32
            )
        counts = counts.astype(jnp.int32)
        for d in range(n):
            out_ref[d, pl.ds(1 + req_rows + r, 1), :] = counts[d : d + 1, :]

    ends = []
    for d in range(n - 1):
        below = jnp.zeros((SUB, LANES), jnp.float32)
        for x in tiles:
            below += (x < ((d + 1) << dest_shift)).astype(jnp.float32)
        ends.append(jnp.sum(below).astype(jnp.int32))
    ends.append(live_total)

    empty = jnp.full((SUB, LANES), NONE, jnp.int32)
    tiles = sort_tiles(tiles + [empty] * ((1 << bits_for(len(tiles))) - len(tiles)))
    count = len(tiles)
    for t, x in enumerate(tiles):
        order[pl.ds(t * SUB, SUB), :] = x
    lines = [order[pl.ds(s, count, stride=SUB), :] for s in range(SUB)]
    straight = jnp.concatenate(lines, axis=0).T
    pad[0:LANES, :] = straight
    pad[LANES:, :] = jnp.full((pad.shape[0] - LANES, LANES), NONE, jnp.int32)

    lane = lax.broadcasted_iota(jnp.int32, (req_rows, LANES), 1)
    slot = lax.broadcasted_iota(jnp.int32, (req_rows, LANES), 0) * LANES + lane
    nothing = jnp.full((1, LANES), -1, jnp.int32)

    def ahead(x, by):
        turned = pltpu.roll(x, (LANES - by) & (LANES - 1), axis=1)
        return jnp.where(lane < LANES - by, turned[:req_rows], turned[1:])

    start = jnp.int32(0)
    for d in range(n):
        count = ends[d] - start
        steps = lax.shift_right_logical(count + GROUP - 1, bits_for(GROUP))
        first = lax.shift_right_logical(start, bits_for(LANES))
        mine = ahead(pad[pl.ds(first, req_rows + 1), :], start & (LANES - 1))
        there = mine & (2 * table_rows - 1)
        cell = lax.shift_right_logical(mine, row_bits) & ((1 << cell_bits) - 1)
        code = jnp.where(slot < count, (there << (cell_bits + 3)) | (cell << 1), dummy)
        cell = jnp.where(slot < count, cell, -1)
        later = ahead(jnp.concatenate([cell, nothing], axis=0), steps)
        twice = jnp.max(jnp.where((cell == later) & (cell >= 0), 1.0, 0.0))
        out_ref[d, pl.ds(1, req_rows), :] = code
        head = steps | jnp.where(twice > 0, FLAG, 0)
        out_ref[d, pl.ds(0, 1), :] = jnp.full((1, LANES), head, jnp.int32)
        start = ends[d]


def add_kernel(n, stride, cell_bits, chains, packets, request_ref, own_ref, other_ref, *rest):
    keep_refs = rest[: len(chains)]
    packet_refs = rest[len(chains) : len(chains) + len(packets)]
    narrow, table, sums, scales, lists, near_sems, far_sems, sems = rest[
        len(chains) + len(packets) :
    ]
    near = min(NEAR, stride)

    def read(s, at, size, read_sems):
        at = pl.ds(pl.multiple_of(s * stride + at, LANES), size)
        return pltpu.make_async_copy(request_ref.at[at], lists.at[at], read_sems.at[s])

    def read_near(s):
        return read(s, 0, near, near_sems)

    def read_far(s):
        return read(s, near, stride - near, far_sems)

    def start_near(s, _):
        read_near(s).start()
        return 0

    rows = own_ref.shape[0]
    tables = [
        pltpu.make_async_copy(ref, narrow.at[pl.ds(part * rows, rows), :], sems.at[part])
        for part, ref in enumerate((own_ref, other_ref))
    ]
    for copy in tables:
        copy.start()
    lax.fori_loop(0, n, start_near, 0)

    def clear(i, _):
        sums[pl.ds(i * 256, 256), :] = jnp.zeros((256, LANES), jnp.float32)
        return 0

    lax.fori_loop(0, sums.shape[0] // 256, clear, 0)

    def arrive(s, _):
        read_near(s).wait()

        @pl.when(LANES + (lists[s * stride] & (FLAG - 1)) * GROUP > near)
        def _():
            read_far(s).start()

        return 0

    lax.fori_loop(0, n, arrive, 0)
    for copy in tables:
        copy.wait()

    def widen(i, _):
        x = narrow[pl.ds(i * LANES, LANES), :].astype(jnp.float32)
        table[pl.ds(i * 2 * LANES, LANES, stride=2), :] = x[:, :LANES]
        table[pl.ds(i * 2 * LANES + 1, LANES, stride=2), :] = x[:, LANES:]
        return 0

    lax.fori_loop(0, 2 * rows // LANES, widen, 0)
    low = (4 << cell_bits) - 1

    def cell_at(code):
        return pl.ds(pl.multiple_of(code & low, 2), 2)

    def row_at(code):
        return pl.ds(pl.multiple_of(lax.shift_right_logical(code, cell_bits + 2), 2), 2)

    def source(s, _):
        head = lists[s * stride]
        steps = head & (FLAG - 1)
        begin = s * stride + LANES

        @pl.when(LANES + steps * GROUP > near)
        def _():
            read_far(s).wait()

        def step(at):
            new = []
            for k in range(GROUP):
                code = lists[at]
                new.append((code, sums[cell_at(code), :] + table[row_at(code), :]))
                at = at + steps
            for code, value in new:
                sums[cell_at(code), :] = value

        @pl.when(head < FLAG)
        def _():
            def two_steps(i, _):
                step(begin + 2 * i)
                step(begin + 2 * i + 1)
                return 0

            lax.fori_loop(0, lax.shift_right_logical(steps, 1), two_steps, 0)

            @pl.when((steps & 1) == 1)
            def _():
                step(begin + steps - 1)

        @pl.when(head >= FLAG)
        def _():
            def single(i, _):
                code = lists[begin + i]
                sums[cell_at(code), :] = sums[cell_at(code), :] + table[row_at(code), :]
                return 0

            lax.fori_loop(0, steps * GROUP, single, 0)

        return 0

    lax.fori_loop(0, n, source, 0)
    keeps = [
        pltpu.make_async_copy(
            sums.at[pl.ds(lo * K, size * (K // 2)), :], ref, sems.at[2 + c]
        )
        for c, ((lo, size, _), ref) in enumerate(zip(chains, keep_refs))
    ]
    for copy in keeps:
        copy.start()
    for packet, ref in zip(packets, packet_refs):
        sources = [(sums, chains[c][0] * K + rows) for c, rows in packet[1]]
        encode(packet, sources, ref, scales)
    for copy in keeps:
        copy.wait()


def merge_kernel(chains, arrived, packets, *refs):
    refs = list(refs)
    take = lambda k: [refs.pop(0) for _ in range(k)]
    kept, came = take(chains), take(len(arrived))
    keep_refs, packet_refs = take(chains), take(len(packets))
    sums, scales = refs[:chains], refs[chains]
    for ref, total in zip(kept, sums):
        total[...] = ref[...]
    for packet, ref in zip(arrived, came):
        add_packet(packet, ref, sums, scales)
    for total, ref in zip(sums, keep_refs):
        ref[...] = total[pl.ds(0, ref.shape[0]), :]
    for packet, ref in zip(packets, packet_refs):
        encode(packet, [(sums[c], rows) for c, rows in packet[1]], ref, scales)


def merge(kept, came, arrived, packets):
    last = not packets
    shapes = [
        jax.ShapeDtypeStruct((x.shape[0] if last else x.shape[0] // 2, LANES), x.dtype)
        for x in kept
    ] + [packet_shape(p) for p in packets]
    lines = max(x.shape[0] for x in came)
    outs = pl.pallas_call(
        functools.partial(merge_kernel, len(kept), arrived, packets),
        out_shape=shapes,
        in_specs=[pl.BlockSpec(memory_space=pltpu.VMEM)] * (len(kept) + len(came)),
        out_specs=[pl.BlockSpec(memory_space=pltpu.VMEM)] * len(shapes),
        scratch_shapes=[pltpu.VMEM(x.shape, x.dtype) for x in kept]
        + [pltpu.VMEM((scale_lines(lines) + 16, LANES), jnp.float32)],
        compiler_params=pltpu.CompilerParams(vmem_limit_bytes=16 * 1024 * 1024),
    )(*kept, *came)
    return list(outs[: len(kept)]), list(outs[len(kept) :])


def exchange(blocks, packets, n):
    return [
        lax.ppermute(block, "tm", [(i, i ^ (2 << packet[0])) for i in range(n)])
        for block, packet in zip(blocks, packets)
    ]


def per_device(item_table, item_shard, item_row, cluster_id, lengths):
    n = lax.axis_size("tm")
    users, slab = item_row.shape[1:]
    rows, width = item_table.shape
    total = users * slab
    owned = K // n
    m = bits_for(n) - 1
    cells = users * K // 2
    cell_bits = bits_for(cells)
    row_bits = bits_for(2 * rows)
    dest_shift = cell_bits + row_bits
    cap_rows = -(-4 * total // n // LANES)
    count_rows = users * owned // LANES
    req_rows = cap_rows + 1
    block_rows = -(-(1 + req_rows + count_rows) // SUB) * SUB
    chains = user_chains(users, m)
    dummy = cells * 2

    other = lax.ppermute(item_table, "tm", [(i, i ^ 1) for i in range(n)])
    buckets = pl.pallas_call(
        functools.partial(
            prepare_kernel, n, owned, rows, dest_shift, row_bits, cell_bits, req_rows, count_rows,
            dummy, chains,
        ),
        out_shape=jax.ShapeDtypeStruct((n, block_rows, LANES), jnp.int32),
        in_specs=[pl.BlockSpec(memory_space=pltpu.SMEM)]
        + [pl.BlockSpec(memory_space=pltpu.VMEM)] * 3,
        out_specs=pl.BlockSpec(memory_space=pltpu.VMEM),
        scratch_shapes=[
            pltpu.VMEM((LANES, LANES), jnp.int32),
            pltpu.VMEM((LANES + -(-(req_rows + 1) // SUB) * SUB, LANES), jnp.int32),
        ],
    )(
        lengths,
        item_shard.reshape(total // LANES, LANES),
        item_row.reshape(users, slab),
        cluster_id.reshape(users, slab),
    )
    requests = lax.all_to_all(buckets, "tm", split_axis=0, concat_axis=0, tiled=True)
    counts = jnp.sum(requests[:, 1 + req_rows : 1 + req_rows + count_rows, :], axis=0)
    counts = counts.reshape(users, owned).astype(jnp.float32)

    sums_rows = -(-(cells + 1) * 2 // 256) * 256
    lines = [size * (K // 2) for _, size, _ in chains]
    packets = packets_of(chains, 0, lines)
    parts = pl.pallas_call(
        functools.partial(add_kernel, n, block_rows * LANES, cell_bits, chains, packets),
        out_shape=[jax.ShapeDtypeStruct((r, LANES), jnp.float32) for r in lines]
        + [packet_shape(p) for p in packets],
        in_specs=[
            pl.BlockSpec(memory_space=pltpu.VMEM),
            pl.BlockSpec(memory_space=pl.ANY),
            pl.BlockSpec(memory_space=pl.ANY),
        ],
        out_specs=[pl.BlockSpec(memory_space=pl.ANY)] * len(chains)
        + [pl.BlockSpec(memory_space=pltpu.VMEM)] * len(packets),
        scratch_shapes=[
            pltpu.VMEM((rows * 2, width), jnp.bfloat16),
            pltpu.VMEM((rows * 4, LANES), jnp.float32),
            pltpu.VMEM((sums_rows, LANES), jnp.float32),
            pltpu.VMEM((scale_lines(cells * 2) + 16, LANES), jnp.float32),
            pltpu.SMEM((n * block_rows * LANES,), jnp.int32),
            pltpu.SemaphoreType.DMA((n,)),
            pltpu.SemaphoreType.DMA((n,)),
            pltpu.SemaphoreType.DMA((2 + len(chains),)),
        ],
        compiler_params=pltpu.CompilerParams(vmem_limit_bytes=48 * 1024 * 1024),
    )(requests.reshape(-1), item_table, other)
    kept, sent = list(parts[: len(chains)]), list(parts[len(chains) :])

    for stage in range(m):
        came = exchange(sent, packets, n)
        arrived = packets
        lines = [r // 2 for r in lines]
        packets = packets_of(chains, stage + 1, lines)
        kept, sent = merge(kept, came, arrived, packets)
    done = [x.reshape(size, owned, width) for x, (_, size, _) in zip(kept, chains)]
    return jnp.concatenate(done, axis=0) / jnp.maximum(counts, 1.0)[..., None]


def solution(mesh):
    return jax.shard_map(
        per_device,
        mesh=mesh,
        in_specs=(
            P("tm", None),
            P("tm", ("groups", "users"), None, None),
            P("tm", ("groups", "users"), None),
            P("tm", ("groups", "users"), None),
            P(("groups", "users")),
        ),
        out_specs=P(("groups", "users"), "tm", None),
        check_vma=False,
    )
```

```python
import functools
import math

import jax
import jax.numpy as jnp
from jax import lax
from jax.experimental import pallas as pl
from jax.experimental.pallas import tpu as pltpu
from jax.sharding import PartitionSpec as P

K = 1024
LANES = 128
SUB = 8
RUNS = 16
MODE = 16
NONE = 2**31 - 1
CODE_TOP = 32766.0


def bits_for(count):
    return (count - 1).bit_length()


def user_chains(users, m):
    orders = [(0, 2, 1, 3), (2, 1, 0, 3), (1, 0, 3, 2)] if m == 4 else [tuple(range(m))] * 3
    sizes = [-(-users * 3 // 8), users * 3 // 8]
    sizes.append(users - sum(sizes))
    chains, lo = [], 0
    for size, order in zip(sizes, orders):
        if size:
            chains.append((lo, size, order))
        lo += size
    return chains


def packets_of(chains, stage, rows):
    if stage == len(chains[0][2]):
        return []
    bits = {}
    for c, (_, _, order) in enumerate(chains):
        bits.setdefault(order[stage], []).append(c)
    return [
        (bit, [(c, rows[c]) for c in members], all(rows[c] % LANES == 0 for c in members))
        for bit, members in bits.items()
    ]


def packet_shape(packet):
    _, members, coded = packet
    lines = sum(rows for _, rows in members)
    if not coded:
        return jax.ShapeDtypeStruct((lines, LANES), jnp.float32)
    return jax.ShapeDtypeStruct((lines + scale_lines(lines), LANES), jnp.int16)


def scale_lines(lines):
    return -(-lines // LANES // 16) * 16


def scale_of(exponent):
    return jnp.exp(exponent * (math.log(2.0) / 64.0))


def encode(packet, sources, out_ref, scales):
    done = 0
    for (_, rows), (ref, start) in zip(packet[1], sources):
        if not packet[2]:
            out_ref[pl.ds(done, rows), :] = ref[pl.ds(start, rows), :]
            done += rows
            continue

        def block(i, _, ref=ref, start=start, done=done):
            x = ref[pl.ds(start + i * LANES, LANES), :]
            top = jnp.maximum(jnp.max(jnp.abs(x), axis=0, keepdims=True), 1e-33)
            exponent = jnp.ceil(jnp.log(top) * (64.0 / math.log(2.0)))
            code = jnp.round(x * (CODE_TOP / scale_of(exponent)))
            code = code.astype(jnp.int32).astype(jnp.int16)
            out_ref[pl.ds(pl.multiple_of(done + i * LANES, LANES), LANES), :] = code
            scales[pl.ds(done // LANES + i, 1), :] = exponent
            return 0

        lax.fori_loop(0, rows // LANES, block, 0)
        done += rows
    if packet[2]:
        out_ref[pl.ds(done, scale_lines(done)), :] = (
            scales[pl.ds(0, scale_lines(done)), :].astype(jnp.int32).astype(jnp.int16)
        )


def add_packet(packet, ref, sums, scales):
    if packet[2]:
        lines = sum(rows for _, rows in packet[1])
        scales[pl.ds(0, scale_lines(lines)), :] = ref[
            pl.ds(lines, scale_lines(lines)), :
        ].astype(jnp.float32)
    done = 0
    for c, rows in packet[1]:
        if not packet[2]:
            sums[c][...] = sums[c][...] + ref[pl.ds(done, rows), :]
            done += rows
            continue

        def block(i, _, c=c, done=done):
            exponent = scales[pl.ds(done // LANES + i, 1), :]
            code = ref[pl.ds(pl.multiple_of(done + i * LANES, LANES), LANES), :]
            at = pl.ds(pl.multiple_of(i * LANES, LANES), LANES)
            value = code.astype(jnp.float32) * (scale_of(exponent) * (1.0 / CODE_TOP))
            sums[c][at, :] = sums[c][at, :] + value
            return 0

        lax.fori_loop(0, rows // LANES, block, 0)
        done += rows


def sort_tiles(tiles):
    count = len(tiles)
    tile_bits = bits_for(count)
    sub = lax.broadcasted_iota(jnp.int32, (SUB, LANES), 0)
    lane = lax.broadcasted_iota(jnp.int32, (SUB, LANES), 1)
    total_bits = tile_bits + 3 + 7

    def bit_mask(bit):
        if bit < tile_bits + 3:
            return ((sub >> (bit - tile_bits)) & 1) == 1
        return ((lane >> (bit - tile_bits - 3)) & 1) == 1

    masks = {b: bit_mask(b) for b in range(tile_bits, total_bits)}
    flips = {b: jnp.where(masks[b], -1, 0) for b in masks}

    def flip(t, phase):
        if phase >= total_bits:
            return 0
        if phase < tile_bits:
            return -1 if (t >> phase) & 1 else 0
        return flips[phase]

    for phase in range(1, total_bits + 1):
        changed = []
        for t in range(count):
            old = flip(t, phase - 1) if phase > 1 else 0
            new = flip(t, phase)
            if isinstance(old, int) and isinstance(new, int):
                turn = old ^ new
                changed.append(tiles[t] if turn == 0 else ~tiles[t])
            else:
                changed.append(tiles[t] ^ (old ^ new))
        tiles = changed
        for bit in reversed(range(phase)):
            if bit < tile_bits:
                step = 1 << bit
                tiles = list(tiles)
                for t in range(count):
                    if not t & step:
                        a, b = tiles[t], tiles[t | step]
                        tiles[t], tiles[t | step] = jnp.minimum(a, b), jnp.maximum(a, b)
                continue
            if bit < tile_bits + 3:
                axis, step, size = 0, 1 << (bit - tile_bits), SUB
            else:
                axis, step, size = 1, 1 << (bit - tile_bits - 3), LANES
            upper = masks[bit]
            moved = []
            for x in tiles:
                down = pltpu.roll(x, step, axis=axis)
                if 2 * step == size:
                    other = down
                else:
                    other = jnp.where(upper, down, pltpu.roll(x, size - step, axis=axis))
                moved.append(
                    jnp.where(upper, jnp.maximum(x, other), jnp.minimum(x, other))
                )
            tiles = moved
    return tiles


def prepare_kernel(
    n, owned, table_rows, dest_shift, row_bits, cell_bits, dummy, chains,
    lengths_ref, shard_ref, row_ref, cluster_ref, out_ref, order, straight, runs,
):
    users, slab = row_ref.shape
    sub = lax.broadcasted_iota(jnp.int32, (SUB, LANES), 0)
    lane = lax.broadcasted_iota(jnp.int32, (SUB, LANES), 1)
    me = lax.axis_index("tm")
    length = jnp.zeros((SUB, LANES), jnp.int32)
    live_total = jnp.int32(0)
    for u in range(users):
        length = jnp.where(sub == u, lengths_ref[u], length)
        live_total += jnp.clip(lengths_ref[u] - me * slab, 0, slab)
    length = length - me * slab

    base = jnp.zeros((SUB, LANES), jnp.int32)
    in_chain = jnp.zeros((SUB, LANES), jnp.int32)
    chain_size = jnp.zeros((SUB, LANES), jnp.int32)
    chain_at = []
    for lo, size, _ in chains:
        inside = (sub >= lo) & (sub < lo + size)
        base = jnp.where(inside, lo * (K // 2), base)
        in_chain = jnp.where(inside, sub - lo, in_chain)
        chain_size = jnp.where(inside, size, chain_size)
        chain_at.append(inside)

    owner_shift = bits_for(owned)
    tiles = []
    spare = LANES - owned
    hot_owner = [[] for _ in range(users)]
    hot_slot = [[] for _ in range(users)]
    owner_iota = lax.broadcasted_iota(jnp.int32, (n, LANES), 0)
    slot_iota = lax.broadcasted_iota(jnp.int32, (LANES, LANES), 0)
    for j in range(slab // LANES):
        at = pl.ds(j * LANES, LANES)
        row, cluster = row_ref[:, at], cluster_ref[:, at]
        shard = shard_ref[pl.ds(j, users, stride=slab // LANES), :]
        owner = lax.shift_right_logical(cluster, owner_shift)
        low = cluster & (owned - 1)
        live = lane + j * LANES < length
        dest = (shard & ~1) | (owner & 1)
        away = lax.shift_right_logical(owner ^ dest, 1)
        spread = jnp.zeros((SUB, LANES), jnp.int32)
        by_order = {}
        for (_, _, bits), inside in zip(chains, chain_at):
            if bits not in by_order:
                turned = jnp.zeros((SUB, LANES), jnp.int32)
                for bit in bits:
                    turned = turned * 2 + ((away >> bit) & 1)
                by_order[bits] = turned
            spread = jnp.where(inside, by_order[bits], spread)
        cell = base + ((spread * chain_size + in_chain) << owner_shift) + low
        there = ((shard ^ owner) & 1) * table_rows + row
        key = (dest << dest_shift) | (cell << row_bits) | there
        tiles.append(jnp.where(live, key, NONE))
        live_owner = jnp.where(live, owner, -1)
        for u in range(users):
            hot_owner[u].append((owner_iota == live_owner[u : u + 1, :]).astype(jnp.bfloat16))
            hot_slot[u].append((slot_iota == low[u : u + 1, :] + spare).astype(jnp.bfloat16))

    for u in range(users):
        counts = jnp.zeros((n, LANES), jnp.float32)
        for a, b in zip(hot_owner[u], hot_slot[u]):
            counts += lax.dot_general(
                a, b, (((1,), (1,)), ((), ())), preferred_element_type=jnp.float32
            )
        counts = counts.astype(jnp.int32)
        for d in range(n):
            out_ref[d, pl.ds(u, 1), :] = counts[d : d + 1, :]

    ends = []
    for d in range(n - 1):
        below = jnp.zeros((SUB, LANES), jnp.float32)
        for x in tiles:
            below += (x < ((d + 1) << dest_shift)).astype(jnp.float32)
        ends.append(jnp.sum(below).astype(jnp.int32))
    ends.append(live_total)

    empty = jnp.full((SUB, LANES), NONE, jnp.int32)
    tiles = sort_tiles(tiles + [empty] * ((1 << bits_for(len(tiles))) - len(tiles)))
    count = len(tiles)
    for t, x in enumerate(tiles):
        order[pl.ds(t * SUB, SUB), :] = x
    lines = [order[pl.ds(s, count, stride=SUB), :] for s in range(SUB)]
    straight[...] = jnp.concatenate(lines, axis=0).T

    at = (RUNS, LANES)
    run = lax.broadcasted_iota(jnp.int32, at, 0)
    lane = lax.broadcasted_iota(jnp.int32, at, 1)
    one_line = lax.broadcasted_iota(jnp.int32, (1, LANES), 1)
    start = jnp.int32(0)
    for d in range(n):
        count = ends[d] - start
        steps = lax.shift_right_logical(count + RUNS - 1, bits_for(RUNS))
        for j in range(RUNS):
            begin = start + j * steps
            off = begin & (LANES - 1)
            two = straight[pl.ds(lax.shift_right_logical(begin, bits_for(LANES)), 2), :]
            two = pltpu.roll(two, (LANES - off) & (LANES - 1), axis=1)
            runs[pl.ds(d * RUNS + j, 1), :] = jnp.where(one_line < LANES - off, two[:1], two[1:])
        mine = runs[pl.ds(d * RUNS, RUNS), :]
        valid = (lane < steps) & (run * steps + lane < count)
        there = mine & (2 * table_rows - 1)
        cell = lax.shift_right_logical(mine, row_bits) & ((1 << cell_bits) - 1)
        code = jnp.where(valid, (there << (cell_bits + 3)) | (cell << 1), dummy)
        cell = jnp.where(valid, cell, -1)
        half = lax.shift_right_logical(steps + 1, 1)
        following = jnp.where(run < RUNS - 1, pltpu.roll(cell, RUNS - 1, axis=0), -2)
        between = pltpu.roll(cell, (LANES - half) & (LANES - 1), axis=1)
        one = (cell >= 0) & (cell == following)
        two = (between >= 0) & (lane < half) & ((between == cell) | (between == following))
        mode = jnp.max(jnp.where(one, 2.0, jnp.where(two, 1.0, 0.0))).astype(jnp.int32)
        head = jnp.full((RUNS, LANES), steps | (mode << MODE), jnp.int32)
        beside = jnp.where(run < users, out_ref[d], head)
        out_ref[d] = jnp.where(lane < spare, code, beside)
        start = ends[d]


def add_kernel(n, head_at, cell_bits, chains, packets, request_ref, own_ref, other_ref, *rest):
    keep_refs = rest[: len(chains)]
    packet_refs = rest[len(chains) : len(chains) + len(packets)]
    narrow, table, sums, scales, lists, list_sems, sems = rest[
        len(chains) + len(packets) :
    ]
    stride = RUNS * LANES

    def read(s):
        at = pl.ds(pl.multiple_of(s * stride, stride), stride)
        return pltpu.make_async_copy(request_ref.at[at], lists.at[at], list_sems.at[s])

    def start_read(s, _):
        read(s).start()
        return 0

    rows = own_ref.shape[0]
    tables = [
        pltpu.make_async_copy(ref, narrow.at[pl.ds(part * rows, rows), :], sems.at[part])
        for part, ref in enumerate((own_ref, other_ref))
    ]
    for copy in tables:
        copy.start()
    lax.fori_loop(0, n, start_read, 0)

    def clear(i, _):
        sums[pl.ds(i * 256, 256), :] = jnp.zeros((256, LANES), jnp.float32)
        return 0

    lax.fori_loop(0, sums.shape[0] // 256, clear, 0)

    for copy in tables:
        copy.wait()

    def widen(i, _):
        x = narrow[pl.ds(i * LANES, LANES), :].astype(jnp.float32)
        table[pl.ds(i * 2 * LANES, LANES, stride=2), :] = x[:, :LANES]
        table[pl.ds(i * 2 * LANES + 1, LANES, stride=2), :] = x[:, LANES:]
        return 0

    lax.fori_loop(0, 2 * rows // LANES, widen, 0)
    low = (4 << cell_bits) - 1

    def cell_at(code):
        return pl.ds(pl.multiple_of(code & low, 2), 2)

    def row_at(code):
        return pl.ds(pl.multiple_of(lax.shift_right_logical(code, cell_bits + 2), 2), 2)

    def add_all(ats):
        new = []
        for at in ats:
            for k in range(RUNS):
                code = lists[at + k * LANES]
                new.append((code, sums[cell_at(code), :] + table[row_at(code), :]))
        for code, value in new:
            sums[cell_at(code), :] = value

    def source(s, _):
        read(s).wait()
        begin = s * stride
        head = lists[begin + head_at]
        steps = head & ((1 << MODE) - 1)
        mode = lax.shift_right_logical(head, MODE)
        half = lax.shift_right_logical(steps + 1, 1)

        @pl.when(mode == 0)
        def _():
            def step(i, _):
                add_all([begin + i, begin + half + i])
                return 0

            lax.fori_loop(0, half, step, 0)

        @pl.when(mode == 1)
        def _():
            def step(i, _):
                add_all([begin + i])
                return 0

            lax.fori_loop(0, steps, step, 0)

        @pl.when(mode == 2)
        def _():
            def step(i, _):
                for k in range(RUNS):
                    code = lists[begin + i + k * LANES]
                    sums[cell_at(code), :] = sums[cell_at(code), :] + table[row_at(code), :]
                return 0

            lax.fori_loop(0, steps, step, 0)

        return 0

    lax.fori_loop(0, n, source, 0)
    keeps = [
        pltpu.make_async_copy(
            sums.at[pl.ds(lo * K, size * (K // 2)), :], ref, sems.at[2 + c]
        )
        for c, ((lo, size, _), ref) in enumerate(zip(chains, keep_refs))
    ]
    for copy in keeps:
        copy.start()
    for packet, ref in zip(packets, packet_refs):
        sources = [(sums, chains[c][0] * K + rows) for c, rows in packet[1]]
        encode(packet, sources, ref, scales)
    for copy in keeps:
        copy.wait()


def merge_kernel(chains, arrived, packets, *refs):
    refs = list(refs)
    take = lambda k: [refs.pop(0) for _ in range(k)]
    kept, came = take(chains), take(len(arrived))
    keep_refs, packet_refs = take(chains), take(len(packets))
    sums, scales = refs[:chains], refs[chains]
    for ref, total in zip(kept, sums):
        total[...] = ref[...]
    for packet, ref in zip(arrived, came):
        add_packet(packet, ref, sums, scales)
    for total, ref in zip(sums, keep_refs):
        ref[...] = total[pl.ds(0, ref.shape[0]), :]
    for packet, ref in zip(packets, packet_refs):
        encode(packet, [(sums[c], rows) for c, rows in packet[1]], ref, scales)


def merge(kept, came, arrived, packets):
    last = not packets
    shapes = [
        jax.ShapeDtypeStruct((x.shape[0] if last else x.shape[0] // 2, LANES), x.dtype)
        for x in kept
    ] + [packet_shape(p) for p in packets]
    lines = max(x.shape[0] for x in came)
    outs = pl.pallas_call(
        functools.partial(merge_kernel, len(kept), arrived, packets),
        out_shape=shapes,
        in_specs=[pl.BlockSpec(memory_space=pltpu.VMEM)] * (len(kept) + len(came)),
        out_specs=[pl.BlockSpec(memory_space=pltpu.VMEM)] * len(shapes),
        scratch_shapes=[pltpu.VMEM(x.shape, x.dtype) for x in kept]
        + [pltpu.VMEM((scale_lines(lines) + 16, LANES), jnp.float32)],
        compiler_params=pltpu.CompilerParams(vmem_limit_bytes=16 * 1024 * 1024),
    )(*kept, *came)
    return list(outs[: len(kept)]), list(outs[len(kept) :])


def exchange(blocks, packets, n):
    return [
        lax.ppermute(block, "tm", [(i, i ^ (2 << packet[0])) for i in range(n)])
        for block, packet in zip(blocks, packets)
    ]


def per_device(item_table, item_shard, item_row, cluster_id, lengths):
    n = lax.axis_size("tm")
    users, slab = item_row.shape[1:]
    rows, width = item_table.shape
    total = users * slab
    owned = K // n
    m = bits_for(n) - 1
    cells = users * K // 2
    cell_bits = bits_for(cells)
    row_bits = bits_for(2 * rows)
    dest_shift = cell_bits + row_bits
    most = -(-4 * total // n // RUNS)
    assert users * 2 <= RUNS and most <= LANES - owned
    chains = user_chains(users, m)
    dummy = cells * 2

    other = lax.ppermute(item_table, "tm", [(i, i ^ 1) for i in range(n)])
    buckets = pl.pallas_call(
        functools.partial(
            prepare_kernel, n, owned, rows, dest_shift, row_bits, cell_bits, dummy, chains,
        ),
        out_shape=jax.ShapeDtypeStruct((n, RUNS, LANES), jnp.int32),
        in_specs=[pl.BlockSpec(memory_space=pltpu.SMEM)]
        + [pl.BlockSpec(memory_space=pltpu.VMEM)] * 3,
        out_specs=pl.BlockSpec(memory_space=pltpu.VMEM),
        scratch_shapes=[
            pltpu.VMEM((LANES, LANES), jnp.int32),
            pltpu.VMEM((LANES, LANES), jnp.int32),
            pltpu.VMEM((n * RUNS, LANES), jnp.int32),
        ],
    )(
        lengths,
        item_shard.reshape(total // LANES, LANES),
        item_row.reshape(users, slab),
        cluster_id.reshape(users, slab),
    )
    requests = lax.all_to_all(buckets, "tm", split_axis=0, concat_axis=0, tiled=True)
    counts = jnp.sum(requests[:, :users, LANES - owned :], axis=0).astype(jnp.float32)

    sums_rows = -(-(cells + 1) * 2 // 256) * 256
    lines = [size * (K // 2) for _, size, _ in chains]
    packets = packets_of(chains, 0, lines)
    parts = pl.pallas_call(
        functools.partial(
            add_kernel, n, users * LANES + LANES - owned, cell_bits, chains, packets
        ),
        out_shape=[jax.ShapeDtypeStruct((r, LANES), jnp.float32) for r in lines]
        + [packet_shape(p) for p in packets],
        in_specs=[
            pl.BlockSpec(memory_space=pltpu.VMEM),
            pl.BlockSpec(memory_space=pl.ANY),
            pl.BlockSpec(memory_space=pl.ANY),
        ],
        out_specs=[pl.BlockSpec(memory_space=pl.ANY)] * len(chains)
        + [pl.BlockSpec(memory_space=pltpu.VMEM)] * len(packets),
        scratch_shapes=[
            pltpu.VMEM((rows * 2, width), jnp.bfloat16),
            pltpu.VMEM((rows * 4, LANES), jnp.float32),
            pltpu.VMEM((sums_rows, LANES), jnp.float32),
            pltpu.VMEM((scale_lines(cells * 2) + 16, LANES), jnp.float32),
            pltpu.SMEM((n * RUNS * LANES,), jnp.int32),
            pltpu.SemaphoreType.DMA((n,)),
            pltpu.SemaphoreType.DMA((2 + len(chains),)),
        ],
        compiler_params=pltpu.CompilerParams(vmem_limit_bytes=32 * 1024 * 1024),
    )(requests.reshape(-1), item_table, other)
    kept, sent = list(parts[: len(chains)]), list(parts[len(chains) :])

    for stage in range(m):
        came = exchange(sent, packets, n)
        arrived = packets
        lines = [r // 2 for r in lines]
        packets = packets_of(chains, stage + 1, lines)
        kept, sent = merge(kept, came, arrived, packets)
    done = [x.reshape(size, owned, width) for x, (_, size, _) in zip(kept, chains)]
    return jnp.concatenate(done, axis=0) / jnp.maximum(counts, 1.0)[..., None]


def solution(mesh):
    return jax.shard_map(
        per_device,
        mesh=mesh,
        in_specs=(
            P("tm", None),
            P("tm", ("groups", "users"), None, None),
            P("tm", ("groups", "users"), None),
            P("tm", ("groups", "users"), None),
            P(("groups", "users")),
        ),
        out_specs=P(("groups", "users"), "tm", None),
        check_vma=False,
    )
```

```python
import functools
import math

import jax
import jax.numpy as jnp
from jax import lax
from jax.experimental import pallas as pl
from jax.experimental.pallas import tpu as pltpu
from jax.sharding import PartitionSpec as P

K = 1024
LANES = 128
SUB = 8
RUNS = 16
SLOTS = 16
MODE = 16
NONE = 2**31 - 1
CODE_TOP = 32766.0


def bits_for(count):
    return (count - 1).bit_length()


def user_chains(users, m):
    orders = [(0, 2, 1, 3), (2, 1, 0, 3), (1, 0, 3, 2)] if m == 4 else [tuple(range(m))] * 3
    sizes = [-(-users * 3 // 8), users * 3 // 8]
    sizes.append(users - sum(sizes))
    chains, lo = [], 0
    for size, order in zip(sizes, orders):
        if size:
            chains.append((lo, size, order))
        lo += size
    return chains


def packets_of(chains, stage, rows):
    if stage == len(chains[0][2]):
        return []
    bits = {}
    for c, (_, _, order) in enumerate(chains):
        bits.setdefault(order[stage], []).append(c)
    return [
        (bit, [(c, rows[c]) for c in members], all(rows[c] % LANES == 0 for c in members))
        for bit, members in bits.items()
    ]


def packet_shape(packet):
    _, members, coded = packet
    lines = sum(rows for _, rows in members)
    if not coded:
        return jax.ShapeDtypeStruct((lines, LANES), jnp.float32)
    return jax.ShapeDtypeStruct((lines + scale_lines(lines), LANES), jnp.int16)


def scale_lines(lines):
    return -(-lines // LANES // 16) * 16


def scale_of(exponent):
    return jnp.exp(exponent * (math.log(2.0) / 64.0))


def encode(packet, sources, out_ref, scales):
    done = 0
    for (_, rows), (ref, start) in zip(packet[1], sources):
        if not packet[2]:
            out_ref[pl.ds(done, rows), :] = ref[pl.ds(start, rows), :]
            done += rows
            continue

        def block(i, _, ref=ref, start=start, done=done):
            x = ref[pl.ds(start + i * LANES, LANES), :]
            top = jnp.maximum(jnp.max(jnp.abs(x), axis=0, keepdims=True), 1e-33)
            exponent = jnp.ceil(jnp.log(top) * (64.0 / math.log(2.0)))
            code = jnp.round(x * (CODE_TOP / scale_of(exponent)))
            code = code.astype(jnp.int32).astype(jnp.int16)
            out_ref[pl.ds(pl.multiple_of(done + i * LANES, LANES), LANES), :] = code
            scales[pl.ds(done // LANES + i, 1), :] = exponent
            return 0

        lax.fori_loop(0, rows // LANES, block, 0)
        done += rows
    if packet[2]:
        out_ref[pl.ds(done, scale_lines(done)), :] = (
            scales[pl.ds(0, scale_lines(done)), :].astype(jnp.int32).astype(jnp.int16)
        )


def add_packet(packet, ref, sums, scales):
    if packet[2]:
        lines = sum(rows for _, rows in packet[1])
        scales[pl.ds(0, scale_lines(lines)), :] = ref[
            pl.ds(lines, scale_lines(lines)), :
        ].astype(jnp.float32)
    done = 0
    for c, rows in packet[1]:
        if not packet[2]:
            sums[c][...] = sums[c][...] + ref[pl.ds(done, rows), :]
            done += rows
            continue

        def block(i, _, c=c, done=done):
            exponent = scales[pl.ds(done // LANES + i, 1), :]
            code = ref[pl.ds(pl.multiple_of(done + i * LANES, LANES), LANES), :]
            at = pl.ds(pl.multiple_of(i * LANES, LANES), LANES)
            value = code.astype(jnp.float32) * (scale_of(exponent) * (1.0 / CODE_TOP))
            sums[c][at, :] = sums[c][at, :] + value
            return 0

        lax.fori_loop(0, rows // LANES, block, 0)
        done += rows


def sort_tiles(tiles):
    count = len(tiles)
    tile_bits = bits_for(count)
    sub = lax.broadcasted_iota(jnp.int32, (SUB, LANES), 0)
    lane = lax.broadcasted_iota(jnp.int32, (SUB, LANES), 1)
    total_bits = tile_bits + 3 + 7

    def bit_mask(bit):
        if bit < tile_bits + 3:
            return ((sub >> (bit - tile_bits)) & 1) == 1
        return ((lane >> (bit - tile_bits - 3)) & 1) == 1

    masks = {b: bit_mask(b) for b in range(tile_bits, total_bits)}
    flips = {b: jnp.where(masks[b], -1, 0) for b in masks}

    def flip(t, phase):
        if phase >= total_bits:
            return 0
        if phase < tile_bits:
            return -1 if (t >> phase) & 1 else 0
        return flips[phase]

    for phase in range(1, total_bits + 1):
        changed = []
        for t in range(count):
            old = flip(t, phase - 1) if phase > 1 else 0
            new = flip(t, phase)
            if isinstance(old, int) and isinstance(new, int):
                turn = old ^ new
                changed.append(tiles[t] if turn == 0 else ~tiles[t])
            else:
                changed.append(tiles[t] ^ (old ^ new))
        tiles = changed
        for bit in reversed(range(phase)):
            if bit < tile_bits:
                step = 1 << bit
                tiles = list(tiles)
                for t in range(count):
                    if not t & step:
                        a, b = tiles[t], tiles[t | step]
                        tiles[t], tiles[t | step] = jnp.minimum(a, b), jnp.maximum(a, b)
                continue
            if bit < tile_bits + 3:
                axis, step, size = 0, 1 << (bit - tile_bits), SUB
            else:
                axis, step, size = 1, 1 << (bit - tile_bits - 3), LANES
            upper = masks[bit]
            moved = []
            for x in tiles:
                down = pltpu.roll(x, step, axis=axis)
                if 2 * step == size:
                    other = down
                else:
                    other = jnp.where(upper, down, pltpu.roll(x, size - step, axis=axis))
                moved.append(
                    jnp.where(upper, jnp.maximum(x, other), jnp.minimum(x, other))
                )
            tiles = moved
    return tiles


def prepare_kernel(
    n, owned, table_rows, dest_shift, row_bits, cell_bits, dummy, chains,
    lengths_ref, shard_ref, row_ref, cluster_ref, out_ref, order, straight, runs,
):
    users, slab = row_ref.shape
    sub = lax.broadcasted_iota(jnp.int32, (SUB, LANES), 0)
    lane = lax.broadcasted_iota(jnp.int32, (SUB, LANES), 1)
    me = lax.axis_index("tm")
    length = jnp.zeros((SUB, LANES), jnp.int32)
    live_total = jnp.int32(0)
    for u in range(users):
        length = jnp.where(sub == u, lengths_ref[u], length)
        live_total += jnp.clip(lengths_ref[u] - me * slab, 0, slab)
    length = length - me * slab

    base = jnp.zeros((SUB, LANES), jnp.int32)
    in_chain = jnp.zeros((SUB, LANES), jnp.int32)
    chain_size = jnp.zeros((SUB, LANES), jnp.int32)
    chain_at = []
    for lo, size, _ in chains:
        inside = (sub >= lo) & (sub < lo + size)
        base = jnp.where(inside, lo * (K // 2), base)
        in_chain = jnp.where(inside, sub - lo, in_chain)
        chain_size = jnp.where(inside, size, chain_size)
        chain_at.append(inside)

    owner_shift = bits_for(owned)
    tiles = []
    spare = LANES - owned
    hot_owner = [[] for _ in range(users)]
    hot_slot = [[] for _ in range(users)]
    owner_iota = lax.broadcasted_iota(jnp.int32, (n, LANES), 0)
    slot_iota = lax.broadcasted_iota(jnp.int32, (LANES, LANES), 0)
    for j in range(slab // LANES):
        at = pl.ds(j * LANES, LANES)
        row, cluster = row_ref[:, at], cluster_ref[:, at]
        shard = shard_ref[pl.ds(j, users, stride=slab // LANES), :]
        owner = lax.shift_right_logical(cluster, owner_shift)
        low = cluster & (owned - 1)
        live = lane + j * LANES < length
        dest = (shard & ~1) | (owner & 1)
        away = lax.shift_right_logical(owner ^ dest, 1)
        spread = jnp.zeros((SUB, LANES), jnp.int32)
        by_order = {}
        for (_, _, bits), inside in zip(chains, chain_at):
            if bits not in by_order:
                turned = jnp.zeros((SUB, LANES), jnp.int32)
                for bit in bits:
                    turned = turned * 2 + ((away >> bit) & 1)
                by_order[bits] = turned
            spread = jnp.where(inside, by_order[bits], spread)
        cell = base + ((spread * chain_size + in_chain) << owner_shift) + low
        there = ((shard ^ owner) & 1) * table_rows + row
        key = (dest << dest_shift) | (cell << row_bits) | there
        tiles.append(jnp.where(live, key, NONE))
        live_owner = jnp.where(live, owner, -1)
        for u in range(users):
            hot_owner[u].append((owner_iota == live_owner[u : u + 1, :]).astype(jnp.bfloat16))
            hot_slot[u].append((slot_iota == low[u : u + 1, :] + spare).astype(jnp.bfloat16))

    for u in range(users):
        counts = jnp.zeros((n, LANES), jnp.float32)
        for a, b in zip(hot_owner[u], hot_slot[u]):
            counts += lax.dot_general(
                a, b, (((1,), (1,)), ((), ())), preferred_element_type=jnp.float32
            )
        counts = counts.astype(jnp.int32)
        for d in range(n):
            out_ref[d, pl.ds(u, 1), :] = counts[d : d + 1, :]

    ends = []
    for d in range(n - 1):
        below = jnp.zeros((SUB, LANES), jnp.float32)
        for x in tiles:
            below += (x < ((d + 1) << dest_shift)).astype(jnp.float32)
        ends.append(jnp.sum(below).astype(jnp.int32))
    ends.append(live_total)

    empty = jnp.full((SUB, LANES), NONE, jnp.int32)
    tiles = sort_tiles(tiles + [empty] * ((1 << bits_for(len(tiles))) - len(tiles)))
    count = len(tiles)
    for t, x in enumerate(tiles):
        order[pl.ds(t * SUB, SUB), :] = x
    lines = [order[pl.ds(s, count, stride=SUB), :] for s in range(SUB)]
    straight[...] = jnp.concatenate(lines, axis=0).T

    at = (RUNS, LANES)
    run = lax.broadcasted_iota(jnp.int32, at, 0)
    lane = lax.broadcasted_iota(jnp.int32, at, 1)
    one_line = lax.broadcasted_iota(jnp.int32, (1, LANES), 1)
    start = jnp.int32(0)
    for d in range(n):
        count = ends[d] - start
        steps = lax.shift_right_logical(count + RUNS - 1, bits_for(RUNS))
        for j in range(RUNS):
            begin = start + j * steps
            off = begin & (LANES - 1)
            two = straight[pl.ds(lax.shift_right_logical(begin, bits_for(LANES)), 2), :]
            two = pltpu.roll(two, (LANES - off) & (LANES - 1), axis=1)
            runs[pl.ds(d * RUNS + j, 1), :] = jnp.where(one_line < LANES - off, two[:1], two[1:])
        mine = runs[pl.ds(d * RUNS, RUNS), :]
        valid = (lane < steps) & (run * steps + lane < count)
        there = mine & (2 * table_rows - 1)
        cell = lax.shift_right_logical(mine, row_bits) & ((1 << cell_bits) - 1)
        code = jnp.where(valid, (there << (cell_bits + 3)) | (cell << 1), dummy)
        cell = jnp.where(valid, cell, -1)
        following = pltpu.roll(cell, RUNS - 1, axis=0)
        same = (cell >= 0) & (cell == following) & (run < RUNS - 1)
        twice = jnp.max(jnp.where(same, 1.0, 0.0)).astype(jnp.int32)
        head = jnp.full((RUNS, LANES), steps | (twice << MODE), jnp.int32)
        beside = jnp.where(run < users, out_ref[d], head)
        out_ref[d] = jnp.where(lane < spare, code, beside)
        start = ends[d]


def add_kernel(n, head_at, cell_bits, chains, packets, request_ref, own_ref, other_ref, *rest):
    keep_refs = rest[: len(chains)]
    packet_refs = rest[len(chains) : len(chains) + len(packets)]
    narrow, table, sums, scales, lists, cells, rows_at, list_sems, sems = rest[
        len(chains) + len(packets) :
    ]
    stride = RUNS * LANES

    low = (4 << cell_bits) - 1

    def reads(s):
        at = pl.ds(pl.multiple_of(s * stride, stride), stride)
        slot = lax.rem(s, SLOTS)
        to = pl.ds(pl.multiple_of(slot * stride, stride), stride)
        return [
            pltpu.make_async_copy(lists.at[part, at], ref.at[to], list_sems.at[part, slot])
            for part, ref in enumerate((cells, rows_at))
        ]

    def take_apart(s, _):
        at = pl.ds(pl.multiple_of(s * stride, stride), stride)
        code = request_ref[at]
        lists[0, at] = code & low
        lists[1, at] = lax.shift_right_logical(code, cell_bits + 2)

        @pl.when(s < SLOTS)
        def _():
            for copy in reads(s):
                copy.start()

        return 0

    rows = own_ref.shape[0]
    tables = [
        pltpu.make_async_copy(ref, narrow.at[pl.ds(part * rows, rows), :], sems.at[part])
        for part, ref in enumerate((own_ref, other_ref))
    ]
    for copy in tables:
        copy.start()
    lax.fori_loop(0, n, take_apart, 0)

    def clear(i, _):
        sums[pl.ds(i * 256, 256), :] = jnp.zeros((256, LANES), jnp.float32)
        return 0

    lax.fori_loop(0, sums.shape[0] // 256, clear, 0)

    for copy in tables:
        copy.wait()

    def widen(i, _):
        x = narrow[pl.ds(i * LANES, LANES), :].astype(jnp.float32)
        table[pl.ds(i * 2 * LANES, LANES, stride=2), :] = x[:, :LANES]
        table[pl.ds(i * 2 * LANES + 1, LANES, stride=2), :] = x[:, LANES:]
        return 0

    lax.fori_loop(0, 2 * rows // LANES, widen, 0)

    def two_lines(at):
        return pl.ds(pl.multiple_of(at, 2), 2)

    def source(s, _):
        for copy in reads(s):
            copy.wait()
        begin = lax.rem(s, SLOTS) * stride
        head = cells[begin + head_at] | rows_at[begin + head_at] << (cell_bits + 2)
        steps = head & ((1 << MODE) - 1)

        @pl.when(head < (1 << MODE))
        def _():
            def step(i, _):
                new = []
                for k in range(RUNS):
                    cell = two_lines(cells[begin + i + k * LANES])
                    row = two_lines(rows_at[begin + i + k * LANES])
                    new.append((cell, sums[cell, :] + table[row, :]))
                for cell, value in new:
                    sums[cell, :] = value
                return 0

            lax.fori_loop(0, steps, step, 0)

        @pl.when(head >= (1 << MODE))
        def _():
            def step(i, _):
                for k in range(RUNS):
                    cell = two_lines(cells[begin + i + k * LANES])
                    row = two_lines(rows_at[begin + i + k * LANES])
                    sums[cell, :] = sums[cell, :] + table[row, :]
                return 0

            lax.fori_loop(0, steps, step, 0)

        @pl.when(s + SLOTS < n)
        def _():
            for copy in reads(s + SLOTS):
                copy.start()

        return 0

    lax.fori_loop(0, n, source, 0)
    keeps = [
        pltpu.make_async_copy(
            sums.at[pl.ds(lo * K, size * (K // 2)), :], ref, sems.at[2 + c]
        )
        for c, ((lo, size, _), ref) in enumerate(zip(chains, keep_refs))
    ]
    for copy in keeps:
        copy.start()
    for packet, ref in zip(packets, packet_refs):
        sources = [(sums, chains[c][0] * K + rows) for c, rows in packet[1]]
        encode(packet, sources, ref, scales)
    for copy in keeps:
        copy.wait()


def merge_kernel(chains, arrived, packets, *refs):
    refs = list(refs)
    take = lambda k: [refs.pop(0) for _ in range(k)]
    kept, came = take(chains), take(len(arrived))
    keep_refs, packet_refs = take(chains), take(len(packets))
    sums, scales = refs[:chains], refs[chains]
    for ref, total in zip(kept, sums):
        total[...] = ref[...]
    for packet, ref in zip(arrived, came):
        add_packet(packet, ref, sums, scales)
    for total, ref in zip(sums, keep_refs):
        ref[...] = total[pl.ds(0, ref.shape[0]), :]
    for packet, ref in zip(packets, packet_refs):
        encode(packet, [(sums[c], rows) for c, rows in packet[1]], ref, scales)


def merge(kept, came, arrived, packets):
    last = not packets
    shapes = [
        jax.ShapeDtypeStruct((x.shape[0] if last else x.shape[0] // 2, LANES), x.dtype)
        for x in kept
    ] + [packet_shape(p) for p in packets]
    lines = max(x.shape[0] for x in came)
    outs = pl.pallas_call(
        functools.partial(merge_kernel, len(kept), arrived, packets),
        out_shape=shapes,
        in_specs=[pl.BlockSpec(memory_space=pltpu.VMEM)] * (len(kept) + len(came)),
        out_specs=[pl.BlockSpec(memory_space=pltpu.VMEM)] * len(shapes),
        scratch_shapes=[pltpu.VMEM(x.shape, x.dtype) for x in kept]
        + [pltpu.VMEM((scale_lines(lines) + 16, LANES), jnp.float32)],
        compiler_params=pltpu.CompilerParams(vmem_limit_bytes=16 * 1024 * 1024),
    )(*kept, *came)
    return list(outs[: len(kept)]), list(outs[len(kept) :])


def exchange(blocks, packets, n):
    return [
        lax.ppermute(block, "tm", [(i, i ^ (2 << packet[0])) for i in range(n)])
        for block, packet in zip(blocks, packets)
    ]


def per_device(item_table, item_shard, item_row, cluster_id, lengths):
    n = lax.axis_size("tm")
    users, slab = item_row.shape[1:]
    rows, width = item_table.shape
    total = users * slab
    owned = K // n
    m = bits_for(n) - 1
    cells = users * K // 2
    cell_bits = bits_for(cells)
    row_bits = bits_for(2 * rows)
    dest_shift = cell_bits + row_bits
    most = -(-4 * total // n // RUNS)
    assert users * 2 <= RUNS and most <= LANES - owned
    chains = user_chains(users, m)
    dummy = cells * 2

    other = lax.ppermute(item_table, "tm", [(i, i ^ 1) for i in range(n)])
    buckets = pl.pallas_call(
        functools.partial(
            prepare_kernel, n, owned, rows, dest_shift, row_bits, cell_bits, dummy, chains,
        ),
        out_shape=jax.ShapeDtypeStruct((n, RUNS, LANES), jnp.int32),
        in_specs=[pl.BlockSpec(memory_space=pltpu.SMEM)]
        + [pl.BlockSpec(memory_space=pltpu.VMEM)] * 3,
        out_specs=pl.BlockSpec(memory_space=pltpu.VMEM),
        scratch_shapes=[
            pltpu.VMEM((LANES, LANES), jnp.int32),
            pltpu.VMEM((LANES, LANES), jnp.int32),
            pltpu.VMEM((n * RUNS, LANES), jnp.int32),
        ],
    )(
        lengths,
        item_shard.reshape(total // LANES, LANES),
        item_row.reshape(users, slab),
        cluster_id.reshape(users, slab),
    )
    requests = lax.all_to_all(buckets, "tm", split_axis=0, concat_axis=0, tiled=True)
    counts = jnp.sum(requests[:, :users, LANES - owned :], axis=0).astype(jnp.float32)

    sums_rows = -(-(cells + 1) * 2 // 256) * 256
    lines = [size * (K // 2) for _, size, _ in chains]
    packets = packets_of(chains, 0, lines)
    parts = pl.pallas_call(
        functools.partial(
            add_kernel, n, users * LANES + LANES - owned, cell_bits, chains, packets
        ),
        out_shape=[jax.ShapeDtypeStruct((r, LANES), jnp.float32) for r in lines]
        + [packet_shape(p) for p in packets],
        in_specs=[
            pl.BlockSpec(memory_space=pltpu.VMEM),
            pl.BlockSpec(memory_space=pl.ANY),
            pl.BlockSpec(memory_space=pl.ANY),
        ],
        out_specs=[pl.BlockSpec(memory_space=pl.ANY)] * len(chains)
        + [pl.BlockSpec(memory_space=pltpu.VMEM)] * len(packets),
        scratch_shapes=[
            pltpu.VMEM((rows * 2, width), jnp.bfloat16),
            pltpu.VMEM((rows * 4, LANES), jnp.float32),
            pltpu.VMEM((sums_rows, LANES), jnp.float32),
            pltpu.VMEM((scale_lines(cells * 2) + 16, LANES), jnp.float32),
            pltpu.VMEM((2, n * RUNS * LANES), jnp.int32),
            pltpu.SMEM((SLOTS * RUNS * LANES,), jnp.int32),
            pltpu.SMEM((SLOTS * RUNS * LANES,), jnp.int32),
            pltpu.SemaphoreType.DMA((2, SLOTS)),
            pltpu.SemaphoreType.DMA((2 + len(chains),)),
        ],
        compiler_params=pltpu.CompilerParams(vmem_limit_bytes=32 * 1024 * 1024),
    )(requests.reshape(-1), item_table, other)
    kept, sent = list(parts[: len(chains)]), list(parts[len(chains) :])

    for stage in range(m):
        came = exchange(sent, packets, n)
        arrived = packets
        lines = [r // 2 for r in lines]
        packets = packets_of(chains, stage + 1, lines)
        kept, sent = merge(kept, came, arrived, packets)
    done = [x.reshape(size, owned, width) for x, (_, size, _) in zip(kept, chains)]
    return jnp.concatenate(done, axis=0) / jnp.maximum(counts, 1.0)[..., None]


def solution(mesh):
    return jax.shard_map(
        per_device,
        mesh=mesh,
        in_specs=(
            P("tm", None),
            P("tm", ("groups", "users"), None, None),
            P("tm", ("groups", "users"), None),
            P("tm", ("groups", "users"), None),
            P(("groups", "users")),
        ),
        out_specs=P(("groups", "users"), "tm", None),
        check_vma=False,
    )
```

```python
import functools
import math

import jax
import jax.numpy as jnp
from jax import lax
from jax.experimental import pallas as pl
from jax.experimental.pallas import tpu as pltpu
from jax.sharding import PartitionSpec as P

K = 1024
LANES = 128
SUB = 8
RUNS = 16
SLOTS = 16
MODE = 16
NONE = 2**31 - 1
CODE_TOP = 32766.0
TALL = 64


def bits_for(count):
    return (count - 1).bit_length()


def user_chains(users, m):
    orders = [(0, 2, 1, 3), (2, 1, 0, 3), (1, 0, 3, 2)] if m == 4 else [tuple(range(m))] * 3
    sizes = [-(-users * 3 // 8), users * 3 // 8]
    sizes.append(users - sum(sizes))
    chains, lo = [], 0
    for size, order in zip(sizes, orders):
        if size:
            chains.append((lo, size, order))
        lo += size
    return chains


def packets_of(chains, stage, rows):
    if stage == len(chains[0][2]):
        return []
    bits = {}
    for c, (_, _, order) in enumerate(chains):
        bits.setdefault(order[stage], []).append(c)
    return [
        (bit, [(c, rows[c]) for c in members], all(rows[c] % TALL == 0 for c in members))
        for bit, members in bits.items()
    ]


def packet_shape(packet):
    _, members, coded = packet
    lines = sum(rows for _, rows in members)
    if not coded:
        return jax.ShapeDtypeStruct((lines, LANES), jnp.float32)
    return jax.ShapeDtypeStruct((lines + scale_lines(lines), LANES), jnp.int16)


def scale_lines(lines):
    return -(-lines // TALL // 16) * 16


def scale_of(exponent):
    return jnp.exp(exponent * (math.log(2.0) / 64.0))


def encode(packet, sources, out_ref, scales):
    done = 0
    for (_, rows), (ref, start) in zip(packet[1], sources):
        if not packet[2]:
            out_ref[pl.ds(done, rows), :] = ref[pl.ds(start, rows), :]
            done += rows
            continue

        def block(i, _, ref=ref, start=start, done=done):
            x = ref[pl.ds(start + i * TALL, TALL), :]
            top = jnp.maximum(jnp.max(jnp.abs(x), axis=0, keepdims=True), 1e-33)
            exponent = jnp.ceil(jnp.log(top) * (64.0 / math.log(2.0)))
            code = jnp.round(x * (CODE_TOP / scale_of(exponent)))
            code = code.astype(jnp.int32).astype(jnp.int16)
            out_ref[pl.ds(pl.multiple_of(done + i * TALL, TALL), TALL), :] = code
            scales[pl.ds(done // TALL + i, 1), :] = exponent
            return 0

        lax.fori_loop(0, rows // TALL, block, 0)
        done += rows
    if packet[2]:
        out_ref[pl.ds(done, scale_lines(done)), :] = (
            scales[pl.ds(0, scale_lines(done)), :].astype(jnp.int32).astype(jnp.int16)
        )


def add_packet(packet, ref, sums, scales):
    if packet[2]:
        lines = sum(rows for _, rows in packet[1])
        scales[pl.ds(0, scale_lines(lines)), :] = ref[
            pl.ds(lines, scale_lines(lines)), :
        ].astype(jnp.float32)
    done = 0
    for c, rows in packet[1]:
        if not packet[2]:
            sums[c][...] = sums[c][...] + ref[pl.ds(done, rows), :]
            done += rows
            continue

        def block(i, _, c=c, done=done):
            exponent = scales[pl.ds(done // TALL + i, 1), :]
            code = ref[pl.ds(pl.multiple_of(done + i * TALL, TALL), TALL), :]
            at = pl.ds(pl.multiple_of(i * TALL, TALL), TALL)
            value = code.astype(jnp.float32) * (scale_of(exponent) * (1.0 / CODE_TOP))
            sums[c][at, :] = sums[c][at, :] + value
            return 0

        lax.fori_loop(0, rows // TALL, block, 0)
        done += rows


def sort_tiles(tiles):
    count = len(tiles)
    tile_bits = bits_for(count)
    sub = lax.broadcasted_iota(jnp.int32, (SUB, LANES), 0)
    lane = lax.broadcasted_iota(jnp.int32, (SUB, LANES), 1)
    total_bits = tile_bits + 3 + 7

    def bit_mask(bit):
        if bit < tile_bits + 3:
            return ((sub >> (bit - tile_bits)) & 1) == 1
        return ((lane >> (bit - tile_bits - 3)) & 1) == 1

    masks = {b: bit_mask(b) for b in range(tile_bits, total_bits)}
    flips = {b: jnp.where(masks[b], -1, 0) for b in masks}

    def flip(t, phase):
        if phase >= total_bits:
            return 0
        if phase < tile_bits:
            return -1 if (t >> phase) & 1 else 0
        return flips[phase]

    for phase in range(1, total_bits + 1):
        changed = []
        for t in range(count):
            old = flip(t, phase - 1) if phase > 1 else 0
            new = flip(t, phase)
            if isinstance(old, int) and isinstance(new, int):
                turn = old ^ new
                changed.append(tiles[t] if turn == 0 else ~tiles[t])
            else:
                changed.append(tiles[t] ^ (old ^ new))
        tiles = changed
        for bit in reversed(range(phase)):
            if bit < tile_bits:
                step = 1 << bit
                tiles = list(tiles)
                for t in range(count):
                    if not t & step:
                        a, b = tiles[t], tiles[t | step]
                        tiles[t], tiles[t | step] = jnp.minimum(a, b), jnp.maximum(a, b)
                continue
            if bit < tile_bits + 3:
                axis, step, size = 0, 1 << (bit - tile_bits), SUB
            else:
                axis, step, size = 1, 1 << (bit - tile_bits - 3), LANES
            upper = masks[bit]
            moved = []
            for x in tiles:
                down = pltpu.roll(x, step, axis=axis)
                if 2 * step == size:
                    other = down
                else:
                    other = jnp.where(upper, down, pltpu.roll(x, size - step, axis=axis))
                moved.append(
                    jnp.where(upper, jnp.maximum(x, other), jnp.minimum(x, other))
                )
            tiles = moved
    return tiles


def prepare_kernel(
    n, owned, table_rows, dest_shift, row_bits, cell_bits, dummy, chains,
    lengths_ref, shard_ref, row_ref, cluster_ref, out_ref, order, straight, runs,
):
    users, slab = row_ref.shape
    sub = lax.broadcasted_iota(jnp.int32, (SUB, LANES), 0)
    lane = lax.broadcasted_iota(jnp.int32, (SUB, LANES), 1)
    me = lax.axis_index("tm")
    length = jnp.zeros((SUB, LANES), jnp.int32)
    live_total = jnp.int32(0)
    for u in range(users):
        length = jnp.where(sub == u, lengths_ref[u], length)
        live_total += jnp.clip(lengths_ref[u] - me * slab, 0, slab)
    length = length - me * slab

    base = jnp.zeros((SUB, LANES), jnp.int32)
    in_chain = jnp.zeros((SUB, LANES), jnp.int32)
    chain_size = jnp.zeros((SUB, LANES), jnp.int32)
    chain_at = []
    for lo, size, _ in chains:
        inside = (sub >= lo) & (sub < lo + size)
        base = jnp.where(inside, lo * (K // 2), base)
        in_chain = jnp.where(inside, sub - lo, in_chain)
        chain_size = jnp.where(inside, size, chain_size)
        chain_at.append(inside)

    owner_shift = bits_for(owned)
    tiles = []
    spare = LANES - owned
    hot_owner = [[] for _ in range(users)]
    hot_slot = [[] for _ in range(users)]
    owner_iota = lax.broadcasted_iota(jnp.int32, (n, LANES), 0)
    slot_iota = lax.broadcasted_iota(jnp.int32, (LANES, LANES), 0)
    for j in range(slab // LANES):
        at = pl.ds(j * LANES, LANES)
        row, cluster = row_ref[:, at], cluster_ref[:, at]
        shard = shard_ref[pl.ds(j, users, stride=slab // LANES), :]
        owner = lax.shift_right_logical(cluster, owner_shift)
        low = cluster & (owned - 1)
        live = lane + j * LANES < length
        dest = (shard & ~1) | (owner & 1)
        away = lax.shift_right_logical(owner ^ dest, 1)
        spread = jnp.zeros((SUB, LANES), jnp.int32)
        by_order = {}
        for (_, _, bits), inside in zip(chains, chain_at):
            if bits not in by_order:
                turned = jnp.zeros((SUB, LANES), jnp.int32)
                for bit in bits:
                    turned = turned * 2 + ((away >> bit) & 1)
                by_order[bits] = turned
            spread = jnp.where(inside, by_order[bits], spread)
        cell = base + ((spread * chain_size + in_chain) << owner_shift) + low
        there = ((shard ^ owner) & 1) * table_rows + row
        key = (dest << dest_shift) | (cell << row_bits) | there
        tiles.append(jnp.where(live, key, NONE))
        live_owner = jnp.where(live, owner, -1)
        for u in range(users):
            hot_owner[u].append((owner_iota == live_owner[u : u + 1, :]).astype(jnp.bfloat16))
            hot_slot[u].append((slot_iota == low[u : u + 1, :] + spare).astype(jnp.bfloat16))

    for u in range(users):
        counts = jnp.zeros((n, LANES), jnp.float32)
        for a, b in zip(hot_owner[u], hot_slot[u]):
            counts += lax.dot_general(
                a, b, (((1,), (1,)), ((), ())), preferred_element_type=jnp.float32
            )
        counts = counts.astype(jnp.int32)
        for d in range(n):
            out_ref[d, pl.ds(u, 1), :] = counts[d : d + 1, :]

    ends = []
    for d in range(n - 1):
        below = jnp.zeros((SUB, LANES), jnp.float32)
        for x in tiles:
            below += (x < ((d + 1) << dest_shift)).astype(jnp.float32)
        ends.append(jnp.sum(below).astype(jnp.int32))
    ends.append(live_total)

    empty = jnp.full((SUB, LANES), NONE, jnp.int32)
    tiles = sort_tiles(tiles + [empty] * ((1 << bits_for(len(tiles))) - len(tiles)))
    count = len(tiles)
    for t, x in enumerate(tiles):
        order[pl.ds(t * SUB, SUB), :] = x
    lines = [order[pl.ds(s, count, stride=SUB), :] for s in range(SUB)]
    straight[...] = jnp.concatenate(lines, axis=0).T

    at = (RUNS, LANES)
    run = lax.broadcasted_iota(jnp.int32, at, 0)
    lane = lax.broadcasted_iota(jnp.int32, at, 1)
    one_line = lax.broadcasted_iota(jnp.int32, (1, LANES), 1)
    start = jnp.int32(0)
    for d in range(n):
        count = ends[d] - start
        steps = lax.shift_right_logical(count + RUNS - 1, bits_for(RUNS))
        for j in range(RUNS):
            begin = start + j * steps
            off = begin & (LANES - 1)
            two = straight[pl.ds(lax.shift_right_logical(begin, bits_for(LANES)), 2), :]
            two = pltpu.roll(two, (LANES - off) & (LANES - 1), axis=1)
            runs[pl.ds(d * RUNS + j, 1), :] = jnp.where(one_line < LANES - off, two[:1], two[1:])
        mine = runs[pl.ds(d * RUNS, RUNS), :]
        valid = (lane < steps) & (run * steps + lane < count)
        there = mine & (2 * table_rows - 1)
        cell = lax.shift_right_logical(mine, row_bits) & ((1 << cell_bits) - 1)
        code = jnp.where(valid, (there << (cell_bits + 3)) | (cell << 1), dummy)
        cell = jnp.where(valid, cell, -1)
        following = pltpu.roll(cell, RUNS - 1, axis=0)
        same = (cell >= 0) & (cell == following) & (run < RUNS - 1)
        twice = jnp.max(jnp.where(same, 1.0, 0.0)).astype(jnp.int32)
        head = jnp.full((RUNS, LANES), steps | (twice << MODE), jnp.int32)
        beside = jnp.where(run < users, out_ref[d], head)
        out_ref[d] = jnp.where(lane < spare, code, beside)
        start = ends[d]


def add_kernel(n, head_at, cell_bits, chains, packets, request_ref, own_ref, other_ref, *rest):
    keep_refs = rest[: len(chains)]
    packet_refs = rest[len(chains) : len(chains) + len(packets)]
    narrow, table, sums, scales, lists, cells, rows_at, list_sems, sems = rest[
        len(chains) + len(packets) :
    ]
    stride = RUNS * LANES

    low = (4 << cell_bits) - 1

    def reads(s):
        at = pl.ds(pl.multiple_of(s * stride, stride), stride)
        slot = lax.rem(s, SLOTS)
        to = pl.ds(pl.multiple_of(slot * stride, stride), stride)
        return [
            pltpu.make_async_copy(lists.at[part, at], ref.at[to], list_sems.at[part, slot])
            for part, ref in enumerate((cells, rows_at))
        ]

    def take_apart(s, _):
        at = pl.ds(pl.multiple_of(s * stride, stride), stride)
        code = request_ref[at]
        lists[0, at] = code & low
        lists[1, at] = lax.shift_right_logical(code, cell_bits + 2)

        @pl.when(s < SLOTS)
        def _():
            for copy in reads(s):
                copy.start()

        return 0

    rows = own_ref.shape[0]
    tables = [
        pltpu.make_async_copy(ref, narrow.at[pl.ds(part * rows, rows), :], sems.at[part])
        for part, ref in enumerate((own_ref, other_ref))
    ]
    for copy in tables:
        copy.start()
    lax.fori_loop(0, n, take_apart, 0)

    def clear(i, _):
        sums[pl.ds(i * 256, 256), :] = jnp.zeros((256, LANES), jnp.float32)
        return 0

    lax.fori_loop(0, sums.shape[0] // 256, clear, 0)

    for copy in tables:
        copy.wait()

    def widen(i, _):
        x = narrow[pl.ds(i * LANES, LANES), :].astype(jnp.float32)
        table[pl.ds(i * 2 * LANES, LANES, stride=2), :] = x[:, :LANES]
        table[pl.ds(i * 2 * LANES + 1, LANES, stride=2), :] = x[:, LANES:]
        return 0

    lax.fori_loop(0, 2 * rows // LANES, widen, 0)

    def two_lines(at):
        return pl.ds(pl.multiple_of(at, 2), 2)

    def source(s, _):
        for copy in reads(s):
            copy.wait()
        begin = lax.rem(s, SLOTS) * stride
        head = cells[begin + head_at] | rows_at[begin + head_at] << (cell_bits + 2)
        steps = head & ((1 << MODE) - 1)

        @pl.when(head < (1 << MODE))
        def _():
            def step(at):
                new = []
                for k in range(RUNS):
                    cell = two_lines(cells[at + k * LANES])
                    row = two_lines(rows_at[at + k * LANES])
                    new.append((cell, sums[cell, :] + table[row, :]))
                for cell, value in new:
                    sums[cell, :] = value

            def two_steps(i, _):
                step(begin + 2 * i)
                step(begin + 2 * i + 1)
                return 0

            lax.fori_loop(0, lax.shift_right_logical(steps, 1), two_steps, 0)

            @pl.when((steps & 1) == 1)
            def _():
                step(begin + steps - 1)

        @pl.when(head >= (1 << MODE))
        def _():
            def step(i, _):
                for k in range(RUNS):
                    cell = two_lines(cells[begin + i + k * LANES])
                    row = two_lines(rows_at[begin + i + k * LANES])
                    sums[cell, :] = sums[cell, :] + table[row, :]
                return 0

            lax.fori_loop(0, steps, step, 0)

        @pl.when(s + SLOTS < n)
        def _():
            for copy in reads(s + SLOTS):
                copy.start()

        return 0

    lax.fori_loop(0, n, source, 0)
    keeps = [
        pltpu.make_async_copy(
            sums.at[pl.ds(lo * K, size * (K // 2)), :], ref, sems.at[2 + c]
        )
        for c, ((lo, size, _), ref) in enumerate(zip(chains, keep_refs))
    ]
    for copy in keeps:
        copy.start()
    for packet, ref in zip(packets, packet_refs):
        sources = [(sums, chains[c][0] * K + rows) for c, rows in packet[1]]
        encode(packet, sources, ref, scales)
    for copy in keeps:
        copy.wait()


def merge_kernel(chains, arrived, packets, *refs):
    refs = list(refs)
    take = lambda k: [refs.pop(0) for _ in range(k)]
    kept, came = take(chains), take(len(arrived))
    keep_refs, packet_refs = take(chains), take(len(packets))
    sums, scales = refs[:chains], refs[chains]
    for ref, total in zip(kept, sums):
        total[...] = ref[...]
    for packet, ref in zip(arrived, came):
        add_packet(packet, ref, sums, scales)
    for total, ref in zip(sums, keep_refs):
        ref[...] = total[pl.ds(0, ref.shape[0]), :]
    for packet, ref in zip(packets, packet_refs):
        encode(packet, [(sums[c], rows) for c, rows in packet[1]], ref, scales)


def merge(kept, came, arrived, packets):
    last = not packets
    shapes = [
        jax.ShapeDtypeStruct((x.shape[0] if last else x.shape[0] // 2, LANES), x.dtype)
        for x in kept
    ] + [packet_shape(p) for p in packets]
    lines = max(x.shape[0] for x in came)
    outs = pl.pallas_call(
        functools.partial(merge_kernel, len(kept), arrived, packets),
        out_shape=shapes,
        in_specs=[pl.BlockSpec(memory_space=pltpu.VMEM)] * (len(kept) + len(came)),
        out_specs=[pl.BlockSpec(memory_space=pltpu.VMEM)] * len(shapes),
        scratch_shapes=[pltpu.VMEM(x.shape, x.dtype) for x in kept]
        + [pltpu.VMEM((scale_lines(lines) + 16, LANES), jnp.float32)],
        compiler_params=pltpu.CompilerParams(vmem_limit_bytes=16 * 1024 * 1024),
    )(*kept, *came)
    return list(outs[: len(kept)]), list(outs[len(kept) :])


def exchange(blocks, packets, n):
    return [
        lax.ppermute(block, "tm", [(i, i ^ (2 << packet[0])) for i in range(n)])
        for block, packet in zip(blocks, packets)
    ]


def per_device(item_table, item_shard, item_row, cluster_id, lengths):
    n = lax.axis_size("tm")
    users, slab = item_row.shape[1:]
    rows, width = item_table.shape
    total = users * slab
    owned = K // n
    m = bits_for(n) - 1
    cells = users * K // 2
    cell_bits = bits_for(cells)
    row_bits = bits_for(2 * rows)
    dest_shift = cell_bits + row_bits
    most = -(-4 * total // n // RUNS)
    assert users * 2 <= RUNS and most <= LANES - owned
    chains = user_chains(users, m)
    dummy = cells * 2

    other = lax.ppermute(item_table, "tm", [(i, i ^ 1) for i in range(n)])
    buckets = pl.pallas_call(
        functools.partial(
            prepare_kernel, n, owned, rows, dest_shift, row_bits, cell_bits, dummy, chains,
        ),
        out_shape=jax.ShapeDtypeStruct((n, RUNS, LANES), jnp.int32),
        in_specs=[pl.BlockSpec(memory_space=pltpu.SMEM)]
        + [pl.BlockSpec(memory_space=pltpu.VMEM)] * 3,
        out_specs=pl.BlockSpec(memory_space=pltpu.VMEM),
        scratch_shapes=[
            pltpu.VMEM((LANES, LANES), jnp.int32),
            pltpu.VMEM((LANES, LANES), jnp.int32),
            pltpu.VMEM((n * RUNS, LANES), jnp.int32),
        ],
    )(
        lengths,
        item_shard.reshape(total // LANES, LANES),
        item_row.reshape(users, slab),
        cluster_id.reshape(users, slab),
    )
    requests = lax.all_to_all(buckets, "tm", split_axis=0, concat_axis=0, tiled=True)
    counts = jnp.sum(requests[:, :users, LANES - owned :], axis=0).astype(jnp.float32)

    sums_rows = -(-(cells + 1) * 2 // 256) * 256
    lines = [size * (K // 2) for _, size, _ in chains]
    packets = packets_of(chains, 0, lines)
    parts = pl.pallas_call(
        functools.partial(
            add_kernel, n, users * LANES + LANES - owned, cell_bits, chains, packets
        ),
        out_shape=[jax.ShapeDtypeStruct((r, LANES), jnp.float32) for r in lines]
        + [packet_shape(p) for p in packets],
        in_specs=[
            pl.BlockSpec(memory_space=pltpu.VMEM),
            pl.BlockSpec(memory_space=pl.ANY),
            pl.BlockSpec(memory_space=pl.ANY),
        ],
        out_specs=[pl.BlockSpec(memory_space=pl.ANY)] * len(chains)
        + [pl.BlockSpec(memory_space=pltpu.VMEM)] * len(packets),
        scratch_shapes=[
            pltpu.VMEM((rows * 2, width), jnp.bfloat16),
            pltpu.VMEM((rows * 4, LANES), jnp.float32),
            pltpu.VMEM((sums_rows, LANES), jnp.float32),
            pltpu.VMEM((scale_lines(cells * 2) + 16, LANES), jnp.float32),
            pltpu.VMEM((2, n * RUNS * LANES), jnp.int32),
            pltpu.SMEM((SLOTS * RUNS * LANES,), jnp.int32),
            pltpu.SMEM((SLOTS * RUNS * LANES,), jnp.int32),
            pltpu.SemaphoreType.DMA((2, SLOTS)),
            pltpu.SemaphoreType.DMA((2 + len(chains),)),
        ],
        compiler_params=pltpu.CompilerParams(vmem_limit_bytes=32 * 1024 * 1024),
    )(requests.reshape(-1), item_table, other)
    kept, sent = list(parts[: len(chains)]), list(parts[len(chains) :])

    for stage in range(m):
        came = exchange(sent, packets, n)
        arrived = packets
        lines = [r // 2 for r in lines]
        packets = packets_of(chains, stage + 1, lines)
        kept, sent = merge(kept, came, arrived, packets)
    done = [x.reshape(size, owned, width) for x, (_, size, _) in zip(kept, chains)]
    return jnp.concatenate(done, axis=0) / jnp.maximum(counts, 1.0)[..., None]


def solution(mesh):
    return jax.shard_map(
        per_device,
        mesh=mesh,
        in_specs=(
            P("tm", None),
            P("tm", ("groups", "users"), None, None),
            P("tm", ("groups", "users"), None),
            P("tm", ("groups", "users"), None),
            P(("groups", "users")),
        ),
        out_specs=P(("groups", "users"), "tm", None),
        check_vma=False,
    )
```

```python
import functools
import math

import jax
import jax.numpy as jnp
from jax import lax
from jax.experimental import pallas as pl
from jax.experimental.pallas import tpu as pltpu
from jax.sharding import PartitionSpec as P

K = 1024
LANES = 128
SUB = 8
RUNS = 16
SLOTS = 16
MODE = 16
NONE = 2**31 - 1
CODE_TOP = 32766.0
TALL = 64


def bits_for(count):
    return (count - 1).bit_length()


def user_chains(users, m):
    orders = [(0, 2, 1, 3), (2, 1, 0, 3), (1, 0, 3, 2)] if m == 4 else [tuple(range(m))] * 3
    sizes = [-(-users * 3 // 8), users * 3 // 8]
    sizes.append(users - sum(sizes))
    chains, lo = [], 0
    for size, order in zip(sizes, orders):
        if size:
            chains.append((lo, size, order))
        lo += size
    return chains


def packets_of(chains, stage, rows):
    if stage == len(chains[0][2]):
        return []
    bits = {}
    for c, (_, _, order) in enumerate(chains):
        bits.setdefault(order[stage], []).append(c)
    return [
        (bit, [(c, rows[c]) for c in members], all(rows[c] % TALL == 0 for c in members))
        for bit, members in bits.items()
    ]


def packet_shape(packet):
    _, members, coded = packet
    lines = sum(rows for _, rows in members)
    if not coded:
        return jax.ShapeDtypeStruct((lines, LANES), jnp.float32)
    return jax.ShapeDtypeStruct((lines + scale_lines(lines), LANES), jnp.int16)


def scale_lines(lines):
    return -(-lines // TALL // 16) * 16


def scale_of(exponent):
    return jnp.exp(exponent * (math.log(2.0) / 64.0))


def several(count, block):
    def turn(t, _):
        for k in range(4):
            block(4 * t + k)
        return 0

    lax.fori_loop(0, count // 4, turn, 0)
    for i in range(count // 4 * 4, count):
        block(i)


def encode(packet, sources, out_ref, scales):
    done = 0
    for (_, rows), (ref, start) in zip(packet[1], sources):
        if not packet[2]:
            out_ref[pl.ds(done, rows), :] = ref[pl.ds(start, rows), :]
            done += rows
            continue

        def block(i, ref=ref, start=start, done=done):
            x = ref[pl.ds(start + i * TALL, TALL), :]
            top = jnp.maximum(jnp.max(jnp.abs(x), axis=0, keepdims=True), 1e-33)
            exponent = jnp.ceil(jnp.log(top) * (64.0 / math.log(2.0)))
            code = jnp.round(x * (CODE_TOP / scale_of(exponent)))
            code = code.astype(jnp.int32).astype(jnp.int16)
            out_ref[pl.ds(pl.multiple_of(done + i * TALL, TALL), TALL), :] = code
            scales[pl.ds(done // TALL + i, 1), :] = exponent

        several(rows // TALL, block)
        done += rows
    if packet[2]:
        out_ref[pl.ds(done, scale_lines(done)), :] = (
            scales[pl.ds(0, scale_lines(done)), :].astype(jnp.int32).astype(jnp.int16)
        )


def add_packet(packet, ref, sums, scales):
    if packet[2]:
        lines = sum(rows for _, rows in packet[1])
        scales[pl.ds(0, scale_lines(lines)), :] = ref[
            pl.ds(lines, scale_lines(lines)), :
        ].astype(jnp.float32)
    done = 0
    for c, rows in packet[1]:
        if not packet[2]:
            sums[c][...] = sums[c][...] + ref[pl.ds(done, rows), :]
            done += rows
            continue

        def block(i, c=c, done=done):
            exponent = scales[pl.ds(done // TALL + i, 1), :]
            code = ref[pl.ds(pl.multiple_of(done + i * TALL, TALL), TALL), :]
            at = pl.ds(pl.multiple_of(i * TALL, TALL), TALL)
            value = code.astype(jnp.float32) * (scale_of(exponent) * (1.0 / CODE_TOP))
            sums[c][at, :] = sums[c][at, :] + value

        several(rows // TALL, block)
        done += rows


def sort_tiles(tiles):
    count = len(tiles)
    tile_bits = bits_for(count)
    sub = lax.broadcasted_iota(jnp.int32, (SUB, LANES), 0)
    lane = lax.broadcasted_iota(jnp.int32, (SUB, LANES), 1)
    total_bits = tile_bits + 3 + 7

    def bit_mask(bit):
        if bit < tile_bits + 3:
            return ((sub >> (bit - tile_bits)) & 1) == 1
        return ((lane >> (bit - tile_bits - 3)) & 1) == 1

    masks = {b: bit_mask(b) for b in range(tile_bits, total_bits)}
    flips = {b: jnp.where(masks[b], -1, 0) for b in masks}

    def flip(t, phase):
        if phase >= total_bits:
            return 0
        if phase < tile_bits:
            return -1 if (t >> phase) & 1 else 0
        return flips[phase]

    for phase in range(1, total_bits + 1):
        changed = []
        for t in range(count):
            old = flip(t, phase - 1) if phase > 1 else 0
            new = flip(t, phase)
            if isinstance(old, int) and isinstance(new, int):
                turn = old ^ new
                changed.append(tiles[t] if turn == 0 else ~tiles[t])
            else:
                changed.append(tiles[t] ^ (old ^ new))
        tiles = changed
        for bit in reversed(range(phase)):
            if bit < tile_bits:
                step = 1 << bit
                tiles = list(tiles)
                for t in range(count):
                    if not t & step:
                        a, b = tiles[t], tiles[t | step]
                        tiles[t], tiles[t | step] = jnp.minimum(a, b), jnp.maximum(a, b)
                continue
            if bit < tile_bits + 3:
                axis, step, size = 0, 1 << (bit - tile_bits), SUB
            else:
                axis, step, size = 1, 1 << (bit - tile_bits - 3), LANES
            upper = masks[bit]
            moved = []
            for x in tiles:
                down = pltpu.roll(x, step, axis=axis)
                if 2 * step == size:
                    other = down
                else:
                    other = jnp.where(upper, down, pltpu.roll(x, size - step, axis=axis))
                moved.append(
                    jnp.where(upper, jnp.maximum(x, other), jnp.minimum(x, other))
                )
            tiles = moved
    return tiles


def prepare_kernel(
    n, owned, table_rows, dest_shift, row_bits, cell_bits, dummy, chains,
    lengths_ref, shard_ref, row_ref, cluster_ref, out_ref, order, straight, runs,
):
    users, slab = row_ref.shape
    sub = lax.broadcasted_iota(jnp.int32, (SUB, LANES), 0)
    lane = lax.broadcasted_iota(jnp.int32, (SUB, LANES), 1)
    me = lax.axis_index("tm")
    length = jnp.zeros((SUB, LANES), jnp.int32)
    live_total = jnp.int32(0)
    for u in range(users):
        length = jnp.where(sub == u, lengths_ref[u], length)
        live_total += jnp.clip(lengths_ref[u] - me * slab, 0, slab)
    length = length - me * slab

    base = jnp.zeros((SUB, LANES), jnp.int32)
    in_chain = jnp.zeros((SUB, LANES), jnp.int32)
    chain_size = jnp.zeros((SUB, LANES), jnp.int32)
    chain_at = []
    for lo, size, _ in chains:
        inside = (sub >= lo) & (sub < lo + size)
        base = jnp.where(inside, lo * (K // 2), base)
        in_chain = jnp.where(inside, sub - lo, in_chain)
        chain_size = jnp.where(inside, size, chain_size)
        chain_at.append(inside)

    owner_shift = bits_for(owned)
    tiles = []
    spare = LANES - owned
    hot_owner = [[] for _ in range(users)]
    hot_slot = [[] for _ in range(users)]
    owner_iota = lax.broadcasted_iota(jnp.int32, (n, LANES), 0)
    slot_iota = lax.broadcasted_iota(jnp.int32, (LANES, LANES), 0)
    for j in range(slab // LANES):
        at = pl.ds(j * LANES, LANES)
        row, cluster = row_ref[:, at], cluster_ref[:, at]
        shard = shard_ref[pl.ds(j, users, stride=slab // LANES), :]
        owner = lax.shift_right_logical(cluster, owner_shift)
        low = cluster & (owned - 1)
        live = lane + j * LANES < length
        dest = (shard & ~1) | (owner & 1)
        away = lax.shift_right_logical(owner ^ dest, 1)
        spread = jnp.zeros((SUB, LANES), jnp.int32)
        by_order = {}
        for (_, _, bits), inside in zip(chains, chain_at):
            if bits not in by_order:
                turned = jnp.zeros((SUB, LANES), jnp.int32)
                for bit in bits:
                    turned = turned * 2 + ((away >> bit) & 1)
                by_order[bits] = turned
            spread = jnp.where(inside, by_order[bits], spread)
        cell = base + ((spread * chain_size + in_chain) << owner_shift) + low
        there = ((shard ^ owner) & 1) * table_rows + row
        key = (dest << dest_shift) | (cell << row_bits) | there
        tiles.append(jnp.where(live, key, NONE))
        live_owner = jnp.where(live, owner, -1)
        for u in range(users):
            hot_owner[u].append((owner_iota == live_owner[u : u + 1, :]).astype(jnp.bfloat16))
            hot_slot[u].append((slot_iota == low[u : u + 1, :] + spare).astype(jnp.bfloat16))

    for u in range(users):
        counts = jnp.zeros((n, LANES), jnp.float32)
        for a, b in zip(hot_owner[u], hot_slot[u]):
            counts += lax.dot_general(
                a, b, (((1,), (1,)), ((), ())), preferred_element_type=jnp.float32
            )
        counts = counts.astype(jnp.int32)
        for d in range(n):
            out_ref[d, pl.ds(u, 1), :] = counts[d : d + 1, :]

    ends = []
    for d in range(n - 1):
        below = jnp.zeros((SUB, LANES), jnp.float32)
        for x in tiles:
            below += (x < ((d + 1) << dest_shift)).astype(jnp.float32)
        ends.append(jnp.sum(below).astype(jnp.int32))
    ends.append(live_total)

    empty = jnp.full((SUB, LANES), NONE, jnp.int32)
    tiles = sort_tiles(tiles + [empty] * ((1 << bits_for(len(tiles))) - len(tiles)))
    count = len(tiles)
    for t, x in enumerate(tiles):
        order[pl.ds(t * SUB, SUB), :] = x
    lines = [order[pl.ds(s, count, stride=SUB), :] for s in range(SUB)]
    straight[...] = jnp.concatenate(lines, axis=0).T

    at = (RUNS, LANES)
    run = lax.broadcasted_iota(jnp.int32, at, 0)
    lane = lax.broadcasted_iota(jnp.int32, at, 1)
    one_line = lax.broadcasted_iota(jnp.int32, (1, LANES), 1)
    start = jnp.int32(0)
    for d in range(n):
        count = ends[d] - start
        steps = lax.shift_right_logical(count + RUNS - 1, bits_for(RUNS))
        for j in range(RUNS):
            begin = start + j * steps
            off = begin & (LANES - 1)
            two = straight[pl.ds(lax.shift_right_logical(begin, bits_for(LANES)), 2), :]
            two = pltpu.roll(two, (LANES - off) & (LANES - 1), axis=1)
            runs[pl.ds(d * RUNS + j, 1), :] = jnp.where(one_line < LANES - off, two[:1], two[1:])
        mine = runs[pl.ds(d * RUNS, RUNS), :]
        valid = (lane < steps) & (run * steps + lane < count)
        there = mine & (2 * table_rows - 1)
        cell = lax.shift_right_logical(mine, row_bits) & ((1 << cell_bits) - 1)
        code = jnp.where(valid, (there << (cell_bits + 1)) | cell, dummy)
        cell = jnp.where(valid, cell, -1)
        following = pltpu.roll(cell, RUNS - 1, axis=0)
        same = (cell >= 0) & (cell == following) & (run < RUNS - 1)
        twice = jnp.max(jnp.where(same, 1.0, 0.0)).astype(jnp.int32)
        head = jnp.full((RUNS, LANES), steps | (twice << MODE), jnp.int32)
        beside = jnp.where(run < users, out_ref[d], head)
        out_ref[d] = jnp.where(lane < spare, code, beside)
        start = ends[d]


def widen_kernel(own_ref, other_ref, _, table):
    rows = own_ref.shape[0]

    def widen(i, _):
        for part, ref in enumerate((own_ref, other_ref)):
            x = ref[pl.ds(i * LANES, LANES), :].astype(jnp.float32)
            at = (part * rows + i * LANES) * 2
            table[pl.ds(at, LANES, stride=2), :] = x[:, :LANES]
            table[pl.ds(at + 1, LANES, stride=2), :] = x[:, LANES:]
        return 0

    lax.fori_loop(0, rows // LANES, widen, 0)


def add_kernel(n, head_at, cell_bits, request_ref, table, sums, lists, cells, rows_at, list_sems):
    stride = RUNS * LANES
    low = (2 << cell_bits) - 1

    def reads(s):
        at = pl.ds(pl.multiple_of(s * stride, stride), stride)
        slot = lax.rem(s, SLOTS)
        to = pl.ds(pl.multiple_of(slot * stride, stride), stride)
        return [
            pltpu.make_async_copy(lists.at[part, at], ref.at[to], list_sems.at[part, slot])
            for part, ref in enumerate((cells, rows_at))
        ]

    def take_apart(s, _):
        at = pl.ds(pl.multiple_of(s * stride, stride), stride)
        code = request_ref[at]
        lists[0, at] = code & low
        lists[1, at] = lax.shift_right_logical(code, cell_bits + 1)

        @pl.when(s < SLOTS)
        def _():
            for copy in reads(s):
                copy.start()

        return 0

    lax.fori_loop(0, n, take_apart, 0)

    def clear(i, _):
        sums[pl.ds(i * 64, 64)] = jnp.zeros((64, 2, LANES), jnp.float32)
        return 0

    lax.fori_loop(0, sums.shape[0] // 64, clear, 0)

    def source(s, _):
        for copy in reads(s):
            copy.wait()
        begin = lax.rem(s, SLOTS) * stride
        head = cells[begin + head_at] | rows_at[begin + head_at] << (cell_bits + 1)
        steps = head & ((1 << MODE) - 1)

        @pl.when(head < (1 << MODE))
        def _():
            def step(i, _):
                new = []
                for k in range(RUNS):
                    cell = cells[begin + i + k * LANES]
                    row = rows_at[begin + i + k * LANES]
                    new.append((cell, sums[cell] + table[row]))
                for cell, value in new:
                    sums[cell] = value
                return 0

            lax.fori_loop(0, steps, step, 0)

        @pl.when(head >= (1 << MODE))
        def _():
            def step(i, _):
                for k in range(RUNS):
                    cell = cells[begin + i + k * LANES]
                    row = rows_at[begin + i + k * LANES]
                    sums[cell] = sums[cell] + table[row]
                return 0

            lax.fori_loop(0, steps, step, 0)

        @pl.when(s + SLOTS < n)
        def _():
            for copy in reads(s + SLOTS):
                copy.start()

        return 0

    lax.fori_loop(0, n, source, 0)


def split_kernel(chains, packets, sums, *refs):
    keep_refs, packet_refs, scales = refs[: len(chains)], refs[len(chains) : -1], refs[-1]
    for (lo, size, _), ref in zip(chains, keep_refs):
        ref[...] = sums[pl.ds(lo * K, size * (K // 2)), :]
    for packet, ref in zip(packets, packet_refs):
        sources = [(sums, chains[c][0] * K + rows) for c, rows in packet[1]]
        encode(packet, sources, ref, scales)


def merge_kernel(chains, arrived, packets, *refs):
    refs = list(refs)
    take = lambda k: [refs.pop(0) for _ in range(k)]
    kept, came = take(chains), take(len(arrived))
    keep_refs, packet_refs = take(chains), take(len(packets))
    sums, scales = refs[:chains], refs[chains]
    for ref, total in zip(kept, sums):
        total[...] = ref[...]
    for packet, ref in zip(arrived, came):
        add_packet(packet, ref, sums, scales)
    for total, ref in zip(sums, keep_refs):
        ref[...] = total[pl.ds(0, ref.shape[0]), :]
    for packet, ref in zip(packets, packet_refs):
        encode(packet, [(sums[c], rows) for c, rows in packet[1]], ref, scales)


def merge(kept, came, arrived, packets):
    last = not packets
    shapes = [
        jax.ShapeDtypeStruct((x.shape[0] if last else x.shape[0] // 2, LANES), x.dtype)
        for x in kept
    ] + [packet_shape(p) for p in packets]
    lines = max(x.shape[0] for x in came)
    outs = pl.pallas_call(
        functools.partial(merge_kernel, len(kept), arrived, packets),
        out_shape=shapes,
        in_specs=[pl.BlockSpec(memory_space=pltpu.VMEM)] * (len(kept) + len(came)),
        out_specs=[pl.BlockSpec(memory_space=pltpu.VMEM)] * len(shapes),
        scratch_shapes=[pltpu.VMEM(x.shape, x.dtype) for x in kept]
        + [pltpu.VMEM((scale_lines(lines) + 16, LANES), jnp.float32)],
        compiler_params=pltpu.CompilerParams(vmem_limit_bytes=16 * 1024 * 1024),
    )(*kept, *came)
    return list(outs[: len(kept)]), list(outs[len(kept) :])


def exchange(blocks, packets, n):
    return [
        lax.ppermute(block, "tm", [(i, i ^ (2 << packet[0])) for i in range(n)])
        for block, packet in zip(blocks, packets)
    ]


def per_device(item_table, item_shard, item_row, cluster_id, lengths):
    n = lax.axis_size("tm")
    users, slab = item_row.shape[1:]
    rows, width = item_table.shape
    total = users * slab
    owned = K // n
    m = bits_for(n) - 1
    cells = users * K // 2
    cell_bits = bits_for(cells)
    row_bits = bits_for(2 * rows)
    dest_shift = cell_bits + row_bits
    most = -(-4 * total // n // RUNS)
    assert users * 2 <= RUNS and most <= LANES - owned
    chains = user_chains(users, m)
    dummy = cells

    other = lax.ppermute(item_table, "tm", [(i, i ^ 1) for i in range(n)])
    buckets = pl.pallas_call(
        functools.partial(
            prepare_kernel, n, owned, rows, dest_shift, row_bits, cell_bits, dummy, chains,
        ),
        out_shape=jax.ShapeDtypeStruct((n, RUNS, LANES), jnp.int32),
        in_specs=[pl.BlockSpec(memory_space=pltpu.SMEM)]
        + [pl.BlockSpec(memory_space=pltpu.VMEM)] * 3,
        out_specs=pl.BlockSpec(memory_space=pltpu.VMEM),
        scratch_shapes=[
            pltpu.VMEM((LANES, LANES), jnp.int32),
            pltpu.VMEM((LANES, LANES), jnp.int32),
            pltpu.VMEM((n * RUNS, LANES), jnp.int32),
        ],
    )(
        lengths,
        item_shard.reshape(total // LANES, LANES),
        item_row.reshape(users, slab),
        cluster_id.reshape(users, slab),
    )
    requests = lax.all_to_all(buckets, "tm", split_axis=0, concat_axis=0, tiled=True)
    counts = jnp.sum(requests[:, :users, LANES - owned :], axis=0).astype(jnp.float32)

    requests = requests.reshape(-1)
    table = pl.pallas_call(
        widen_kernel,
        out_shape=jax.ShapeDtypeStruct((rows * 4, LANES), jnp.float32),
        in_specs=[pl.BlockSpec(memory_space=pltpu.VMEM)] * 2
        + [pl.BlockSpec(memory_space=pl.ANY)],
        out_specs=pl.BlockSpec(memory_space=pltpu.VMEM),
        compiler_params=pltpu.CompilerParams(vmem_limit_bytes=16 * 1024 * 1024),
    )(item_table, other, requests)
    sums = pl.pallas_call(
        functools.partial(add_kernel, n, users * LANES + LANES - owned, cell_bits),
        out_shape=jax.ShapeDtypeStruct((cells + 64, 2, LANES), jnp.float32),
        in_specs=[pl.BlockSpec(memory_space=pltpu.VMEM)] * 2,
        out_specs=pl.BlockSpec(memory_space=pltpu.VMEM),
        scratch_shapes=[
            pltpu.VMEM((2, n * RUNS * LANES), jnp.int32),
            pltpu.SMEM((SLOTS * RUNS * LANES,), jnp.int32),
            pltpu.SMEM((SLOTS * RUNS * LANES,), jnp.int32),
            pltpu.SemaphoreType.DMA((2, SLOTS)),
        ],
        compiler_params=pltpu.CompilerParams(vmem_limit_bytes=16 * 1024 * 1024),
    )(requests, table.reshape(rows * 2, 2, LANES))
    lines = [size * (K // 2) for _, size, _ in chains]
    packets = packets_of(chains, 0, lines)
    parts = pl.pallas_call(
        functools.partial(split_kernel, chains, packets),
        out_shape=[jax.ShapeDtypeStruct((r, LANES), jnp.float32) for r in lines]
        + [packet_shape(p) for p in packets],
        in_specs=[pl.BlockSpec(memory_space=pltpu.VMEM)],
        out_specs=[pl.BlockSpec(memory_space=pltpu.VMEM)] * (len(chains) + len(packets)),
        scratch_shapes=[pltpu.VMEM((scale_lines(cells * 2) + 16, LANES), jnp.float32)],
        compiler_params=pltpu.CompilerParams(vmem_limit_bytes=16 * 1024 * 1024),
    )(sums.reshape(-1, LANES))
    kept, sent = list(parts[: len(chains)]), list(parts[len(chains) :])

    for stage in range(m):
        came = exchange(sent, packets, n)
        arrived = packets
        lines = [r // 2 for r in lines]
        packets = packets_of(chains, stage + 1, lines)
        kept, sent = merge(kept, came, arrived, packets)
    done = [x.reshape(size, owned, width) for x, (_, size, _) in zip(kept, chains)]
    return jnp.concatenate(done, axis=0) / jnp.maximum(counts, 1.0)[..., None]


def solution(mesh):
    return jax.shard_map(
        per_device,
        mesh=mesh,
        in_specs=(
            P("tm", None),
            P("tm", ("groups", "users"), None, None),
            P("tm", ("groups", "users"), None),
            P("tm", ("groups", "users"), None),
            P(("groups", "users")),
        ),
        out_specs=P(("groups", "users"), "tm", None),
        check_vma=False,
    )
```

```python
import functools
import math

import jax
import jax.numpy as jnp
from jax import lax
from jax.experimental import pallas as pl
from jax.experimental.pallas import tpu as pltpu
from jax.sharding import PartitionSpec as P

K = 1024
LANES = 128
SUB = 8
RUNS = 16
PART = 8
SLOTS = 16
MODE = 16
NONE = 2**31 - 1
CODE_TOP = 32766.0
TALL = 64


def bits_for(count):
    return (count - 1).bit_length()


def user_chains(users, m):
    orders = [(0, 2, 1, 3), (2, 1, 0, 3), (1, 0, 3, 2)] if m == 4 else [tuple(range(m))] * 3
    sizes = [-(-users * 3 // 8), users * 3 // 8]
    sizes.append(users - sum(sizes))
    chains, lo = [], 0
    for size, order in zip(sizes, orders):
        if size:
            chains.append((lo, size, order))
        lo += size
    return chains


def packets_of(chains, stage, rows):
    if stage == len(chains[0][2]):
        return []
    bits = {}
    for c, (_, _, order) in enumerate(chains):
        bits.setdefault(order[stage], []).append(c)
    return [
        (bit, [(c, rows[c]) for c in members], all(rows[c] % TALL == 0 for c in members))
        for bit, members in bits.items()
    ]


def packet_shape(packet):
    _, members, coded = packet
    lines = sum(rows for _, rows in members)
    if not coded:
        return jax.ShapeDtypeStruct((lines, LANES), jnp.float32)
    return jax.ShapeDtypeStruct((lines + scale_lines(lines), LANES), jnp.int16)


def scale_lines(lines):
    return -(-lines // TALL // 16) * 16


def scale_of(exponent):
    return jnp.exp(exponent * (math.log(2.0) / 64.0))


def several(count, block):
    def turn(t, _):
        for k in range(4):
            block(4 * t + k)
        return 0

    lax.fori_loop(0, count // 4, turn, 0)
    for i in range(count // 4 * 4, count):
        block(i)


def encode(packet, sources, out_ref, scales):
    done = 0
    for (_, rows), (ref, start) in zip(packet[1], sources):
        if not packet[2]:
            out_ref[pl.ds(done, rows), :] = ref[pl.ds(start, rows), :]
            done += rows
            continue

        def block(i, ref=ref, start=start, done=done):
            x = ref[pl.ds(start + i * TALL, TALL), :]
            top = jnp.maximum(jnp.max(jnp.abs(x), axis=0, keepdims=True), 1e-33)
            exponent = jnp.ceil(jnp.log(top) * (64.0 / math.log(2.0)))
            code = jnp.round(x * (CODE_TOP / scale_of(exponent)))
            code = code.astype(jnp.int32).astype(jnp.int16)
            out_ref[pl.ds(pl.multiple_of(done + i * TALL, TALL), TALL), :] = code
            scales[pl.ds(done // TALL + i, 1), :] = exponent

        several(rows // TALL, block)
        done += rows
    if packet[2]:
        out_ref[pl.ds(done, scale_lines(done)), :] = (
            scales[pl.ds(0, scale_lines(done)), :].astype(jnp.int32).astype(jnp.int16)
        )


def add_packet(packet, ref, sums, scales):
    if packet[2]:
        lines = sum(rows for _, rows in packet[1])
        scales[pl.ds(0, scale_lines(lines)), :] = ref[
            pl.ds(lines, scale_lines(lines)), :
        ].astype(jnp.float32)
    done = 0
    for c, rows in packet[1]:
        if not packet[2]:
            sums[c][...] = sums[c][...] + ref[pl.ds(done, rows), :]
            done += rows
            continue

        def block(i, c=c, done=done):
            exponent = scales[pl.ds(done // TALL + i, 1), :]
            code = ref[pl.ds(pl.multiple_of(done + i * TALL, TALL), TALL), :]
            at = pl.ds(pl.multiple_of(i * TALL, TALL), TALL)
            value = code.astype(jnp.float32) * (scale_of(exponent) * (1.0 / CODE_TOP))
            sums[c][at, :] = sums[c][at, :] + value

        several(rows // TALL, block)
        done += rows


def sort_tiles(tiles):
    count = len(tiles)
    tile_bits = bits_for(count)
    sub = lax.broadcasted_iota(jnp.int32, (SUB, LANES), 0)
    lane = lax.broadcasted_iota(jnp.int32, (SUB, LANES), 1)
    total_bits = tile_bits + 3 + 7

    def bit_mask(bit):
        if bit < tile_bits + 3:
            return ((sub >> (bit - tile_bits)) & 1) == 1
        return ((lane >> (bit - tile_bits - 3)) & 1) == 1

    masks = {b: bit_mask(b) for b in range(tile_bits, total_bits)}
    flips = {b: jnp.where(masks[b], -1, 0) for b in masks}

    def flip(t, phase):
        if phase >= total_bits:
            return 0
        if phase < tile_bits:
            return -1 if (t >> phase) & 1 else 0
        return flips[phase]

    for phase in range(1, total_bits + 1):
        changed = []
        for t in range(count):
            old = flip(t, phase - 1) if phase > 1 else 0
            new = flip(t, phase)
            if isinstance(old, int) and isinstance(new, int):
                turn = old ^ new
                changed.append(tiles[t] if turn == 0 else ~tiles[t])
            else:
                changed.append(tiles[t] ^ (old ^ new))
        tiles = changed
        for bit in reversed(range(phase)):
            if bit < tile_bits:
                step = 1 << bit
                tiles = list(tiles)
                for t in range(count):
                    if not t & step:
                        a, b = tiles[t], tiles[t | step]
                        tiles[t], tiles[t | step] = jnp.minimum(a, b), jnp.maximum(a, b)
                continue
            if bit < tile_bits + 3:
                axis, step, size = 0, 1 << (bit - tile_bits), SUB
            else:
                axis, step, size = 1, 1 << (bit - tile_bits - 3), LANES
            upper = masks[bit]
            moved = []
            for x in tiles:
                down = pltpu.roll(x, step, axis=axis)
                if 2 * step == size:
                    other = down
                else:
                    other = jnp.where(upper, down, pltpu.roll(x, size - step, axis=axis))
                moved.append(
                    jnp.where(upper, jnp.maximum(x, other), jnp.minimum(x, other))
                )
            tiles = moved
    return tiles


def prepare_kernel(
    n, owned, table_rows, dest_shift, row_bits, cell_bits, dummy, chains,
    lengths_ref, shard_ref, row_ref, cluster_ref, out_ref, order, straight, runs,
):
    users, slab = row_ref.shape
    sub = lax.broadcasted_iota(jnp.int32, (SUB, LANES), 0)
    lane = lax.broadcasted_iota(jnp.int32, (SUB, LANES), 1)
    me = lax.axis_index("tm")
    length = jnp.zeros((SUB, LANES), jnp.int32)
    live_total = jnp.int32(0)
    for u in range(users):
        length = jnp.where(sub == u, lengths_ref[u], length)
        live_total += jnp.clip(lengths_ref[u] - me * slab, 0, slab)
    length = length - me * slab

    base = jnp.zeros((SUB, LANES), jnp.int32)
    in_chain = jnp.zeros((SUB, LANES), jnp.int32)
    chain_size = jnp.zeros((SUB, LANES), jnp.int32)
    chain_at = []
    for lo, size, _ in chains:
        inside = (sub >= lo) & (sub < lo + size)
        base = jnp.where(inside, lo * (K // 2), base)
        in_chain = jnp.where(inside, sub - lo, in_chain)
        chain_size = jnp.where(inside, size, chain_size)
        chain_at.append(inside)

    owner_shift = bits_for(owned)
    tiles = []
    spare = LANES - owned
    hot_owner = [[] for _ in range(users)]
    hot_slot = [[] for _ in range(users)]
    owner_iota = lax.broadcasted_iota(jnp.int32, (n, LANES), 0)
    slot_iota = lax.broadcasted_iota(jnp.int32, (LANES, LANES), 0)
    for j in range(slab // LANES):
        at = pl.ds(j * LANES, LANES)
        row, cluster = row_ref[:, at], cluster_ref[:, at]
        shard = shard_ref[pl.ds(j, users, stride=slab // LANES), :]
        owner = lax.shift_right_logical(cluster, owner_shift)
        low = cluster & (owned - 1)
        live = lane + j * LANES < length
        dest = (shard & ~1) | (owner & 1)
        away = lax.shift_right_logical(owner ^ dest, 1)
        spread = jnp.zeros((SUB, LANES), jnp.int32)
        by_order = {}
        for (_, _, bits), inside in zip(chains, chain_at):
            if bits not in by_order:
                turned = jnp.zeros((SUB, LANES), jnp.int32)
                for bit in bits:
                    turned = turned * 2 + ((away >> bit) & 1)
                by_order[bits] = turned
            spread = jnp.where(inside, by_order[bits], spread)
        cell = base + ((spread * chain_size + in_chain) << owner_shift) + low
        there = ((shard ^ owner) & 1) * table_rows + row
        key = (dest << dest_shift) | (cell << row_bits) | there
        tiles.append(jnp.where(live, key, NONE))
        live_owner = jnp.where(live, owner, -1)
        for u in range(users):
            hot_owner[u].append((owner_iota == live_owner[u : u + 1, :]).astype(jnp.bfloat16))
            hot_slot[u].append((slot_iota == low[u : u + 1, :] + spare).astype(jnp.bfloat16))

    for u in range(users):
        counts = jnp.zeros((n, LANES), jnp.float32)
        for a, b in zip(hot_owner[u], hot_slot[u]):
            counts += lax.dot_general(
                a, b, (((1,), (1,)), ((), ())), preferred_element_type=jnp.float32
            )
        counts = counts.astype(jnp.int32)
        for d in range(n):
            out_ref[d, pl.ds(u, 1), :] = counts[d : d + 1, :]

    ends = []
    for d in range(n - 1):
        below = jnp.zeros((SUB, LANES), jnp.float32)
        for x in tiles:
            below += (x < ((d + 1) << dest_shift)).astype(jnp.float32)
        ends.append(jnp.sum(below).astype(jnp.int32))
    ends.append(live_total)

    empty = jnp.full((SUB, LANES), NONE, jnp.int32)
    tiles = sort_tiles(tiles + [empty] * ((1 << bits_for(len(tiles))) - len(tiles)))
    count = len(tiles)
    for t, x in enumerate(tiles):
        order[pl.ds(t * SUB, SUB), :] = x
    lines = [order[pl.ds(s, count, stride=SUB), :] for s in range(SUB)]
    straight[...] = jnp.concatenate(lines, axis=0).T

    at = (RUNS, LANES)
    run = lax.broadcasted_iota(jnp.int32, at, 0)
    lane = lax.broadcasted_iota(jnp.int32, at, 1)
    one_line = lax.broadcasted_iota(jnp.int32, (1, LANES), 1)
    start = jnp.int32(0)
    for d in range(n):
        count = ends[d] - start
        steps = lax.shift_right_logical(count + RUNS - 1, bits_for(RUNS))
        for j in range(RUNS):
            begin = start + j * steps
            off = begin & (LANES - 1)
            two = straight[pl.ds(lax.shift_right_logical(begin, bits_for(LANES)), 2), :]
            two = pltpu.roll(two, (LANES - off) & (LANES - 1), axis=1)
            runs[pl.ds(d * RUNS + j, 1), :] = jnp.where(one_line < LANES - off, two[:1], two[1:])
        mine = runs[pl.ds(d * RUNS, RUNS), :]
        valid = (lane < steps) & (run * steps + lane < count)
        there = mine & (2 * table_rows - 1)
        cell = lax.shift_right_logical(mine, row_bits) & ((1 << cell_bits) - 1)
        code = jnp.where(valid, (there << (cell_bits + 3)) | (cell << 1), dummy)
        cell = jnp.where(valid, cell, -1)
        following = pltpu.roll(cell, RUNS - 1, axis=0)
        same = (cell >= 0) & (cell == following) & (run < RUNS - 1)
        twice = jnp.max(jnp.where(same, 1.0, 0.0)).astype(jnp.int32)
        head = jnp.full((RUNS, LANES), steps | (twice << MODE), jnp.int32)
        beside = jnp.where(run < users, out_ref[d], head)
        out_ref[d] = jnp.where(lane < spare, code, beside)
        start = ends[d]


def widen_kernel(own_ref, other_ref, _, table):
    rows = own_ref.shape[0]

    def widen(i, _):
        for part, ref in enumerate((own_ref, other_ref)):
            x = ref[pl.ds(i * LANES, LANES), :].astype(jnp.float32)
            at = (part * rows + i * LANES) * 2
            table[pl.ds(at, LANES, stride=2), :] = x[:, :LANES]
            table[pl.ds(at + 1, LANES, stride=2), :] = x[:, LANES:]
        return 0

    lax.fori_loop(0, rows // LANES, widen, 0)


def add_kernel(n, head_at, cell_bits, request_ref, table, sums, lists, cells, rows_at, list_sems):
    stride = RUNS * LANES
    low = (4 << cell_bits) - 1

    def reads(s):
        at = pl.ds(pl.multiple_of(s * stride, stride), stride)
        slot = lax.rem(s, SLOTS)
        to = pl.ds(pl.multiple_of(slot * stride, stride), stride)
        return [
            pltpu.make_async_copy(lists.at[part, at], ref.at[to], list_sems.at[part, slot])
            for part, ref in enumerate((cells, rows_at))
        ]

    def take_apart(s, _):
        at = pl.ds(pl.multiple_of(s * stride, stride), stride)
        code = request_ref[at]
        lists[0, at] = code & low
        lists[1, at] = lax.shift_right_logical(code, cell_bits + 2)

        @pl.when(s < SLOTS)
        def _():
            for copy in reads(s):
                copy.start()

        return 0

    lax.fori_loop(0, n, take_apart, 0)

    def clear(i, _):
        sums[pl.ds(i * LANES, LANES), :] = jnp.zeros((LANES, LANES), jnp.float32)
        return 0

    lax.fori_loop(0, sums.shape[0] // LANES, clear, 0)

    def two_lines(at):
        return pl.ds(pl.multiple_of(at, 2), 2)

    def source(s, _):
        for copy in reads(s):
            copy.wait()
        begin = lax.rem(s, SLOTS) * stride
        head = cells[begin + head_at] | rows_at[begin + head_at] << (cell_bits + 2)
        steps = head & ((1 << MODE) - 1)

        @pl.when(head < (1 << MODE))
        def _():
            def step(at):
                for first in range(0, RUNS, PART):
                    new = []
                    for k in range(first, first + PART):
                        cell = two_lines(cells[at + k * LANES])
                        row = two_lines(rows_at[at + k * LANES])
                        new.append((cell, sums[cell, :] + table[row, :]))
                    for cell, value in new:
                        sums[cell, :] = value

            def two_steps(i, _):
                step(begin + 2 * i)
                step(begin + 2 * i + 1)
                return 0

            lax.fori_loop(0, lax.shift_right_logical(steps, 1), two_steps, 0)

            @pl.when((steps & 1) == 1)
            def _():
                step(begin + steps - 1)

        @pl.when(head >= (1 << MODE))
        def _():
            def single(i, _):
                for k in range(RUNS):
                    cell = two_lines(cells[begin + i + k * LANES])
                    row = two_lines(rows_at[begin + i + k * LANES])
                    sums[cell, :] = sums[cell, :] + table[row, :]
                return 0

            lax.fori_loop(0, steps, single, 0)

        @pl.when(s + SLOTS < n)
        def _():
            for copy in reads(s + SLOTS):
                copy.start()

        return 0

    lax.fori_loop(0, n, source, 0)


def split_kernel(chains, packets, sums, *refs):
    keep_refs, packet_refs, scales = refs[: len(chains)], refs[len(chains) : -1], refs[-1]
    for (lo, size, _), ref in zip(chains, keep_refs):
        ref[...] = sums[pl.ds(lo * K, size * (K // 2)), :]
    for packet, ref in zip(packets, packet_refs):
        sources = [(sums, chains[c][0] * K + rows) for c, rows in packet[1]]
        encode(packet, sources, ref, scales)


def merge_kernel(chains, arrived, packets, *refs):
    refs = list(refs)
    take = lambda k: [refs.pop(0) for _ in range(k)]
    kept, came = take(chains), take(len(arrived))
    keep_refs, packet_refs = take(chains), take(len(packets))
    sums, scales = refs[:chains], refs[chains]
    for ref, total in zip(kept, sums):
        total[...] = ref[...]
    for packet, ref in zip(arrived, came):
        add_packet(packet, ref, sums, scales)
    for total, ref in zip(sums, keep_refs):
        ref[...] = total[pl.ds(0, ref.shape[0]), :]
    for packet, ref in zip(packets, packet_refs):
        encode(packet, [(sums[c], rows) for c, rows in packet[1]], ref, scales)


def merge(kept, came, arrived, packets):
    last = not packets
    shapes = [
        jax.ShapeDtypeStruct((x.shape[0] if last else x.shape[0] // 2, LANES), x.dtype)
        for x in kept
    ] + [packet_shape(p) for p in packets]
    lines = max(x.shape[0] for x in came)
    outs = pl.pallas_call(
        functools.partial(merge_kernel, len(kept), arrived, packets),
        out_shape=shapes,
        in_specs=[pl.BlockSpec(memory_space=pltpu.VMEM)] * (len(kept) + len(came)),
        out_specs=[pl.BlockSpec(memory_space=pltpu.VMEM)] * len(shapes),
        scratch_shapes=[pltpu.VMEM(x.shape, x.dtype) for x in kept]
        + [pltpu.VMEM((scale_lines(lines) + 16, LANES), jnp.float32)],
        compiler_params=pltpu.CompilerParams(vmem_limit_bytes=16 * 1024 * 1024),
    )(*kept, *came)
    return list(outs[: len(kept)]), list(outs[len(kept) :])


def exchange(blocks, packets, n):
    return [
        lax.ppermute(block, "tm", [(i, i ^ (2 << packet[0])) for i in range(n)])
        for block, packet in zip(blocks, packets)
    ]


def per_device(item_table, item_shard, item_row, cluster_id, lengths):
    n = lax.axis_size("tm")
    users, slab = item_row.shape[1:]
    rows, width = item_table.shape
    total = users * slab
    owned = K // n
    m = bits_for(n) - 1
    cells = users * K // 2
    cell_bits = bits_for(cells)
    row_bits = bits_for(2 * rows)
    dest_shift = cell_bits + row_bits
    most = -(-4 * total // n // RUNS)
    assert users * 2 <= RUNS and most <= LANES - owned
    chains = user_chains(users, m)
    dummy = cells * 2

    other = lax.ppermute(item_table, "tm", [(i, i ^ 1) for i in range(n)])
    buckets = pl.pallas_call(
        functools.partial(
            prepare_kernel, n, owned, rows, dest_shift, row_bits, cell_bits, dummy, chains,
        ),
        out_shape=jax.ShapeDtypeStruct((n, RUNS, LANES), jnp.int32),
        in_specs=[pl.BlockSpec(memory_space=pltpu.SMEM)]
        + [pl.BlockSpec(memory_space=pltpu.VMEM)] * 3,
        out_specs=pl.BlockSpec(memory_space=pltpu.VMEM),
        scratch_shapes=[
            pltpu.VMEM((LANES, LANES), jnp.int32),
            pltpu.VMEM((LANES, LANES), jnp.int32),
            pltpu.VMEM((n * RUNS, LANES), jnp.int32),
        ],
    )(
        lengths,
        item_shard.reshape(total // LANES, LANES),
        item_row.reshape(users, slab),
        cluster_id.reshape(users, slab),
    )
    requests = lax.all_to_all(buckets, "tm", split_axis=0, concat_axis=0, tiled=True)
    counts = jnp.sum(requests[:, :users, LANES - owned :], axis=0).astype(jnp.float32)

    requests = requests.reshape(-1)
    table = pl.pallas_call(
        widen_kernel,
        out_shape=jax.ShapeDtypeStruct((rows * 4, LANES), jnp.float32),
        in_specs=[pl.BlockSpec(memory_space=pltpu.VMEM)] * 2
        + [pl.BlockSpec(memory_space=pl.ANY)],
        out_specs=pl.BlockSpec(memory_space=pltpu.VMEM),
        compiler_params=pltpu.CompilerParams(vmem_limit_bytes=16 * 1024 * 1024),
    )(item_table, other, requests)
    sums = pl.pallas_call(
        functools.partial(add_kernel, n, users * LANES + LANES - owned, cell_bits),
        out_shape=jax.ShapeDtypeStruct((cells * 2 + LANES, LANES), jnp.float32),
        in_specs=[pl.BlockSpec(memory_space=pltpu.VMEM)] * 2,
        out_specs=pl.BlockSpec(memory_space=pltpu.VMEM),
        scratch_shapes=[
            pltpu.VMEM((2, n * RUNS * LANES), jnp.int32),
            pltpu.SMEM((SLOTS * RUNS * LANES,), jnp.int32),
            pltpu.SMEM((SLOTS * RUNS * LANES,), jnp.int32),
            pltpu.SemaphoreType.DMA((2, SLOTS)),
        ],
        compiler_params=pltpu.CompilerParams(vmem_limit_bytes=16 * 1024 * 1024),
    )(requests, table)
    lines = [size * (K // 2) for _, size, _ in chains]
    packets = packets_of(chains, 0, lines)
    parts = pl.pallas_call(
        functools.partial(split_kernel, chains, packets),
        out_shape=[jax.ShapeDtypeStruct((r, LANES), jnp.float32) for r in lines]
        + [packet_shape(p) for p in packets],
        in_specs=[pl.BlockSpec(memory_space=pltpu.VMEM)],
        out_specs=[pl.BlockSpec(memory_space=pltpu.VMEM)] * (len(chains) + len(packets)),
        scratch_shapes=[pltpu.VMEM((scale_lines(cells * 2) + 16, LANES), jnp.float32)],
        compiler_params=pltpu.CompilerParams(vmem_limit_bytes=16 * 1024 * 1024),
    )(sums)
    kept, sent = list(parts[: len(chains)]), list(parts[len(chains) :])

    for stage in range(m):
        came = exchange(sent, packets, n)
        arrived = packets
        lines = [r // 2 for r in lines]
        packets = packets_of(chains, stage + 1, lines)
        kept, sent = merge(kept, came, arrived, packets)
    done = [x.reshape(size, owned, width) for x, (_, size, _) in zip(kept, chains)]
    return jnp.concatenate(done, axis=0) / jnp.maximum(counts, 1.0)[..., None]


def solution(mesh):
    return jax.shard_map(
        per_device,
        mesh=mesh,
        in_specs=(
            P("tm", None),
            P("tm", ("groups", "users"), None, None),
            P("tm", ("groups", "users"), None),
            P("tm", ("groups", "users"), None),
            P(("groups", "users")),
        ),
        out_specs=P(("groups", "users"), "tm", None),
        check_vma=False,
    )
```

```python
import functools
import math

import jax
import jax.numpy as jnp
from jax import lax
from jax.experimental import pallas as pl
from jax.experimental.pallas import tpu as pltpu
from jax.sharding import PartitionSpec as P

K = 1024
LANES = 128
SUB = 8
RUNS = 16
PART = 8
SLOTS = 16
MODE = 16
NONE = 2**31 - 1
CODE_TOP = 32766.0
TALL = 64


def bits_for(count):
    return (count - 1).bit_length()


def user_chains(users, m):
    orders = [(0, 2, 1, 3), (2, 1, 0, 3), (1, 0, 3, 2)] if m == 4 else [tuple(range(m))] * 3
    sizes = [-(-users * 3 // 8), users * 3 // 8]
    sizes.append(users - sum(sizes))
    chains, lo = [], 0
    for size, order in zip(sizes, orders):
        if size:
            chains.append((lo, size, order))
        lo += size
    return chains


def packets_of(chains, stage, rows):
    if stage == len(chains[0][2]):
        return []
    bits = {}
    for c, (_, _, order) in enumerate(chains):
        bits.setdefault(order[stage], []).append(c)
    return [
        (bit, [(c, rows[c]) for c in members], all(rows[c] % TALL == 0 for c in members))
        for bit, members in bits.items()
    ]


def packet_shape(packet):
    _, members, coded = packet
    lines = sum(rows for _, rows in members)
    if not coded:
        return jax.ShapeDtypeStruct((lines, LANES), jnp.float32)
    return jax.ShapeDtypeStruct((lines + scale_lines(lines), LANES), jnp.int16)


def scale_lines(lines):
    return -(-lines // TALL // 16) * 16


def scale_of(exponent):
    return jnp.exp(exponent * (math.log(2.0) / 64.0))


def several(count, block):
    def turn(t, _):
        for k in range(4):
            block(4 * t + k)
        return 0

    lax.fori_loop(0, count // 4, turn, 0)
    for i in range(count // 4 * 4, count):
        block(i)


def encode(packet, sources, out_ref, scales):
    done = 0
    for (_, rows), (ref, start) in zip(packet[1], sources):
        if not packet[2]:
            out_ref[pl.ds(done, rows), :] = ref[pl.ds(start, rows), :]
            done += rows
            continue

        def block(i, ref=ref, start=start, done=done):
            x = ref[pl.ds(start + i * TALL, TALL), :]
            top = jnp.maximum(jnp.max(jnp.abs(x), axis=0, keepdims=True), 1e-33)
            exponent = jnp.ceil(jnp.log(top) * (64.0 / math.log(2.0)))
            code = jnp.round(x * (CODE_TOP / scale_of(exponent)))
            code = code.astype(jnp.int32).astype(jnp.int16)
            out_ref[pl.ds(pl.multiple_of(done + i * TALL, TALL), TALL), :] = code
            scales[pl.ds(done // TALL + i, 1), :] = exponent

        several(rows // TALL, block)
        done += rows
    if packet[2]:
        out_ref[pl.ds(done, scale_lines(done)), :] = (
            scales[pl.ds(0, scale_lines(done)), :].astype(jnp.int32).astype(jnp.int16)
        )


def add_packet(packet, ref, sums, scales):
    if packet[2]:
        lines = sum(rows for _, rows in packet[1])
        scales[pl.ds(0, scale_lines(lines)), :] = ref[
            pl.ds(lines, scale_lines(lines)), :
        ].astype(jnp.float32)
    done = 0
    for c, rows in packet[1]:
        if not packet[2]:
            sums[c][...] = sums[c][...] + ref[pl.ds(done, rows), :]
            done += rows
            continue

        def block(i, c=c, done=done):
            exponent = scales[pl.ds(done // TALL + i, 1), :]
            code = ref[pl.ds(pl.multiple_of(done + i * TALL, TALL), TALL), :]
            at = pl.ds(pl.multiple_of(i * TALL, TALL), TALL)
            value = code.astype(jnp.float32) * (scale_of(exponent) * (1.0 / CODE_TOP))
            sums[c][at, :] = sums[c][at, :] + value

        several(rows // TALL, block)
        done += rows


def sort_tiles(tiles):
    count = len(tiles)
    tile_bits = bits_for(count)
    sub = lax.broadcasted_iota(jnp.int32, (SUB, LANES), 0)
    lane = lax.broadcasted_iota(jnp.int32, (SUB, LANES), 1)
    total_bits = tile_bits + 3 + 7

    def bit_mask(bit):
        if bit < tile_bits + 3:
            return ((sub >> (bit - tile_bits)) & 1) == 1
        return ((lane >> (bit - tile_bits - 3)) & 1) == 1

    masks = {b: bit_mask(b) for b in range(tile_bits, total_bits)}
    flips = {b: jnp.where(masks[b], -1, 0) for b in masks}

    def flip(t, phase):
        if phase >= total_bits:
            return 0
        if phase < tile_bits:
            return -1 if (t >> phase) & 1 else 0
        return flips[phase]

    for phase in range(1, total_bits + 1):
        changed = []
        for t in range(count):
            old = flip(t, phase - 1) if phase > 1 else 0
            new = flip(t, phase)
            if isinstance(old, int) and isinstance(new, int):
                turn = old ^ new
                changed.append(tiles[t] if turn == 0 else ~tiles[t])
            else:
                changed.append(tiles[t] ^ (old ^ new))
        tiles = changed
        for bit in reversed(range(phase)):
            if bit < tile_bits:
                step = 1 << bit
                tiles = list(tiles)
                for t in range(count):
                    if not t & step:
                        a, b = tiles[t], tiles[t | step]
                        tiles[t], tiles[t | step] = jnp.minimum(a, b), jnp.maximum(a, b)
                continue
            if bit < tile_bits + 3:
                axis, step, size = 0, 1 << (bit - tile_bits), SUB
            else:
                axis, step, size = 1, 1 << (bit - tile_bits - 3), LANES
            upper = masks[bit]
            moved = []
            for x in tiles:
                down = pltpu.roll(x, step, axis=axis)
                if 2 * step == size:
                    other = down
                else:
                    other = jnp.where(upper, down, pltpu.roll(x, size - step, axis=axis))
                moved.append(
                    jnp.where(upper, jnp.maximum(x, other), jnp.minimum(x, other))
                )
            tiles = moved
    return tiles


def prepare_kernel(
    n, owned, table_rows, dest_shift, row_bits, cell_bits, dummy, chains,
    lengths_ref, shard_ref, row_ref, cluster_ref, out_ref, order, straight, runs,
):
    users, slab = row_ref.shape
    sub = lax.broadcasted_iota(jnp.int32, (SUB, LANES), 0)
    lane = lax.broadcasted_iota(jnp.int32, (SUB, LANES), 1)
    me = lax.axis_index("tm")
    length = jnp.zeros((SUB, LANES), jnp.int32)
    live_total = jnp.int32(0)
    for u in range(users):
        length = jnp.where(sub == u, lengths_ref[u], length)
        live_total += jnp.clip(lengths_ref[u] - me * slab, 0, slab)
    length = length - me * slab

    base = jnp.zeros((SUB, LANES), jnp.int32)
    in_chain = jnp.zeros((SUB, LANES), jnp.int32)
    chain_size = jnp.zeros((SUB, LANES), jnp.int32)
    chain_at = []
    for lo, size, _ in chains:
        inside = (sub >= lo) & (sub < lo + size)
        base = jnp.where(inside, lo * (K // 2), base)
        in_chain = jnp.where(inside, sub - lo, in_chain)
        chain_size = jnp.where(inside, size, chain_size)
        chain_at.append(inside)

    owner_shift = bits_for(owned)
    tiles = []
    spare = LANES - owned
    hot_owner = [[] for _ in range(users)]
    hot_slot = [[] for _ in range(users)]
    owner_iota = lax.broadcasted_iota(jnp.int32, (n, LANES), 0)
    slot_iota = lax.broadcasted_iota(jnp.int32, (LANES, LANES), 0)
    for j in range(slab // LANES):
        at = pl.ds(j * LANES, LANES)
        row, cluster = row_ref[:, at], cluster_ref[:, at]
        shard = shard_ref[pl.ds(j, users, stride=slab // LANES), :]
        owner = lax.shift_right_logical(cluster, owner_shift)
        low = cluster & (owned - 1)
        live = lane + j * LANES < length
        dest = (shard & ~1) | (owner & 1)
        away = lax.shift_right_logical(owner ^ dest, 1)
        spread = jnp.zeros((SUB, LANES), jnp.int32)
        by_order = {}
        for (_, _, bits), inside in zip(chains, chain_at):
            if bits not in by_order:
                turned = jnp.zeros((SUB, LANES), jnp.int32)
                for bit in bits:
                    turned = turned * 2 + ((away >> bit) & 1)
                by_order[bits] = turned
            spread = jnp.where(inside, by_order[bits], spread)
        cell = base + ((spread * chain_size + in_chain) << owner_shift) + low
        there = ((shard ^ owner) & 1) * table_rows + row
        key = (dest << dest_shift) | (cell << row_bits) | there
        tiles.append(jnp.where(live, key, NONE))
        live_owner = jnp.where(live, owner, -1)
        for u in range(users):
            hot_owner[u].append((owner_iota == live_owner[u : u + 1, :]).astype(jnp.bfloat16))
            hot_slot[u].append((slot_iota == low[u : u + 1, :] + spare).astype(jnp.bfloat16))

    for u in range(users):
        counts = jnp.zeros((n, LANES), jnp.float32)
        for a, b in zip(hot_owner[u], hot_slot[u]):
            counts += lax.dot_general(
                a, b, (((1,), (1,)), ((), ())), preferred_element_type=jnp.float32
            )
        counts = counts.astype(jnp.int32)
        for d in range(n):
            out_ref[d, pl.ds(u, 1), :] = counts[d : d + 1, :]

    ends = []
    for d in range(n - 1):
        below = jnp.zeros((SUB, LANES), jnp.float32)
        for x in tiles:
            below += (x < ((d + 1) << dest_shift)).astype(jnp.float32)
        ends.append(jnp.sum(below).astype(jnp.int32))
    ends.append(live_total)

    empty = jnp.full((SUB, LANES), NONE, jnp.int32)
    tiles = sort_tiles(tiles + [empty] * ((1 << bits_for(len(tiles))) - len(tiles)))
    count = len(tiles)
    for t, x in enumerate(tiles):
        order[pl.ds(t * SUB, SUB), :] = x
    lines = [order[pl.ds(s, count, stride=SUB), :] for s in range(SUB)]
    straight[...] = jnp.concatenate(lines, axis=0).T

    at = (RUNS, LANES)
    run = lax.broadcasted_iota(jnp.int32, at, 0)
    lane = lax.broadcasted_iota(jnp.int32, at, 1)
    one_line = lax.broadcasted_iota(jnp.int32, (1, LANES), 1)
    start = jnp.int32(0)
    for d in range(n):
        count = ends[d] - start
        steps = lax.shift_right_logical(count + RUNS - 1, bits_for(RUNS))
        for j in range(RUNS):
            begin = start + j * steps
            off = begin & (LANES - 1)
            two = straight[pl.ds(lax.shift_right_logical(begin, bits_for(LANES)), 2), :]
            two = pltpu.roll(two, (LANES - off) & (LANES - 1), axis=1)
            runs[pl.ds(d * RUNS + j, 1), :] = jnp.where(one_line < LANES - off, two[:1], two[1:])
        mine = runs[pl.ds(d * RUNS, RUNS), :]
        valid = (lane < steps) & (run * steps + lane < count)
        there = mine & (2 * table_rows - 1)
        cell = lax.shift_right_logical(mine, row_bits) & ((1 << cell_bits) - 1)
        code = jnp.where(valid, (there << (cell_bits + 3)) | (cell << 1), dummy)
        cell = jnp.where(valid, cell, -1)
        following = pltpu.roll(cell, RUNS - 1, axis=0)
        same = (cell >= 0) & (cell == following) & (run < RUNS - 1)
        twice = jnp.max(jnp.where(same, 1.0, 0.0)).astype(jnp.int32)
        head = jnp.full((RUNS, LANES), steps | (twice << MODE), jnp.int32)
        beside = jnp.where(run < users, out_ref[d], head)
        out_ref[d] = jnp.where(lane < spare, code, beside)
        start = ends[d]


def add_kernel(
    n, head_at, cell_bits, request_ref, own_ref, other_ref, sums, narrow, table, codes, code_sems, sems
):
    stride = RUNS * LANES
    low = (4 << cell_bits) - 1
    rows = own_ref.shape[0]

    def read(s):
        at = pl.ds(pl.multiple_of(s * stride, stride), stride)
        slot = lax.rem(s, SLOTS)
        to = pl.ds(pl.multiple_of(slot * stride, stride), stride)
        return pltpu.make_async_copy(request_ref.at[at], codes.at[to], code_sems.at[slot])

    tables = [
        pltpu.make_async_copy(ref, narrow.at[pl.ds(part * rows, rows), :], sems.at[part])
        for part, ref in enumerate((own_ref, other_ref))
    ]
    for copy in tables:
        copy.start()

    def start_read(s, _):
        read(s).start()
        return 0

    lax.fori_loop(0, min(SLOTS, n), start_read, 0)

    def clear(i, _):
        sums[pl.ds(i * LANES, LANES), :] = jnp.zeros((LANES, LANES), jnp.float32)
        return 0

    lax.fori_loop(0, sums.shape[0] // LANES, clear, 0)

    def widen(i, _):
        x = narrow[pl.ds(i * LANES, LANES), :].astype(jnp.float32)
        table[pl.ds(i * 2 * LANES, LANES, stride=2), :] = x[:, :LANES]
        table[pl.ds(i * 2 * LANES + 1, LANES, stride=2), :] = x[:, LANES:]
        return 0

    blocks = rows // LANES
    for part, copy in enumerate(tables):
        copy.wait()
        lax.fori_loop(part * blocks, (part + 1) * blocks, widen, 0)

    def place(code):
        cell = pl.multiple_of(code & low, 2)
        row = pl.multiple_of(lax.shift_right_logical(code, cell_bits + 2), 2)
        return pl.ds(cell, 2), pl.ds(row, 2)

    def source(s, _):
        read(s).wait()
        begin = lax.rem(s, SLOTS) * stride
        head = codes[begin + head_at]
        steps = head & ((1 << MODE) - 1)

        @pl.when(head < (1 << MODE))
        def _():
            def step(at):
                for first in range(0, RUNS, PART):
                    new = []
                    for k in range(first, first + PART):
                        cell, row = place(codes[at + k * LANES])
                        new.append((cell, sums[cell, :] + table[row, :]))
                    for cell, value in new:
                        sums[cell, :] = value

            def two_steps(i, _):
                step(begin + 2 * i)
                step(begin + 2 * i + 1)
                return 0

            lax.fori_loop(0, lax.shift_right_logical(steps, 1), two_steps, 0)

            @pl.when((steps & 1) == 1)
            def _():
                step(begin + steps - 1)

        @pl.when(head >= (1 << MODE))
        def _():
            def single(i, _):
                for k in range(RUNS):
                    cell, row = place(codes[begin + i + k * LANES])
                    sums[cell, :] = sums[cell, :] + table[row, :]
                return 0

            lax.fori_loop(0, steps, single, 0)

        @pl.when(s + SLOTS < n)
        def _():
            read(s + SLOTS).start()

        return 0

    lax.fori_loop(0, n, source, 0)


def split_kernel(chains, packets, sums, *refs):
    keep_refs, packet_refs, scales = refs[: len(chains)], refs[len(chains) : -1], refs[-1]
    for (lo, size, _), ref in zip(chains, keep_refs):
        ref[...] = sums[pl.ds(lo * K, size * (K // 2)), :]
    for packet, ref in zip(packets, packet_refs):
        sources = [(sums, chains[c][0] * K + rows) for c, rows in packet[1]]
        encode(packet, sources, ref, scales)


def merge_kernel(chains, arrived, packets, *refs):
    refs = list(refs)
    take = lambda k: [refs.pop(0) for _ in range(k)]
    kept, came = take(chains), take(len(arrived))
    count_ref = refs.pop(0) if not packets else None
    keep_refs, packet_refs = take(chains if packets else 1), take(len(packets))
    sums, scales = refs[:chains], refs[chains]
    for ref, total in zip(kept, sums):
        total[...] = ref[...]
    for packet, ref in zip(arrived, came):
        add_packet(packet, ref, sums, scales)
    if not packets:
        at = 0
        for total in sums:
            rows = total.shape[0] // 2
            members = jnp.maximum(count_ref[pl.ds(at, rows), :], 1.0)
            for side in range(2):
                mean = total[pl.ds(side, rows, stride=2), :] / members
                keep_refs[0][pl.ds(at, rows), pl.ds(side * LANES, LANES)] = mean
            at += rows
        return
    for total, ref in zip(sums, keep_refs):
        ref[...] = total[pl.ds(0, ref.shape[0]), :]
    for packet, ref in zip(packets, packet_refs):
        encode(packet, [(sums[c], rows) for c, rows in packet[1]], ref, scales)


def merge(kept, came, arrived, packets, counts):
    if packets:
        shapes = [jax.ShapeDtypeStruct((x.shape[0] // 2, LANES), x.dtype) for x in kept]
        shapes += [packet_shape(p) for p in packets]
        extra = []
    else:
        lines = sum(x.shape[0] for x in kept)
        shapes = [jax.ShapeDtypeStruct((lines // 2, 2 * LANES), jnp.float32)]
        extra = [counts]
    lines = max(x.shape[0] for x in came)
    outs = pl.pallas_call(
        functools.partial(merge_kernel, len(kept), arrived, packets),
        out_shape=shapes,
        in_specs=[pl.BlockSpec(memory_space=pltpu.VMEM)] * (len(kept) + len(came) + len(extra)),
        out_specs=[pl.BlockSpec(memory_space=pltpu.VMEM)] * len(shapes),
        scratch_shapes=[pltpu.VMEM(x.shape, x.dtype) for x in kept]
        + [pltpu.VMEM((scale_lines(lines) + 16, LANES), jnp.float32)],
        compiler_params=pltpu.CompilerParams(vmem_limit_bytes=16 * 1024 * 1024),
    )(*kept, *came, *extra)
    if not packets:
        return outs[0]
    return list(outs[: len(kept)]), list(outs[len(kept) :])


def exchange(blocks, packets, n):
    return [
        lax.ppermute(block, "tm", [(i, i ^ (2 << packet[0])) for i in range(n)])
        for block, packet in zip(blocks, packets)
    ]


def per_device(item_table, item_shard, item_row, cluster_id, lengths):
    n = lax.axis_size("tm")
    users, slab = item_row.shape[1:]
    rows, width = item_table.shape
    total = users * slab
    owned = K // n
    m = bits_for(n) - 1
    cells = users * K // 2
    cell_bits = bits_for(cells)
    row_bits = bits_for(2 * rows)
    dest_shift = cell_bits + row_bits
    most = -(-4 * total // n // RUNS)
    assert users * 2 <= RUNS and most <= LANES - owned
    chains = user_chains(users, m)
    dummy = cells * 2

    other = lax.ppermute(item_table, "tm", [(i, i ^ 1) for i in range(n)])
    buckets = pl.pallas_call(
        functools.partial(
            prepare_kernel, n, owned, rows, dest_shift, row_bits, cell_bits, dummy, chains,
        ),
        out_shape=jax.ShapeDtypeStruct((n, RUNS, LANES), jnp.int32),
        in_specs=[pl.BlockSpec(memory_space=pltpu.SMEM)]
        + [pl.BlockSpec(memory_space=pltpu.VMEM)] * 3,
        out_specs=pl.BlockSpec(memory_space=pltpu.VMEM),
        scratch_shapes=[
            pltpu.VMEM((LANES, LANES), jnp.int32),
            pltpu.VMEM((LANES, LANES), jnp.int32),
            pltpu.VMEM((n * RUNS, LANES), jnp.int32),
        ],
    )(
        lengths,
        item_shard.reshape(total // LANES, LANES),
        item_row.reshape(users, slab),
        cluster_id.reshape(users, slab),
    )
    requests = lax.all_to_all(buckets, "tm", split_axis=0, concat_axis=0, tiled=True)
    counts = jnp.sum(requests[:, :users, LANES - owned :], axis=0).astype(jnp.float32)
    counts = counts.reshape(users * owned, 1)

    requests = requests.reshape(-1)
    sums = pl.pallas_call(
        functools.partial(add_kernel, n, users * LANES + LANES - owned, cell_bits),
        out_shape=jax.ShapeDtypeStruct((cells * 2 + LANES, LANES), jnp.float32),
        in_specs=[
            pl.BlockSpec(memory_space=pltpu.VMEM),
            pl.BlockSpec(memory_space=pltpu.HBM),
            pl.BlockSpec(memory_space=pl.ANY),
        ],
        out_specs=pl.BlockSpec(memory_space=pltpu.VMEM),
        scratch_shapes=[
            pltpu.VMEM((rows * 2, width), jnp.bfloat16),
            pltpu.VMEM((rows * 4, LANES), jnp.float32),
            pltpu.SMEM((SLOTS * RUNS * LANES,), jnp.int32),
            pltpu.SemaphoreType.DMA((SLOTS,)),
            pltpu.SemaphoreType.DMA((2,)),
        ],
        compiler_params=pltpu.CompilerParams(vmem_limit_bytes=32 * 1024 * 1024),
    )(requests, item_table, other)
    lines = [size * (K // 2) for _, size, _ in chains]
    packets = packets_of(chains, 0, lines)
    parts = pl.pallas_call(
        functools.partial(split_kernel, chains, packets),
        out_shape=[jax.ShapeDtypeStruct((r, LANES), jnp.float32) for r in lines]
        + [packet_shape(p) for p in packets],
        in_specs=[pl.BlockSpec(memory_space=pltpu.VMEM)],
        out_specs=[pl.BlockSpec(memory_space=pltpu.VMEM)] * (len(chains) + len(packets)),
        scratch_shapes=[pltpu.VMEM((scale_lines(cells * 2) + 16, LANES), jnp.float32)],
        compiler_params=pltpu.CompilerParams(vmem_limit_bytes=16 * 1024 * 1024),
    )(sums)
    kept, sent = list(parts[: len(chains)]), list(parts[len(chains) :])

    for stage in range(m):
        came = exchange(sent, packets, n)
        arrived = packets
        lines = [r // 2 for r in lines]
        packets = packets_of(chains, stage + 1, lines)
        if packets:
            kept, sent = merge(kept, came, arrived, packets, counts)
    means = merge(kept, came, arrived, packets, counts)
    return means.reshape(users, owned, width)


def solution(mesh):
    return jax.shard_map(
        per_device,
        mesh=mesh,
        in_specs=(
            P("tm", None),
            P("tm", ("groups", "users"), None, None),
            P("tm", ("groups", "users"), None),
            P("tm", ("groups", "users"), None),
            P(("groups", "users")),
        ),
        out_specs=P(("groups", "users"), "tm", None),
        check_vma=False,
    )
```

```python
import functools
import math

import jax
import jax.numpy as jnp
from jax import lax
from jax.experimental import pallas as pl
from jax.experimental.pallas import tpu as pltpu
from jax.sharding import PartitionSpec as P

K = 1024
LANES = 128
SUB = 8
RUNS = 16
PART = 8
SLOTS = 16
MODE = 16
NONE = 2**31 - 1
CODE_TOP = 32766.0
TALL = 64


def bits_for(count):
    return (count - 1).bit_length()


def user_chains(users, m):
    orders = [(0, 2, 1, 3), (2, 1, 0, 3), (1, 0, 3, 2)] if m == 4 else [tuple(range(m))] * 3
    sizes = [-(-users * 3 // 8), users * 3 // 8]
    sizes.append(users - sum(sizes))
    chains, lo = [], 0
    for size, order in zip(sizes, orders):
        if size:
            chains.append((lo, size, order))
        lo += size
    return chains


def packet_of(chain, stage, rows):
    order = chain[2]
    return (order[stage], rows, rows % TALL == 0) if stage < len(order) else None


def packet_shape(packet):
    _, lines, coded = packet
    if not coded:
        return jax.ShapeDtypeStruct((lines, LANES), jnp.float32)
    return jax.ShapeDtypeStruct((lines + scale_lines(lines), LANES), jnp.int16)


def scale_lines(lines):
    return -(-lines // TALL // 16) * 16


def scale_of(exponent):
    return jnp.exp(exponent * (math.log(2.0) / 64.0))


def several(count, block):
    def turn(t, _):
        for k in range(4):
            block(4 * t + k)
        return 0

    lax.fori_loop(0, count // 4, turn, 0)
    for i in range(count // 4 * 4, count):
        block(i)


def encode(packet, ref, start, out_ref, scales):
    _, rows, coded = packet
    if not coded:
        out_ref[...] = ref[pl.ds(start, rows), :]
        return

    def block(i):
        x = ref[pl.ds(start + i * TALL, TALL), :]
        top = jnp.maximum(jnp.max(jnp.abs(x), axis=0, keepdims=True), 1e-33)
        exponent = jnp.ceil(jnp.log(top) * (64.0 / math.log(2.0)))
        code = jnp.round(x * (CODE_TOP / scale_of(exponent)))
        code = code.astype(jnp.int32).astype(jnp.int16)
        out_ref[pl.ds(pl.multiple_of(i * TALL, TALL), TALL), :] = code
        scales[pl.ds(i, 1), :] = exponent

    several(rows // TALL, block)
    out_ref[pl.ds(rows, scale_lines(rows)), :] = (
        scales[pl.ds(0, scale_lines(rows)), :].astype(jnp.int32).astype(jnp.int16)
    )


def add_packet(packet, ref, total, scales):
    _, rows, coded = packet
    if not coded:
        total[...] = total[...] + ref[...]
        return
    scales[pl.ds(0, scale_lines(rows)), :] = ref[pl.ds(rows, scale_lines(rows)), :].astype(
        jnp.float32
    )

    def block(i):
        at = pl.ds(pl.multiple_of(i * TALL, TALL), TALL)
        scale = scale_of(scales[pl.ds(i, 1), :]) * (1.0 / CODE_TOP)
        total[at, :] = total[at, :] + ref[at, :].astype(jnp.float32) * scale

    several(rows // TALL, block)


def sort_tiles(tiles):
    count = len(tiles)
    tile_bits = bits_for(count)
    sub = lax.broadcasted_iota(jnp.int32, (SUB, LANES), 0)
    lane = lax.broadcasted_iota(jnp.int32, (SUB, LANES), 1)
    total_bits = tile_bits + 3 + 7

    def bit_mask(bit):
        if bit < tile_bits + 3:
            return ((sub >> (bit - tile_bits)) & 1) == 1
        return ((lane >> (bit - tile_bits - 3)) & 1) == 1

    masks = {b: bit_mask(b) for b in range(tile_bits, total_bits)}
    flips = {b: jnp.where(masks[b], -1, 0) for b in masks}

    def flip(t, phase):
        if phase >= total_bits:
            return 0
        if phase < tile_bits:
            return -1 if (t >> phase) & 1 else 0
        return flips[phase]

    for phase in range(1, total_bits + 1):
        changed = []
        for t in range(count):
            old = flip(t, phase - 1) if phase > 1 else 0
            new = flip(t, phase)
            if isinstance(old, int) and isinstance(new, int):
                turn = old ^ new
                changed.append(tiles[t] if turn == 0 else ~tiles[t])
            else:
                changed.append(tiles[t] ^ (old ^ new))
        tiles = changed
        for bit in reversed(range(phase)):
            if bit < tile_bits:
                step = 1 << bit
                tiles = list(tiles)
                for t in range(count):
                    if not t & step:
                        a, b = tiles[t], tiles[t | step]
                        tiles[t], tiles[t | step] = jnp.minimum(a, b), jnp.maximum(a, b)
                continue
            if bit < tile_bits + 3:
                axis, step, size = 0, 1 << (bit - tile_bits), SUB
            else:
                axis, step, size = 1, 1 << (bit - tile_bits - 3), LANES
            upper = masks[bit]
            moved = []
            for x in tiles:
                down = pltpu.roll(x, step, axis=axis)
                if 2 * step == size:
                    other = down
                else:
                    other = jnp.where(upper, down, pltpu.roll(x, size - step, axis=axis))
                moved.append(
                    jnp.where(upper, jnp.maximum(x, other), jnp.minimum(x, other))
                )
            tiles = moved
    return tiles


def prepare_kernel(
    n, owned, table_rows, dest_shift, row_bits, cell_bits, dummy, chains,
    lengths_ref, shard_ref, row_ref, cluster_ref, out_ref, order, straight, runs,
):
    users, slab = row_ref.shape
    sub = lax.broadcasted_iota(jnp.int32, (SUB, LANES), 0)
    lane = lax.broadcasted_iota(jnp.int32, (SUB, LANES), 1)
    me = lax.axis_index("tm")
    length = jnp.zeros((SUB, LANES), jnp.int32)
    live_total = jnp.int32(0)
    for u in range(users):
        length = jnp.where(sub == u, lengths_ref[u], length)
        live_total += jnp.clip(lengths_ref[u] - me * slab, 0, slab)
    length = length - me * slab

    base = jnp.zeros((SUB, LANES), jnp.int32)
    in_chain = jnp.zeros((SUB, LANES), jnp.int32)
    chain_size = jnp.zeros((SUB, LANES), jnp.int32)
    chain_at = []
    for lo, size, _ in chains:
        inside = (sub >= lo) & (sub < lo + size)
        base = jnp.where(inside, lo * (K // 2), base)
        in_chain = jnp.where(inside, sub - lo, in_chain)
        chain_size = jnp.where(inside, size, chain_size)
        chain_at.append(inside)

    owner_shift = bits_for(owned)
    tiles = []
    spare = LANES - owned
    hot_owner = [[] for _ in range(users)]
    hot_slot = [[] for _ in range(users)]
    owner_iota = lax.broadcasted_iota(jnp.int32, (n, LANES), 0)
    slot_iota = lax.broadcasted_iota(jnp.int32, (LANES, LANES), 0)
    for j in range(slab // LANES):
        at = pl.ds(j * LANES, LANES)
        row, cluster = row_ref[:, at], cluster_ref[:, at]
        shard = shard_ref[pl.ds(j, users, stride=slab // LANES), :]
        owner = lax.shift_right_logical(cluster, owner_shift)
        low = cluster & (owned - 1)
        live = lane + j * LANES < length
        dest = (shard & ~1) | (owner & 1)
        away = lax.shift_right_logical(owner ^ dest, 1)
        spread = jnp.zeros((SUB, LANES), jnp.int32)
        by_order = {}
        for (_, _, bits), inside in zip(chains, chain_at):
            if bits not in by_order:
                turned = jnp.zeros((SUB, LANES), jnp.int32)
                for bit in bits:
                    turned = turned * 2 + ((away >> bit) & 1)
                by_order[bits] = turned
            spread = jnp.where(inside, by_order[bits], spread)
        cell = base + ((spread * chain_size + in_chain) << owner_shift) + low
        there = ((shard ^ owner) & 1) * table_rows + row
        key = (dest << dest_shift) | (cell << row_bits) | there
        tiles.append(jnp.where(live, key, NONE))
        live_owner = jnp.where(live, owner, -1)
        for u in range(users):
            hot_owner[u].append((owner_iota == live_owner[u : u + 1, :]).astype(jnp.bfloat16))
            hot_slot[u].append((slot_iota == low[u : u + 1, :] + spare).astype(jnp.bfloat16))

    for u in range(users):
        counts = jnp.zeros((n, LANES), jnp.float32)
        for a, b in zip(hot_owner[u], hot_slot[u]):
            counts += lax.dot_general(
                a, b, (((1,), (1,)), ((), ())), preferred_element_type=jnp.float32
            )
        counts = counts.astype(jnp.int32)
        for d in range(n):
            out_ref[d, pl.ds(u, 1), :] = counts[d : d + 1, :]

    ends = []
    for d in range(n - 1):
        below = jnp.zeros((SUB, LANES), jnp.float32)
        for x in tiles:
            below += (x < ((d + 1) << dest_shift)).astype(jnp.float32)
        ends.append(jnp.sum(below).astype(jnp.int32))
    ends.append(live_total)

    empty = jnp.full((SUB, LANES), NONE, jnp.int32)
    tiles = sort_tiles(tiles + [empty] * ((1 << bits_for(len(tiles))) - len(tiles)))
    count = len(tiles)
    for t, x in enumerate(tiles):
        order[pl.ds(t * SUB, SUB), :] = x
    lines = [order[pl.ds(s, count, stride=SUB), :] for s in range(SUB)]
    straight[...] = jnp.concatenate(lines, axis=0).T

    at = (RUNS, LANES)
    run = lax.broadcasted_iota(jnp.int32, at, 0)
    lane = lax.broadcasted_iota(jnp.int32, at, 1)
    one_line = lax.broadcasted_iota(jnp.int32, (1, LANES), 1)
    start = jnp.int32(0)
    for d in range(n):
        count = ends[d] - start
        steps = lax.shift_right_logical(count + RUNS - 1, bits_for(RUNS))
        for j in range(RUNS):
            begin = start + j * steps
            off = begin & (LANES - 1)
            two = straight[pl.ds(lax.shift_right_logical(begin, bits_for(LANES)), 2), :]
            two = pltpu.roll(two, (LANES - off) & (LANES - 1), axis=1)
            runs[pl.ds(d * RUNS + j, 1), :] = jnp.where(one_line < LANES - off, two[:1], two[1:])
        mine = runs[pl.ds(d * RUNS, RUNS), :]
        valid = (lane < steps) & (run * steps + lane < count)
        there = mine & (2 * table_rows - 1)
        cell = lax.shift_right_logical(mine, row_bits) & ((1 << cell_bits) - 1)
        code = jnp.where(valid, (there << (cell_bits + 3)) | (cell << 1), dummy)
        cell = jnp.where(valid, cell, -1)
        following = pltpu.roll(cell, RUNS - 1, axis=0)
        same = (cell >= 0) & (cell == following) & (run < RUNS - 1)
        twice = jnp.max(jnp.where(same, 1.0, 0.0)).astype(jnp.int32)
        head = jnp.full((RUNS, LANES), steps | (twice << MODE), jnp.int32)
        beside = jnp.where(run < users, out_ref[d], head)
        out_ref[d] = jnp.where(lane < spare, code, beside)
        start = ends[d]


def add_kernel(
    n, head_at, cell_bits, request_ref, own_ref, other_ref, sums, narrow, table, codes, code_sems, sems
):
    stride = RUNS * LANES
    low = (4 << cell_bits) - 1
    rows = own_ref.shape[0]

    def read(s):
        at = pl.ds(pl.multiple_of(s * stride, stride), stride)
        slot = lax.rem(s, SLOTS)
        to = pl.ds(pl.multiple_of(slot * stride, stride), stride)
        return pltpu.make_async_copy(request_ref.at[at], codes.at[to], code_sems.at[slot])

    tables = [
        pltpu.make_async_copy(ref, narrow.at[pl.ds(part * rows, rows), :], sems.at[part])
        for part, ref in enumerate((own_ref, other_ref))
    ]
    for copy in tables:
        copy.start()

    def start_read(s, _):
        read(s).start()
        return 0

    lax.fori_loop(0, min(SLOTS, n), start_read, 0)

    def clear(i, _):
        sums[pl.ds(i * LANES, LANES), :] = jnp.zeros((LANES, LANES), jnp.float32)
        return 0

    lax.fori_loop(0, sums.shape[0] // LANES, clear, 0)

    def widen(i, _):
        x = narrow[pl.ds(i * LANES, LANES), :].astype(jnp.float32)
        table[pl.ds(i * 2 * LANES, LANES, stride=2), :] = x[:, :LANES]
        table[pl.ds(i * 2 * LANES + 1, LANES, stride=2), :] = x[:, LANES:]
        return 0

    blocks = rows // LANES
    for part, copy in enumerate(tables):
        copy.wait()
        lax.fori_loop(part * blocks, (part + 1) * blocks, widen, 0)

    def place(code):
        cell = pl.multiple_of(code & low, 2)
        row = pl.multiple_of(lax.shift_right_logical(code, cell_bits + 2), 2)
        return pl.ds(cell, 2), pl.ds(row, 2)

    def source(s, _):
        read(s).wait()
        begin = lax.rem(s, SLOTS) * stride
        head = codes[begin + head_at]
        steps = head & ((1 << MODE) - 1)

        @pl.when(head < (1 << MODE))
        def _():
            def step(at):
                for first in range(0, RUNS, PART):
                    new = []
                    for k in range(first, first + PART):
                        cell, row = place(codes[at + k * LANES])
                        new.append((cell, sums[cell, :] + table[row, :]))
                    for cell, value in new:
                        sums[cell, :] = value

            def two_steps(i, _):
                step(begin + 2 * i)
                step(begin + 2 * i + 1)
                return 0

            lax.fori_loop(0, lax.shift_right_logical(steps, 1), two_steps, 0)

            @pl.when((steps & 1) == 1)
            def _():
                step(begin + steps - 1)

        @pl.when(head >= (1 << MODE))
        def _():
            def single(i, _):
                for k in range(RUNS):
                    cell, row = place(codes[begin + i + k * LANES])
                    sums[cell, :] = sums[cell, :] + table[row, :]
                return 0

            lax.fori_loop(0, steps, single, 0)

        @pl.when(s + SLOTS < n)
        def _():
            read(s + SLOTS).start()

        return 0

    lax.fori_loop(0, n, source, 0)


def split_kernel(start, packet, sums, _, keep_ref, packet_ref, scales):
    rows = packet[1]
    keep_ref[...] = sums[pl.ds(start, rows), :]
    encode(packet, sums, start + rows, packet_ref, scales)


def split(sums, start, packet, after):
    rows = packet[1]
    return pl.pallas_call(
        functools.partial(split_kernel, start, packet),
        out_shape=[jax.ShapeDtypeStruct((rows, LANES), jnp.float32), packet_shape(packet)],
        in_specs=[
            pl.BlockSpec(memory_space=pltpu.VMEM),
            pl.BlockSpec(memory_space=pl.ANY),
        ],
        out_specs=[pl.BlockSpec(memory_space=pltpu.VMEM)] * 2,
        scratch_shapes=[pltpu.VMEM((scale_lines(rows), LANES), jnp.float32)],
        compiler_params=pltpu.CompilerParams(vmem_limit_bytes=16 * 1024 * 1024),
    )(sums, after)


def merge_kernel(arrived, packet, kept, came, _, keep_ref, packet_ref, total, scales):
    rows = packet[1]
    total[...] = kept[...]
    add_packet(arrived, came, total, scales)
    keep_ref[...] = total[pl.ds(0, rows), :]
    encode(packet, total, rows, packet_ref, scales)


def merge(kept, came, arrived, packet, after):
    lines = kept.shape[0]
    return pl.pallas_call(
        functools.partial(merge_kernel, arrived, packet),
        out_shape=[
            jax.ShapeDtypeStruct((lines // 2, LANES), jnp.float32),
            packet_shape(packet),
        ],
        in_specs=[pl.BlockSpec(memory_space=pltpu.VMEM)] * 2
        + [pl.BlockSpec(memory_space=pl.ANY)],
        out_specs=[pl.BlockSpec(memory_space=pltpu.VMEM)] * 2,
        scratch_shapes=[
            pltpu.VMEM((lines, LANES), jnp.float32),
            pltpu.VMEM((scale_lines(lines), LANES), jnp.float32),
        ],
        compiler_params=pltpu.CompilerParams(vmem_limit_bytes=16 * 1024 * 1024),
    )(kept, came, after)


def finish_kernel(arrived, count_ref, *refs):
    k = len(arrived)
    kept, came, out_ref = refs[:k], refs[k : 2 * k], refs[2 * k]
    totals, scales = refs[2 * k + 1 : -1], refs[-1]
    at = 0
    for packet, mine, other, total in zip(arrived, kept, came, totals):
        total[...] = mine[...]
        add_packet(packet, other, total, scales)
        rows = total.shape[0] // 2
        members = jnp.maximum(count_ref[pl.ds(at, rows), :], 1.0)
        for side in range(2):
            mean = total[pl.ds(side, rows, stride=2), :] / members
            out_ref[pl.ds(at, rows), pl.ds(side * LANES, LANES)] = mean
        at += rows


def finish(kept, came, arrived, counts):
    lines = sum(x.shape[0] for x in kept)
    return pl.pallas_call(
        functools.partial(finish_kernel, arrived),
        out_shape=jax.ShapeDtypeStruct((lines // 2, 2 * LANES), jnp.float32),
        in_specs=[pl.BlockSpec(memory_space=pltpu.VMEM)] * (1 + 2 * len(kept)),
        out_specs=pl.BlockSpec(memory_space=pltpu.VMEM),
        scratch_shapes=[pltpu.VMEM(x.shape, x.dtype) for x in kept]
        + [pltpu.VMEM((scale_lines(lines), LANES), jnp.float32)],
        compiler_params=pltpu.CompilerParams(vmem_limit_bytes=16 * 1024 * 1024),
    )(counts, *kept, *came)


def exchange(block, packet, n):
    return lax.ppermute(block, "tm", [(i, i ^ (2 << packet[0])) for i in range(n)])


def per_device(item_table, item_shard, item_row, cluster_id, lengths):
    n = lax.axis_size("tm")
    users, slab = item_row.shape[1:]
    rows, width = item_table.shape
    total = users * slab
    owned = K // n
    m = bits_for(n) - 1
    cells = users * K // 2
    cell_bits = bits_for(cells)
    row_bits = bits_for(2 * rows)
    dest_shift = cell_bits + row_bits
    most = -(-4 * total // n // RUNS)
    assert users * 2 <= RUNS and most <= LANES - owned
    chains = user_chains(users, m)
    dummy = cells * 2

    other = lax.ppermute(item_table, "tm", [(i, i ^ 1) for i in range(n)])
    buckets = pl.pallas_call(
        functools.partial(
            prepare_kernel, n, owned, rows, dest_shift, row_bits, cell_bits, dummy, chains,
        ),
        out_shape=jax.ShapeDtypeStruct((n, RUNS, LANES), jnp.int32),
        in_specs=[pl.BlockSpec(memory_space=pltpu.SMEM)]
        + [pl.BlockSpec(memory_space=pltpu.VMEM)] * 3,
        out_specs=pl.BlockSpec(memory_space=pltpu.VMEM),
        scratch_shapes=[
            pltpu.VMEM((LANES, LANES), jnp.int32),
            pltpu.VMEM((LANES, LANES), jnp.int32),
            pltpu.VMEM((n * RUNS, LANES), jnp.int32),
        ],
    )(
        lengths,
        item_shard.reshape(total // LANES, LANES),
        item_row.reshape(users, slab),
        cluster_id.reshape(users, slab),
    )
    requests = lax.all_to_all(buckets, "tm", split_axis=0, concat_axis=0, tiled=True)
    counts = jnp.sum(requests[:, :users, LANES - owned :], axis=0).astype(jnp.float32)
    counts = counts.reshape(users * owned, 1)

    requests = requests.reshape(-1)
    sums = pl.pallas_call(
        functools.partial(add_kernel, n, users * LANES + LANES - owned, cell_bits),
        out_shape=jax.ShapeDtypeStruct((cells * 2 + LANES, LANES), jnp.float32),
        in_specs=[
            pl.BlockSpec(memory_space=pltpu.VMEM),
            pl.BlockSpec(memory_space=pltpu.HBM),
            pl.BlockSpec(memory_space=pl.ANY),
        ],
        out_specs=pl.BlockSpec(memory_space=pltpu.VMEM),
        scratch_shapes=[
            pltpu.VMEM((rows * 2, width), jnp.bfloat16),
            pltpu.VMEM((rows * 4, LANES), jnp.float32),
            pltpu.SMEM((SLOTS * RUNS * LANES,), jnp.int32),
            pltpu.SemaphoreType.DMA((SLOTS,)),
            pltpu.SemaphoreType.DMA((2,)),
        ],
        compiler_params=pltpu.CompilerParams(vmem_limit_bytes=32 * 1024 * 1024),
    )(requests, item_table, other)

    after = requests
    kept, came, arrived = [], [], []
    for lo, size, order in chains:
        packet = packet_of((lo, size, order), 0, size * (K // 2))
        mine, sent = split(sums, lo * K, packet, after)
        after = mine
        kept.append(mine)
        came.append(exchange(sent, packet, n))
        arrived.append(packet)
    for stage in range(1, m):
        for c, chain in enumerate(chains):
            packet = packet_of(chain, stage, arrived[c][1] // 2)
            mine, sent = merge(kept[c], came[c], arrived[c], packet, after)
            after = mine
            kept[c], came[c], arrived[c] = mine, exchange(sent, packet, n), packet
    return finish(kept, came, arrived, counts).reshape(users, owned, width)


def solution(mesh):
    return jax.shard_map(
        per_device,
        mesh=mesh,
        in_specs=(
            P("tm", None),
            P("tm", ("groups", "users"), None, None),
            P("tm", ("groups", "users"), None),
            P("tm", ("groups", "users"), None),
            P(("groups", "users")),
        ),
        out_specs=P(("groups", "users"), "tm", None),
        check_vma=False,
    )
```

```python
import functools
import math

import jax
import jax.numpy as jnp
from jax import lax
from jax.experimental import pallas as pl
from jax.experimental.pallas import tpu as pltpu
from jax.sharding import PartitionSpec as P

K = 1024
LANES = 128
SUB = 8
RUNS = 16
PART = 8
SLOTS = 16
MODE = 16
NONE = 2**31 - 1
CODE_TOP = 32766.0
TALL = 64


def bits_for(count):
    return (count - 1).bit_length()


def user_chains(users, m):
    orders = [(0, 2, 1, 3), (2, 1, 0, 3), (1, 0, 3, 2)] if m == 4 else [tuple(range(m))] * 3
    sizes = [-(-users * 3 // 8), users * 3 // 8]
    sizes.append(users - sum(sizes))
    chains, lo = [], 0
    for size, order in zip(sizes, orders):
        if size:
            chains.append((lo, size, order))
        lo += size
    return chains


def packet_of(chain, stage, rows):
    order = chain[2]
    return (order[stage], rows, rows % TALL == 0) if stage < len(order) else None


def packet_shape(packet):
    _, lines, coded = packet
    if not coded:
        return jax.ShapeDtypeStruct((lines, LANES), jnp.float32)
    return jax.ShapeDtypeStruct((lines + scale_lines(lines), LANES), jnp.int16)


def scale_lines(lines):
    return -(-lines // TALL // 16) * 16


def scale_of(exponent):
    return jnp.exp(exponent * (math.log(2.0) / 64.0))


def several(count, block):
    def turn(t, _):
        for k in range(4):
            block(4 * t + k)
        return 0

    lax.fori_loop(0, count // 4, turn, 0)
    for i in range(count // 4 * 4, count):
        block(i)


def encode(packet, ref, start, out_ref, scales):
    _, rows, coded = packet
    if not coded:
        out_ref[...] = ref[pl.ds(start, rows), :]
        return

    def block(i):
        x = ref[pl.ds(start + i * TALL, TALL), :]
        top = jnp.maximum(jnp.max(jnp.abs(x), axis=0, keepdims=True), 1e-33)
        exponent = jnp.ceil(jnp.log(top) * (64.0 / math.log(2.0)))
        code = jnp.round(x * (CODE_TOP / scale_of(exponent)))
        code = code.astype(jnp.int32).astype(jnp.int16)
        out_ref[pl.ds(pl.multiple_of(i * TALL, TALL), TALL), :] = code
        scales[pl.ds(i, 1), :] = exponent

    several(rows // TALL, block)
    out_ref[pl.ds(rows, scale_lines(rows)), :] = (
        scales[pl.ds(0, scale_lines(rows)), :].astype(jnp.int32).astype(jnp.int16)
    )


def add_packet(packet, ref, total, scales):
    _, rows, coded = packet
    if not coded:
        total[...] = total[...] + ref[...]
        return
    scales[pl.ds(0, scale_lines(rows)), :] = ref[pl.ds(rows, scale_lines(rows)), :].astype(
        jnp.float32
    )

    def block(i):
        at = pl.ds(pl.multiple_of(i * TALL, TALL), TALL)
        scale = scale_of(scales[pl.ds(i, 1), :]) * (1.0 / CODE_TOP)
        total[at, :] = total[at, :] + ref[at, :].astype(jnp.float32) * scale

    several(rows // TALL, block)


def sort_tiles(tiles):
    count = len(tiles)
    tile_bits = bits_for(count)
    sub = lax.broadcasted_iota(jnp.int32, (SUB, LANES), 0)
    lane = lax.broadcasted_iota(jnp.int32, (SUB, LANES), 1)
    total_bits = tile_bits + 3 + 7

    def bit_mask(bit):
        if bit < tile_bits + 3:
            return ((sub >> (bit - tile_bits)) & 1) == 1
        return ((lane >> (bit - tile_bits - 3)) & 1) == 1

    masks = {b: bit_mask(b) for b in range(tile_bits, total_bits)}
    flips = {b: jnp.where(masks[b], -1, 0) for b in masks}

    def flip(t, phase):
        if phase >= total_bits:
            return 0
        if phase < tile_bits:
            return -1 if (t >> phase) & 1 else 0
        return flips[phase]

    for phase in range(1, total_bits + 1):
        changed = []
        for t in range(count):
            old = flip(t, phase - 1) if phase > 1 else 0
            new = flip(t, phase)
            if isinstance(old, int) and isinstance(new, int):
                turn = old ^ new
                changed.append(tiles[t] if turn == 0 else ~tiles[t])
            else:
                changed.append(tiles[t] ^ (old ^ new))
        tiles = changed
        for bit in reversed(range(phase)):
            if bit < tile_bits:
                step = 1 << bit
                tiles = list(tiles)
                for t in range(count):
                    if not t & step:
                        a, b = tiles[t], tiles[t | step]
                        tiles[t], tiles[t | step] = jnp.minimum(a, b), jnp.maximum(a, b)
                continue
            if bit < tile_bits + 3:
                axis, step, size = 0, 1 << (bit - tile_bits), SUB
            else:
                axis, step, size = 1, 1 << (bit - tile_bits - 3), LANES
            upper = masks[bit]
            moved = []
            for x in tiles:
                down = pltpu.roll(x, step, axis=axis)
                if 2 * step == size:
                    other = down
                else:
                    other = jnp.where(upper, down, pltpu.roll(x, size - step, axis=axis))
                moved.append(
                    jnp.where(upper, jnp.maximum(x, other), jnp.minimum(x, other))
                )
            tiles = moved
    return tiles


def prepare_kernel(
    n, owned, table_rows, dest_shift, row_bits, cell_bits, dummy, chains,
    lengths_ref, shard_ref, row_ref, cluster_ref, out_ref, order, straight, runs,
):
    users, slab = row_ref.shape
    sub = lax.broadcasted_iota(jnp.int32, (SUB, LANES), 0)
    lane = lax.broadcasted_iota(jnp.int32, (SUB, LANES), 1)
    me = lax.axis_index("tm")
    length = jnp.zeros((SUB, LANES), jnp.int32)
    live_total = jnp.int32(0)
    for u in range(users):
        length = jnp.where(sub == u, lengths_ref[u], length)
        live_total += jnp.clip(lengths_ref[u] - me * slab, 0, slab)
    length = length - me * slab

    base = jnp.zeros((SUB, LANES), jnp.int32)
    in_chain = jnp.zeros((SUB, LANES), jnp.int32)
    chain_size = jnp.zeros((SUB, LANES), jnp.int32)
    chain_at = []
    for lo, size, _ in chains:
        inside = (sub >= lo) & (sub < lo + size)
        base = jnp.where(inside, lo * (K // 2), base)
        in_chain = jnp.where(inside, sub - lo, in_chain)
        chain_size = jnp.where(inside, size, chain_size)
        chain_at.append(inside)

    owner_shift = bits_for(owned)
    tiles = []
    spare = LANES - owned
    hot_owner = [[] for _ in range(users)]
    hot_slot = [[] for _ in range(users)]
    owner_iota = lax.broadcasted_iota(jnp.int32, (n, LANES), 0)
    slot_iota = lax.broadcasted_iota(jnp.int32, (LANES, LANES), 0)
    for j in range(slab // LANES):
        at = pl.ds(j * LANES, LANES)
        row, cluster = row_ref[:, at], cluster_ref[:, at]
        shard = shard_ref[pl.ds(j, users, stride=slab // LANES), :]
        owner = lax.shift_right_logical(cluster, owner_shift)
        low = cluster & (owned - 1)
        live = lane + j * LANES < length
        dest = (shard & ~1) | (owner & 1)
        away = lax.shift_right_logical(owner ^ dest, 1)
        spread = jnp.zeros((SUB, LANES), jnp.int32)
        by_order = {}
        for (_, _, bits), inside in zip(chains, chain_at):
            if bits not in by_order:
                turned = jnp.zeros((SUB, LANES), jnp.int32)
                for bit in bits:
                    turned = turned * 2 + ((away >> bit) & 1)
                by_order[bits] = turned
            spread = jnp.where(inside, by_order[bits], spread)
        cell = base + ((spread * chain_size + in_chain) << owner_shift) + low
        there = ((shard ^ owner) & 1) * table_rows + row
        key = (dest << dest_shift) | (cell << row_bits) | there
        tiles.append(jnp.where(live, key, NONE))
        live_owner = jnp.where(live, owner, -1)
        for u in range(users):
            hot_owner[u].append((owner_iota == live_owner[u : u + 1, :]).astype(jnp.bfloat16))
            hot_slot[u].append((slot_iota == low[u : u + 1, :] + spare).astype(jnp.bfloat16))

    for u in range(users):
        counts = jnp.zeros((n, LANES), jnp.float32)
        for a, b in zip(hot_owner[u], hot_slot[u]):
            counts += lax.dot_general(
                a, b, (((1,), (1,)), ((), ())), preferred_element_type=jnp.float32
            )
        counts = counts.astype(jnp.int32)
        for d in range(n):
            out_ref[d, pl.ds(u, 1), :] = counts[d : d + 1, :]

    ends = []
    for d in range(n - 1):
        below = jnp.zeros((SUB, LANES), jnp.float32)
        for x in tiles:
            below += (x < ((d + 1) << dest_shift)).astype(jnp.float32)
        ends.append(jnp.sum(below).astype(jnp.int32))
    ends.append(live_total)

    empty = jnp.full((SUB, LANES), NONE, jnp.int32)
    tiles = sort_tiles(tiles + [empty] * ((1 << bits_for(len(tiles))) - len(tiles)))
    count = len(tiles)
    for t, x in enumerate(tiles):
        order[pl.ds(t * SUB, SUB), :] = x
    lines = [order[pl.ds(s, count, stride=SUB), :] for s in range(SUB)]
    straight[...] = jnp.concatenate(lines, axis=0).T

    at = (RUNS, LANES)
    run = lax.broadcasted_iota(jnp.int32, at, 0)
    lane = lax.broadcasted_iota(jnp.int32, at, 1)
    one_line = lax.broadcasted_iota(jnp.int32, (1, LANES), 1)
    start = jnp.int32(0)
    for d in range(n):
        count = ends[d] - start
        steps = lax.shift_right_logical(count + RUNS - 1, bits_for(RUNS))
        for j in range(RUNS):
            begin = start + j * steps
            off = begin & (LANES - 1)
            two = straight[pl.ds(lax.shift_right_logical(begin, bits_for(LANES)), 2), :]
            two = pltpu.roll(two, (LANES - off) & (LANES - 1), axis=1)
            runs[pl.ds(d * RUNS + j, 1), :] = jnp.where(one_line < LANES - off, two[:1], two[1:])
        mine = runs[pl.ds(d * RUNS, RUNS), :]
        valid = (lane < steps) & (run * steps + lane < count)
        there = mine & (2 * table_rows - 1)
        cell = lax.shift_right_logical(mine, row_bits) & ((1 << cell_bits) - 1)
        code = jnp.where(valid, (there << (cell_bits + 3)) | (cell << 1), dummy)
        cell = jnp.where(valid, cell, -1)
        following = pltpu.roll(cell, RUNS - 1, axis=0)
        same = (cell >= 0) & (cell == following) & (run < RUNS - 1)
        beyond = pltpu.roll(following, 1, axis=1)
        near = (cell >= 0) & (cell == beyond) & (run == PART - 1) & (lane > 0)
        mode = jnp.max(jnp.where(same, 2.0, jnp.where(near, 1.0, 0.0))).astype(jnp.int32)
        head = jnp.full((RUNS, LANES), steps | (mode << MODE), jnp.int32)
        beside = jnp.where(run < users, out_ref[d], head)
        out_ref[d] = jnp.where(lane < spare, code, beside)
        start = ends[d]


def add_kernel(
    n, head_at, cell_bits, request_ref, own_ref, other_ref, sums, narrow, table, codes, code_sems, sems
):
    stride = RUNS * LANES
    low = (4 << cell_bits) - 1
    rows = own_ref.shape[0]

    def read(s):
        at = pl.ds(pl.multiple_of(s * stride, stride), stride)
        slot = lax.rem(s, SLOTS)
        to = pl.ds(pl.multiple_of(slot * stride, stride), stride)
        return pltpu.make_async_copy(request_ref.at[at], codes.at[to], code_sems.at[slot])

    tables = [
        pltpu.make_async_copy(ref, narrow.at[pl.ds(part * rows, rows), :], sems.at[part])
        for part, ref in enumerate((own_ref, other_ref))
    ]
    for copy in tables:
        copy.start()

    def start_read(s, _):
        read(s).start()
        return 0

    lax.fori_loop(0, min(SLOTS, n), start_read, 0)

    def clear(i, _):
        sums[pl.ds(i * LANES, LANES), :] = jnp.zeros((LANES, LANES), jnp.float32)
        return 0

    lax.fori_loop(0, sums.shape[0] // LANES, clear, 0)

    def widen(i, _):
        x = narrow[pl.ds(i * LANES, LANES), :].astype(jnp.float32)
        table[pl.ds(i * 2 * LANES, LANES, stride=2), :] = x[:, :LANES]
        table[pl.ds(i * 2 * LANES + 1, LANES, stride=2), :] = x[:, LANES:]
        return 0

    blocks = rows // LANES
    for part, copy in enumerate(tables):
        copy.wait()
        lax.fori_loop(part * blocks, (part + 1) * blocks, widen, 0)

    def place(code):
        cell = pl.multiple_of(code & low, 2)
        row = pl.multiple_of(lax.shift_right_logical(code, cell_bits + 2), 2)
        return pl.ds(cell, 2), pl.ds(row, 2)

    def source(s, _):
        read(s).wait()
        begin = lax.rem(s, SLOTS) * stride
        head = codes[begin + head_at]
        steps = head & ((1 << MODE) - 1)

        def load(at, first):
            new = []
            for k in range(first, first + PART):
                cell, row = place(codes[at + k * LANES])
                new.append((cell, sums[cell, :] + table[row, :]))
            return new

        def store(new):
            for cell, value in new:
                sums[cell, :] = value

        mode = lax.shift_right_logical(head, MODE)
        turns = jnp.where(mode == 0, lax.shift_right_logical(steps, 2), 0)

        @pl.when(mode < 2)
        def _():
            def turn(i, _):
                waiting = []
                for k in range(4):
                    for first in (0, PART):
                        new = load(begin + 4 * i + k, first)
                        store(waiting)
                        waiting = new
                store(waiting)
                return 0

            lax.fori_loop(0, turns, turn, 0)

            def step(i, _):
                new = load(begin + i, 0)
                store(new)
                store(load(begin + i, PART))
                return 0

            lax.fori_loop(4 * turns, steps, step, 0)

        @pl.when(mode == 2)
        def _():
            def single(i, _):
                for k in range(RUNS):
                    cell, row = place(codes[begin + i + k * LANES])
                    sums[cell, :] = sums[cell, :] + table[row, :]
                return 0

            lax.fori_loop(0, steps, single, 0)

        @pl.when(s + SLOTS < n)
        def _():
            read(s + SLOTS).start()

        return 0

    lax.fori_loop(0, n, source, 0)


def split_kernel(start, packet, sums, _, keep_ref, packet_ref, scales):
    rows = packet[1]
    keep_ref[...] = sums[pl.ds(start, rows), :]
    encode(packet, sums, start + rows, packet_ref, scales)


def split(sums, start, packet, after):
    rows = packet[1]
    return pl.pallas_call(
        functools.partial(split_kernel, start, packet),
        out_shape=[jax.ShapeDtypeStruct((rows, LANES), jnp.float32), packet_shape(packet)],
        in_specs=[
            pl.BlockSpec(memory_space=pltpu.VMEM),
            pl.BlockSpec(memory_space=pl.ANY),
        ],
        out_specs=[pl.BlockSpec(memory_space=pltpu.VMEM)] * 2,
        scratch_shapes=[pltpu.VMEM((scale_lines(rows), LANES), jnp.float32)],
        compiler_params=pltpu.CompilerParams(vmem_limit_bytes=16 * 1024 * 1024),
    )(sums, after)


def merge_kernel(arrived, packet, kept, came, _, keep_ref, packet_ref, total, scales):
    rows = packet[1]
    total[...] = kept[...]
    add_packet(arrived, came, total, scales)
    keep_ref[...] = total[pl.ds(0, rows), :]
    encode(packet, total, rows, packet_ref, scales)


def merge(kept, came, arrived, packet, after):
    lines = kept.shape[0]
    return pl.pallas_call(
        functools.partial(merge_kernel, arrived, packet),
        out_shape=[
            jax.ShapeDtypeStruct((lines // 2, LANES), jnp.float32),
            packet_shape(packet),
        ],
        in_specs=[pl.BlockSpec(memory_space=pltpu.VMEM)] * 2
        + [pl.BlockSpec(memory_space=pl.ANY)],
        out_specs=[pl.BlockSpec(memory_space=pltpu.VMEM)] * 2,
        scratch_shapes=[
            pltpu.VMEM((lines, LANES), jnp.float32),
            pltpu.VMEM((scale_lines(lines), LANES), jnp.float32),
        ],
        compiler_params=pltpu.CompilerParams(vmem_limit_bytes=16 * 1024 * 1024),
    )(kept, came, after)


def finish_kernel(arrived, count_ref, *refs):
    k = len(arrived)
    kept, came, out_ref = refs[:k], refs[k : 2 * k], refs[2 * k]
    totals, scales = refs[2 * k + 1 : -1], refs[-1]
    at = 0
    for packet, mine, other, total in zip(arrived, kept, came, totals):
        total[...] = mine[...]
        add_packet(packet, other, total, scales)
        rows = total.shape[0] // 2
        members = jnp.maximum(count_ref[pl.ds(at, rows), :], 1.0)
        for side in range(2):
            mean = total[pl.ds(side, rows, stride=2), :] / members
            out_ref[pl.ds(at, rows), pl.ds(side * LANES, LANES)] = mean
        at += rows


def finish(kept, came, arrived, counts):
    lines = sum(x.shape[0] for x in kept)
    return pl.pallas_call(
        functools.partial(finish_kernel, arrived),
        out_shape=jax.ShapeDtypeStruct((lines // 2, 2 * LANES), jnp.float32),
        in_specs=[pl.BlockSpec(memory_space=pltpu.VMEM)] * (1 + 2 * len(kept)),
        out_specs=pl.BlockSpec(memory_space=pltpu.VMEM),
        scratch_shapes=[pltpu.VMEM(x.shape, x.dtype) for x in kept]
        + [pltpu.VMEM((scale_lines(lines), LANES), jnp.float32)],
        compiler_params=pltpu.CompilerParams(vmem_limit_bytes=16 * 1024 * 1024),
    )(counts, *kept, *came)


def exchange(block, packet, n):
    return lax.ppermute(block, "tm", [(i, i ^ (2 << packet[0])) for i in range(n)])


def per_device(item_table, item_shard, item_row, cluster_id, lengths):
    n = lax.axis_size("tm")
    users, slab = item_row.shape[1:]
    rows, width = item_table.shape
    total = users * slab
    owned = K // n
    m = bits_for(n) - 1
    cells = users * K // 2
    cell_bits = bits_for(cells)
    row_bits = bits_for(2 * rows)
    dest_shift = cell_bits + row_bits
    most = -(-4 * total // n // RUNS)
    assert users * 2 <= RUNS and most <= LANES - owned
    chains = user_chains(users, m)
    dummy = cells * 2

    other = lax.ppermute(item_table, "tm", [(i, i ^ 1) for i in range(n)])
    buckets = pl.pallas_call(
        functools.partial(
            prepare_kernel, n, owned, rows, dest_shift, row_bits, cell_bits, dummy, chains,
        ),
        out_shape=jax.ShapeDtypeStruct((n, RUNS, LANES), jnp.int32),
        in_specs=[pl.BlockSpec(memory_space=pltpu.SMEM)]
        + [pl.BlockSpec(memory_space=pltpu.VMEM)] * 3,
        out_specs=pl.BlockSpec(memory_space=pltpu.VMEM),
        scratch_shapes=[
            pltpu.VMEM((LANES, LANES), jnp.int32),
            pltpu.VMEM((LANES, LANES), jnp.int32),
            pltpu.VMEM((n * RUNS, LANES), jnp.int32),
        ],
    )(
        lengths,
        item_shard.reshape(total // LANES, LANES),
        item_row.reshape(users, slab),
        cluster_id.reshape(users, slab),
    )
    requests = lax.all_to_all(buckets, "tm", split_axis=0, concat_axis=0, tiled=True)
    counts = jnp.sum(requests[:, :users, LANES - owned :], axis=0).astype(jnp.float32)
    counts = counts.reshape(users * owned, 1)

    requests = requests.reshape(-1)
    sums = pl.pallas_call(
        functools.partial(add_kernel, n, users * LANES + LANES - owned, cell_bits),
        out_shape=jax.ShapeDtypeStruct((cells * 2 + LANES, LANES), jnp.float32),
        in_specs=[
            pl.BlockSpec(memory_space=pltpu.VMEM),
            pl.BlockSpec(memory_space=pltpu.HBM),
            pl.BlockSpec(memory_space=pl.ANY),
        ],
        out_specs=pl.BlockSpec(memory_space=pltpu.VMEM),
        scratch_shapes=[
            pltpu.VMEM((rows * 2, width), jnp.bfloat16),
            pltpu.VMEM((rows * 4, LANES), jnp.float32),
            pltpu.SMEM((SLOTS * RUNS * LANES,), jnp.int32),
            pltpu.SemaphoreType.DMA((SLOTS,)),
            pltpu.SemaphoreType.DMA((2,)),
        ],
        compiler_params=pltpu.CompilerParams(vmem_limit_bytes=32 * 1024 * 1024),
    )(requests, item_table, other)

    after = requests
    kept, came, arrived = [], [], []
    for lo, size, order in chains:
        packet = packet_of((lo, size, order), 0, size * (K // 2))
        mine, sent = split(sums, lo * K, packet, after)
        after = mine
        kept.append(mine)
        came.append(exchange(sent, packet, n))
        arrived.append(packet)
    for stage in range(1, m):
        for c, chain in enumerate(chains):
            packet = packet_of(chain, stage, arrived[c][1] // 2)
            mine, sent = merge(kept[c], came[c], arrived[c], packet, after)
            after = mine
            kept[c], came[c], arrived[c] = mine, exchange(sent, packet, n), packet
    return finish(kept, came, arrived, counts).reshape(users, owned, width)


def solution(mesh):
    return jax.shard_map(
        per_device,
        mesh=mesh,
        in_specs=(
            P("tm", None),
            P("tm", ("groups", "users"), None, None),
            P("tm", ("groups", "users"), None),
            P("tm", ("groups", "users"), None),
            P(("groups", "users")),
        ),
        out_specs=P(("groups", "users"), "tm", None),
        check_vma=False,
    )
```

```python
import functools
import math

import jax
import jax.numpy as jnp
from jax import lax
from jax.experimental import pallas as pl
from jax.experimental.pallas import tpu as pltpu
from jax.sharding import PartitionSpec as P

K = 1024
LANES = 128
SUB = 8
RUNS = 16
PART = 4
SLOTS = 16
MODE = 16
NONE = 2**31 - 1
CODE_TOP = 32766.0
TALL = 64


def bits_for(count):
    return (count - 1).bit_length()


def user_chains(users, m):
    orders = [(0, 2, 1, 3), (2, 1, 0, 3), (1, 0, 3, 2)] if m == 4 else [tuple(range(m))] * 3
    sizes = [-(-users * 3 // 8), users * 3 // 8]
    sizes.append(users - sum(sizes))
    chains, lo = [], 0
    for size, order in zip(sizes, orders):
        if size:
            chains.append((lo, size, order))
        lo += size
    return chains


def packet_of(chain, stage, rows):
    order = chain[2]
    return (order[stage], rows, rows % TALL == 0) if stage < len(order) else None


def packet_shape(packet):
    _, lines, coded = packet
    if not coded:
        return jax.ShapeDtypeStruct((lines, LANES), jnp.float32)
    return jax.ShapeDtypeStruct((lines + scale_lines(lines), LANES), jnp.int16)


def scale_lines(lines):
    return -(-lines // TALL // 16) * 16


def scale_of(exponent):
    return jnp.exp(exponent * (math.log(2.0) / 64.0))


def several(count, block):
    def turn(t, _):
        for k in range(4):
            block(4 * t + k)
        return 0

    lax.fori_loop(0, count // 4, turn, 0)
    for i in range(count // 4 * 4, count):
        block(i)


def encode(packet, ref, start, out_ref, scales):
    _, rows, coded = packet
    if not coded:
        out_ref[...] = ref[pl.ds(start, rows), :]
        return

    def block(i):
        x = ref[pl.ds(start + i * TALL, TALL), :]
        top = jnp.maximum(jnp.max(jnp.abs(x), axis=0, keepdims=True), 1e-33)
        exponent = jnp.ceil(jnp.log(top) * (64.0 / math.log(2.0)))
        code = jnp.round(x * (CODE_TOP / scale_of(exponent)))
        code = code.astype(jnp.int32).astype(jnp.int16)
        out_ref[pl.ds(pl.multiple_of(i * TALL, TALL), TALL), :] = code
        scales[pl.ds(i, 1), :] = exponent

    several(rows // TALL, block)
    out_ref[pl.ds(rows, scale_lines(rows)), :] = (
        scales[pl.ds(0, scale_lines(rows)), :].astype(jnp.int32).astype(jnp.int16)
    )


def add_packet(packet, ref, total, scales):
    _, rows, coded = packet
    if not coded:
        total[...] = total[...] + ref[...]
        return
    scales[pl.ds(0, scale_lines(rows)), :] = ref[pl.ds(rows, scale_lines(rows)), :].astype(
        jnp.float32
    )

    def block(i):
        at = pl.ds(pl.multiple_of(i * TALL, TALL), TALL)
        scale = scale_of(scales[pl.ds(i, 1), :]) * (1.0 / CODE_TOP)
        total[at, :] = total[at, :] + ref[at, :].astype(jnp.float32) * scale

    several(rows // TALL, block)


def sort_tiles(tiles):
    count = len(tiles)
    tile_bits = bits_for(count)
    sub = lax.broadcasted_iota(jnp.int32, (SUB, LANES), 0)
    lane = lax.broadcasted_iota(jnp.int32, (SUB, LANES), 1)
    total_bits = tile_bits + 3 + 7

    def bit_mask(bit):
        if bit < tile_bits + 3:
            return ((sub >> (bit - tile_bits)) & 1) == 1
        return ((lane >> (bit - tile_bits - 3)) & 1) == 1

    masks = {b: bit_mask(b) for b in range(tile_bits, total_bits)}
    flips = {b: jnp.where(masks[b], -1, 0) for b in masks}

    def flip(t, phase):
        if phase >= total_bits:
            return 0
        if phase < tile_bits:
            return -1 if (t >> phase) & 1 else 0
        return flips[phase]

    for phase in range(1, total_bits + 1):
        changed = []
        for t in range(count):
            old = flip(t, phase - 1) if phase > 1 else 0
            new = flip(t, phase)
            if isinstance(old, int) and isinstance(new, int):
                turn = old ^ new
                changed.append(tiles[t] if turn == 0 else ~tiles[t])
            else:
                changed.append(tiles[t] ^ (old ^ new))
        tiles = changed
        for bit in reversed(range(phase)):
            if bit < tile_bits:
                step = 1 << bit
                tiles = list(tiles)
                for t in range(count):
                    if not t & step:
                        a, b = tiles[t], tiles[t | step]
                        tiles[t], tiles[t | step] = jnp.minimum(a, b), jnp.maximum(a, b)
                continue
            if bit < tile_bits + 3:
                axis, step, size = 0, 1 << (bit - tile_bits), SUB
            else:
                axis, step, size = 1, 1 << (bit - tile_bits - 3), LANES
            upper = masks[bit]
            moved = []
            for x in tiles:
                down = pltpu.roll(x, step, axis=axis)
                if 2 * step == size:
                    other = down
                else:
                    other = jnp.where(upper, down, pltpu.roll(x, size - step, axis=axis))
                moved.append(
                    jnp.where(upper, jnp.maximum(x, other), jnp.minimum(x, other))
                )
            tiles = moved
    return tiles


def prepare_kernel(
    n, owned, table_rows, dest_shift, row_bits, cell_bits, dummy, chains,
    lengths_ref, shard_ref, row_ref, cluster_ref, out_ref, order, straight, runs,
):
    users, slab = row_ref.shape
    sub = lax.broadcasted_iota(jnp.int32, (SUB, LANES), 0)
    lane = lax.broadcasted_iota(jnp.int32, (SUB, LANES), 1)
    me = lax.axis_index("tm")
    length = jnp.zeros((SUB, LANES), jnp.int32)
    live_total = jnp.int32(0)
    for u in range(users):
        length = jnp.where(sub == u, lengths_ref[u], length)
        live_total += jnp.clip(lengths_ref[u] - me * slab, 0, slab)
    length = length - me * slab

    base = jnp.zeros((SUB, LANES), jnp.int32)
    in_chain = jnp.zeros((SUB, LANES), jnp.int32)
    chain_size = jnp.zeros((SUB, LANES), jnp.int32)
    chain_at = []
    for lo, size, _ in chains:
        inside = (sub >= lo) & (sub < lo + size)
        base = jnp.where(inside, lo * (K // 2), base)
        in_chain = jnp.where(inside, sub - lo, in_chain)
        chain_size = jnp.where(inside, size, chain_size)
        chain_at.append(inside)

    owner_shift = bits_for(owned)
    tiles = []
    spare = LANES - owned
    hot_owner = [[] for _ in range(users)]
    hot_slot = [[] for _ in range(users)]
    owner_iota = lax.broadcasted_iota(jnp.int32, (n, LANES), 0)
    slot_iota = lax.broadcasted_iota(jnp.int32, (LANES, LANES), 0)
    for j in range(slab // LANES):
        at = pl.ds(j * LANES, LANES)
        row, cluster = row_ref[:, at], cluster_ref[:, at]
        shard = shard_ref[pl.ds(j, users, stride=slab // LANES), :]
        owner = lax.shift_right_logical(cluster, owner_shift)
        low = cluster & (owned - 1)
        live = lane + j * LANES < length
        dest = (shard & ~1) | (owner & 1)
        away = lax.shift_right_logical(owner ^ dest, 1)
        spread = jnp.zeros((SUB, LANES), jnp.int32)
        by_order = {}
        for (_, _, bits), inside in zip(chains, chain_at):
            if bits not in by_order:
                turned = jnp.zeros((SUB, LANES), jnp.int32)
                for bit in bits:
                    turned = turned * 2 + ((away >> bit) & 1)
                by_order[bits] = turned
            spread = jnp.where(inside, by_order[bits], spread)
        cell = base + ((spread * chain_size + in_chain) << owner_shift) + low
        there = ((shard ^ owner) & 1) * table_rows + row
        key = (dest << dest_shift) | (cell << row_bits) | there
        tiles.append(jnp.where(live, key, NONE))
        live_owner = jnp.where(live, owner, -1)
        for u in range(users):
            hot_owner[u].append((owner_iota == live_owner[u : u + 1, :]).astype(jnp.bfloat16))
            hot_slot[u].append((slot_iota == low[u : u + 1, :] + spare).astype(jnp.bfloat16))

    for u in range(users):
        counts = jnp.zeros((n, LANES), jnp.float32)
        for a, b in zip(hot_owner[u], hot_slot[u]):
            counts += lax.dot_general(
                a, b, (((1,), (1,)), ((), ())), preferred_element_type=jnp.float32
            )
        counts = counts.astype(jnp.int32)
        for d in range(n):
            out_ref[d, pl.ds(u, 1), :] = counts[d : d + 1, :]

    ends = []
    for d in range(n - 1):
        below = jnp.zeros((SUB, LANES), jnp.float32)
        for x in tiles:
            below += (x < ((d + 1) << dest_shift)).astype(jnp.float32)
        ends.append(jnp.sum(below).astype(jnp.int32))
    ends.append(live_total)

    empty = jnp.full((SUB, LANES), NONE, jnp.int32)
    tiles = sort_tiles(tiles + [empty] * ((1 << bits_for(len(tiles))) - len(tiles)))
    count = len(tiles)
    for t, x in enumerate(tiles):
        order[pl.ds(t * SUB, SUB), :] = x
    lines = [order[pl.ds(s, count, stride=SUB), :] for s in range(SUB)]
    straight[...] = jnp.concatenate(lines, axis=0).T

    at = (RUNS, LANES)
    run = lax.broadcasted_iota(jnp.int32, at, 0)
    lane = lax.broadcasted_iota(jnp.int32, at, 1)
    one_line = lax.broadcasted_iota(jnp.int32, (1, LANES), 1)
    start = jnp.int32(0)
    for d in range(n):
        count = ends[d] - start
        steps = lax.shift_right_logical(count + RUNS - 1, bits_for(RUNS))
        for j in range(RUNS):
            begin = start + j * steps
            off = begin & (LANES - 1)
            two = straight[pl.ds(lax.shift_right_logical(begin, bits_for(LANES)), 2), :]
            two = pltpu.roll(two, (LANES - off) & (LANES - 1), axis=1)
            runs[pl.ds(d * RUNS + j, 1), :] = jnp.where(one_line < LANES - off, two[:1], two[1:])
        mine = runs[pl.ds(d * RUNS, RUNS), :]
        valid = (lane < steps) & (run * steps + lane < count)
        there = mine & (2 * table_rows - 1)
        cell = lax.shift_right_logical(mine, row_bits) & ((1 << cell_bits) - 1)
        code = jnp.where(valid, (there << (cell_bits + 3)) | (cell << 1), dummy)
        cell = jnp.where(valid, cell, -1)
        following = pltpu.roll(cell, RUNS - 1, axis=0)
        same = (cell >= 0) & (cell == following) & (run < RUNS - 1)
        beyond = pltpu.roll(following, 1, axis=1)
        near = (cell >= 0) & (cell == beyond) & (run == PART - 1) & (lane > 0)
        mode = jnp.max(jnp.where(same, 2.0, jnp.where(near, 1.0, 0.0))).astype(jnp.int32)
        head = jnp.full((RUNS, LANES), steps | (mode << MODE), jnp.int32)
        beside = jnp.where(run < users, out_ref[d], head)
        out_ref[d] = jnp.where(lane < spare, code, beside)
        start = ends[d]


def add_kernel(
    n, head_at, cell_bits, request_ref, own_ref, other_ref, sums, narrow, table, codes, code_sems, sems
):
    stride = RUNS * LANES
    low = (4 << cell_bits) - 1
    rows = own_ref.shape[0]

    def read(s):
        at = pl.ds(pl.multiple_of(s * stride, stride), stride)
        slot = lax.rem(s, SLOTS)
        to = pl.ds(pl.multiple_of(slot * stride, stride), stride)
        return pltpu.make_async_copy(request_ref.at[at], codes.at[to], code_sems.at[slot])

    tables = [
        pltpu.make_async_copy(ref, narrow.at[pl.ds(part * rows, rows), :], sems.at[part])
        for part, ref in enumerate((own_ref, other_ref))
    ]
    for copy in tables:
        copy.start()

    def start_read(s, _):
        read(s).start()
        return 0

    lax.fori_loop(0, min(SLOTS, n), start_read, 0)

    def clear(i, _):
        sums[pl.ds(i * LANES, LANES), :] = jnp.zeros((LANES, LANES), jnp.float32)
        return 0

    lax.fori_loop(0, sums.shape[0] // LANES, clear, 0)

    def widen(i, _):
        x = narrow[pl.ds(i * LANES, LANES), :].astype(jnp.float32)
        table[pl.ds(i * 2 * LANES, LANES, stride=2), :] = x[:, :LANES]
        table[pl.ds(i * 2 * LANES + 1, LANES, stride=2), :] = x[:, LANES:]
        return 0

    blocks = rows // LANES
    for part, copy in enumerate(tables):
        copy.wait()
        lax.fori_loop(part * blocks, (part + 1) * blocks, widen, 0)

    def place(code):
        cell = pl.multiple_of(code & low, 2)
        row = pl.multiple_of(lax.shift_right_logical(code, cell_bits + 2), 2)
        return pl.ds(cell, 2), pl.ds(row, 2)

    def source(s, _):
        read(s).wait()
        begin = lax.rem(s, SLOTS) * stride
        head = codes[begin + head_at]
        steps = head & ((1 << MODE) - 1)

        def load(at, first):
            new = []
            for k in range(first, first + PART):
                cell, row = place(codes[at + k * LANES])
                new.append((cell, sums[cell, :] + table[row, :]))
            return new

        def store(new):
            for cell, value in new:
                sums[cell, :] = value

        mode = lax.shift_right_logical(head, MODE)
        turns = jnp.where(mode == 0, lax.shift_right_logical(steps, 2), 0)

        @pl.when(mode < 2)
        def _():
            def overlap(ats):
                waiting = []
                for at in ats:
                    for first in range(0, RUNS, PART):
                        new = load(at, first)
                        store(waiting)
                        waiting = new
                store(waiting)

            def turn(i, _):
                overlap([begin + 4 * i + k for k in range(4)])
                return 0

            lax.fori_loop(0, turns, turn, 0)

            def step(i, _):
                overlap([begin + i])
                return 0

            lax.fori_loop(4 * turns, steps, step, 0)

        @pl.when(mode == 2)
        def _():
            def single(i, _):
                for k in range(RUNS):
                    cell, row = place(codes[begin + i + k * LANES])
                    sums[cell, :] = sums[cell, :] + table[row, :]
                return 0

            lax.fori_loop(0, steps, single, 0)

        @pl.when(s + SLOTS < n)
        def _():
            read(s + SLOTS).start()

        return 0

    lax.fori_loop(0, n, source, 0)


def split_kernel(start, packet, sums, _, keep_ref, packet_ref, scales):
    rows = packet[1]
    keep_ref[...] = sums[pl.ds(start, rows), :]
    encode(packet, sums, start + rows, packet_ref, scales)


def split(sums, start, packet, after):
    rows = packet[1]
    return pl.pallas_call(
        functools.partial(split_kernel, start, packet),
        out_shape=[jax.ShapeDtypeStruct((rows, LANES), jnp.float32), packet_shape(packet)],
        in_specs=[
            pl.BlockSpec(memory_space=pltpu.VMEM),
            pl.BlockSpec(memory_space=pl.ANY),
        ],
        out_specs=[pl.BlockSpec(memory_space=pltpu.VMEM)] * 2,
        scratch_shapes=[pltpu.VMEM((scale_lines(rows), LANES), jnp.float32)],
        compiler_params=pltpu.CompilerParams(vmem_limit_bytes=16 * 1024 * 1024),
    )(sums, after)


def merge_kernel(arrived, packet, kept, came, _, keep_ref, packet_ref, total, scales):
    rows = packet[1]
    total[...] = kept[...]
    add_packet(arrived, came, total, scales)
    keep_ref[...] = total[pl.ds(0, rows), :]
    encode(packet, total, rows, packet_ref, scales)


def merge(kept, came, arrived, packet, after):
    lines = kept.shape[0]
    return pl.pallas_call(
        functools.partial(merge_kernel, arrived, packet),
        out_shape=[
            jax.ShapeDtypeStruct((lines // 2, LANES), jnp.float32),
            packet_shape(packet),
        ],
        in_specs=[pl.BlockSpec(memory_space=pltpu.VMEM)] * 2
        + [pl.BlockSpec(memory_space=pl.ANY)],
        out_specs=[pl.BlockSpec(memory_space=pltpu.VMEM)] * 2,
        scratch_shapes=[
            pltpu.VMEM((lines, LANES), jnp.float32),
            pltpu.VMEM((scale_lines(lines), LANES), jnp.float32),
        ],
        compiler_params=pltpu.CompilerParams(vmem_limit_bytes=16 * 1024 * 1024),
    )(kept, came, after)


def finish_kernel(arrived, count_ref, *refs):
    k = len(arrived)
    kept, came, out_ref = refs[:k], refs[k : 2 * k], refs[2 * k]
    totals, scales = refs[2 * k + 1 : -1], refs[-1]
    at = 0
    for packet, mine, other, total in zip(arrived, kept, came, totals):
        total[...] = mine[...]
        add_packet(packet, other, total, scales)
        rows = total.shape[0] // 2
        members = jnp.maximum(count_ref[pl.ds(at, rows), :], 1.0)
        for side in range(2):
            mean = total[pl.ds(side, rows, stride=2), :] / members
            out_ref[pl.ds(at, rows), pl.ds(side * LANES, LANES)] = mean
        at += rows


def finish(kept, came, arrived, counts):
    lines = sum(x.shape[0] for x in kept)
    return pl.pallas_call(
        functools.partial(finish_kernel, arrived),
        out_shape=jax.ShapeDtypeStruct((lines // 2, 2 * LANES), jnp.float32),
        in_specs=[pl.BlockSpec(memory_space=pltpu.VMEM)] * (1 + 2 * len(kept)),
        out_specs=pl.BlockSpec(memory_space=pltpu.VMEM),
        scratch_shapes=[pltpu.VMEM(x.shape, x.dtype) for x in kept]
        + [pltpu.VMEM((scale_lines(lines), LANES), jnp.float32)],
        compiler_params=pltpu.CompilerParams(vmem_limit_bytes=16 * 1024 * 1024),
    )(counts, *kept, *came)


def exchange(block, packet, n):
    return lax.ppermute(block, "tm", [(i, i ^ (2 << packet[0])) for i in range(n)])


def per_device(item_table, item_shard, item_row, cluster_id, lengths):
    n = lax.axis_size("tm")
    users, slab = item_row.shape[1:]
    rows, width = item_table.shape
    total = users * slab
    owned = K // n
    m = bits_for(n) - 1
    cells = users * K // 2
    cell_bits = bits_for(cells)
    row_bits = bits_for(2 * rows)
    dest_shift = cell_bits + row_bits
    most = -(-4 * total // n // RUNS)
    assert users * 2 <= RUNS and most <= LANES - owned
    chains = user_chains(users, m)
    dummy = cells * 2

    other = lax.ppermute(item_table, "tm", [(i, i ^ 1) for i in range(n)])
    buckets = pl.pallas_call(
        functools.partial(
            prepare_kernel, n, owned, rows, dest_shift, row_bits, cell_bits, dummy, chains,
        ),
        out_shape=jax.ShapeDtypeStruct((n, RUNS, LANES), jnp.int32),
        in_specs=[pl.BlockSpec(memory_space=pltpu.SMEM)]
        + [pl.BlockSpec(memory_space=pltpu.VMEM)] * 3,
        out_specs=pl.BlockSpec(memory_space=pltpu.VMEM),
        scratch_shapes=[
            pltpu.VMEM((LANES, LANES), jnp.int32),
            pltpu.VMEM((LANES, LANES), jnp.int32),
            pltpu.VMEM((n * RUNS, LANES), jnp.int32),
        ],
    )(
        lengths,
        item_shard.reshape(total // LANES, LANES),
        item_row.reshape(users, slab),
        cluster_id.reshape(users, slab),
    )
    requests = lax.all_to_all(buckets, "tm", split_axis=0, concat_axis=0, tiled=True)
    counts = jnp.sum(requests[:, :users, LANES - owned :], axis=0).astype(jnp.float32)
    counts = counts.reshape(users * owned, 1)

    requests = requests.reshape(-1)
    sums = pl.pallas_call(
        functools.partial(add_kernel, n, users * LANES + LANES - owned, cell_bits),
        out_shape=jax.ShapeDtypeStruct((cells * 2 + LANES, LANES), jnp.float32),
        in_specs=[
            pl.BlockSpec(memory_space=pltpu.VMEM),
            pl.BlockSpec(memory_space=pltpu.HBM),
            pl.BlockSpec(memory_space=pl.ANY),
        ],
        out_specs=pl.BlockSpec(memory_space=pltpu.VMEM),
        scratch_shapes=[
            pltpu.VMEM((rows * 2, width), jnp.bfloat16),
            pltpu.VMEM((rows * 4, LANES), jnp.float32),
            pltpu.SMEM((SLOTS * RUNS * LANES,), jnp.int32),
            pltpu.SemaphoreType.DMA((SLOTS,)),
            pltpu.SemaphoreType.DMA((2,)),
        ],
        compiler_params=pltpu.CompilerParams(vmem_limit_bytes=32 * 1024 * 1024),
    )(requests, item_table, other)

    after = requests
    kept, came, arrived = [], [], []
    for lo, size, order in chains:
        packet = packet_of((lo, size, order), 0, size * (K // 2))
        mine, sent = split(sums, lo * K, packet, after)
        after = mine
        kept.append(mine)
        came.append(exchange(sent, packet, n))
        arrived.append(packet)
    for stage in range(1, m):
        for c, chain in enumerate(chains):
            packet = packet_of(chain, stage, arrived[c][1] // 2)
            mine, sent = merge(kept[c], came[c], arrived[c], packet, after)
            after = mine
            kept[c], came[c], arrived[c] = mine, exchange(sent, packet, n), packet
    return finish(kept, came, arrived, counts).reshape(users, owned, width)


def solution(mesh):
    return jax.shard_map(
        per_device,
        mesh=mesh,
        in_specs=(
            P("tm", None),
            P("tm", ("groups", "users"), None, None),
            P("tm", ("groups", "users"), None),
            P("tm", ("groups", "users"), None),
            P(("groups", "users")),
        ),
        out_specs=P(("groups", "users"), "tm", None),
        check_vma=False,
    )
```

```python
import functools
import math

import jax
import jax.numpy as jnp
from jax import lax
from jax.experimental import pallas as pl
from jax.experimental.pallas import tpu as pltpu
from jax.sharding import PartitionSpec as P

K = 1024
LANES = 128
SUB = 8
RUNS = 16
PART = 8
SLOTS = 16
MODE = 16
NONE = 2**31 - 1
CODE_TOP = 32766.0
TALL = 64


def bits_for(count):
    return (count - 1).bit_length()


def user_chains(users, m):
    orders = [(0, 2, 1, 3), (2, 1, 0, 3), (1, 0, 3, 2)] if m == 4 else [tuple(range(m))] * 3
    sizes = [-(-users * 3 // 8), users * 3 // 8]
    sizes.append(users - sum(sizes))
    chains, lo = [], 0
    for size, order in zip(sizes, orders):
        if size:
            chains.append((lo, size, order))
        lo += size
    return chains


def packet_of(chain, stage, rows):
    order = chain[2]
    return (order[stage], rows, rows % TALL == 0) if stage < len(order) else None


def packet_shape(packet):
    _, lines, coded = packet
    if not coded:
        return jax.ShapeDtypeStruct((lines, LANES), jnp.float32)
    return jax.ShapeDtypeStruct((lines + scale_lines(lines), LANES), jnp.int16)


def scale_lines(lines):
    return -(-lines // TALL // 16) * 16


def scale_of(exponent):
    return jnp.exp(exponent * (math.log(2.0) / 64.0))


def several(count, block):
    def turn(t, _):
        for k in range(4):
            block(4 * t + k)
        return 0

    lax.fori_loop(0, count // 4, turn, 0)
    for i in range(count // 4 * 4, count):
        block(i)


def encode(packet, ref, start, out_ref, scales):
    _, rows, coded = packet
    if not coded:
        out_ref[...] = ref[pl.ds(start, rows), :]
        return

    def block(i):
        x = ref[pl.ds(start + i * TALL, TALL), :]
        top = jnp.maximum(jnp.max(jnp.abs(x), axis=0, keepdims=True), 1e-33)
        exponent = jnp.ceil(jnp.log(top) * (64.0 / math.log(2.0)))
        code = jnp.round(x * (CODE_TOP / scale_of(exponent)))
        code = code.astype(jnp.int32).astype(jnp.int16)
        out_ref[pl.ds(pl.multiple_of(i * TALL, TALL), TALL), :] = code
        scales[pl.ds(i, 1), :] = exponent

    several(rows // TALL, block)
    out_ref[pl.ds(rows, scale_lines(rows)), :] = (
        scales[pl.ds(0, scale_lines(rows)), :].astype(jnp.int32).astype(jnp.int16)
    )


def add_packet(packet, ref, total, scales):
    _, rows, coded = packet
    if not coded:
        total[...] = total[...] + ref[...]
        return
    scales[pl.ds(0, scale_lines(rows)), :] = ref[pl.ds(rows, scale_lines(rows)), :].astype(
        jnp.float32
    )

    def block(i):
        at = pl.ds(pl.multiple_of(i * TALL, TALL), TALL)
        scale = scale_of(scales[pl.ds(i, 1), :]) * (1.0 / CODE_TOP)
        total[at, :] = total[at, :] + ref[at, :].astype(jnp.float32) * scale

    several(rows // TALL, block)


def sort_tiles(tiles):
    count = len(tiles)
    tile_bits = bits_for(count)
    sub = lax.broadcasted_iota(jnp.int32, (SUB, LANES), 0)
    lane = lax.broadcasted_iota(jnp.int32, (SUB, LANES), 1)
    total_bits = tile_bits + 3 + 7

    def bit_mask(bit):
        if bit < tile_bits + 3:
            return ((sub >> (bit - tile_bits)) & 1) == 1
        return ((lane >> (bit - tile_bits - 3)) & 1) == 1

    masks = {b: bit_mask(b) for b in range(tile_bits, total_bits)}
    flips = {b: jnp.where(masks[b], -1, 0) for b in masks}

    def flip(t, phase):
        if phase >= total_bits:
            return 0
        if phase < tile_bits:
            return -1 if (t >> phase) & 1 else 0
        return flips[phase]

    for phase in range(1, total_bits + 1):
        changed = []
        for t in range(count):
            old = flip(t, phase - 1) if phase > 1 else 0
            new = flip(t, phase)
            if isinstance(old, int) and isinstance(new, int):
                turn = old ^ new
                changed.append(tiles[t] if turn == 0 else ~tiles[t])
            else:
                changed.append(tiles[t] ^ (old ^ new))
        tiles = changed
        for bit in reversed(range(phase)):
            if bit < tile_bits:
                step = 1 << bit
                tiles = list(tiles)
                for t in range(count):
                    if not t & step:
                        a, b = tiles[t], tiles[t | step]
                        tiles[t], tiles[t | step] = jnp.minimum(a, b), jnp.maximum(a, b)
                continue
            if bit < tile_bits + 3:
                axis, step, size = 0, 1 << (bit - tile_bits), SUB
            else:
                axis, step, size = 1, 1 << (bit - tile_bits - 3), LANES
            upper = masks[bit]
            moved = []
            for x in tiles:
                down = pltpu.roll(x, step, axis=axis)
                if 2 * step == size:
                    other = down
                else:
                    other = jnp.where(upper, down, pltpu.roll(x, size - step, axis=axis))
                moved.append(
                    jnp.where(upper, jnp.maximum(x, other), jnp.minimum(x, other))
                )
            tiles = moved
    return tiles


def prepare_kernel(
    n, owned, table_rows, dest_shift, row_bits, cell_bits, dummy, chains,
    lengths_ref, shard_ref, row_ref, cluster_ref, out_ref, order, straight, runs,
):
    users, slab = row_ref.shape
    sub = lax.broadcasted_iota(jnp.int32, (SUB, LANES), 0)
    lane = lax.broadcasted_iota(jnp.int32, (SUB, LANES), 1)
    me = lax.axis_index("tm")
    length = jnp.zeros((SUB, LANES), jnp.int32)
    live_total = jnp.int32(0)
    for u in range(users):
        length = jnp.where(sub == u, lengths_ref[u], length)
        live_total += jnp.clip(lengths_ref[u] - me * slab, 0, slab)
    length = length - me * slab

    base = jnp.zeros((SUB, LANES), jnp.int32)
    in_chain = jnp.zeros((SUB, LANES), jnp.int32)
    chain_size = jnp.zeros((SUB, LANES), jnp.int32)
    chain_at = []
    for lo, size, _ in chains:
        inside = (sub >= lo) & (sub < lo + size)
        base = jnp.where(inside, lo * (K // 2), base)
        in_chain = jnp.where(inside, sub - lo, in_chain)
        chain_size = jnp.where(inside, size, chain_size)
        chain_at.append(inside)

    owner_shift = bits_for(owned)
    tiles = []
    spare = LANES - owned
    hot_owner = [[] for _ in range(users)]
    hot_slot = [[] for _ in range(users)]
    owner_iota = lax.broadcasted_iota(jnp.int32, (n, LANES), 0)
    slot_iota = lax.broadcasted_iota(jnp.int32, (LANES, LANES), 0)
    for j in range(slab // LANES):
        at = pl.ds(j * LANES, LANES)
        row, cluster = row_ref[:, at], cluster_ref[:, at]
        shard = shard_ref[pl.ds(j, users, stride=slab // LANES), :]
        owner = lax.shift_right_logical(cluster, owner_shift)
        low = cluster & (owned - 1)
        live = lane + j * LANES < length
        dest = (shard & ~1) | (owner & 1)
        away = lax.shift_right_logical(owner ^ dest, 1)
        spread = jnp.zeros((SUB, LANES), jnp.int32)
        by_order = {}
        for (_, _, bits), inside in zip(chains, chain_at):
            if bits not in by_order:
                turned = jnp.zeros((SUB, LANES), jnp.int32)
                for bit in bits:
                    turned = turned * 2 + ((away >> bit) & 1)
                by_order[bits] = turned
            spread = jnp.where(inside, by_order[bits], spread)
        cell = base + ((spread * chain_size + in_chain) << owner_shift) + low
        there = ((shard ^ owner) & 1) * table_rows + row
        key = (dest << dest_shift) | (cell << row_bits) | there
        tiles.append(jnp.where(live, key, NONE))
        live_owner = jnp.where(live, owner, -1)
        for u in range(users):
            hot_owner[u].append((owner_iota == live_owner[u : u + 1, :]).astype(jnp.bfloat16))
            hot_slot[u].append((slot_iota == low[u : u + 1, :] + spare).astype(jnp.bfloat16))

    for u in range(users):
        counts = lax.dot_general(
            jnp.concatenate(hot_owner[u], axis=1),
            jnp.concatenate(hot_slot[u], axis=1),
            (((1,), (1,)), ((), ())),
            preferred_element_type=jnp.float32,
        ).astype(jnp.int32)
        for d in range(n):
            out_ref[d, pl.ds(u, 1), :] = counts[d : d + 1, :]

    ends = []
    for d in range(n - 1):
        below = jnp.zeros((SUB, LANES), jnp.float32)
        for x in tiles:
            below += (x < ((d + 1) << dest_shift)).astype(jnp.float32)
        ends.append(jnp.sum(below).astype(jnp.int32))
    ends.append(live_total)

    empty = jnp.full((SUB, LANES), NONE, jnp.int32)
    tiles = sort_tiles(tiles + [empty] * ((1 << bits_for(len(tiles))) - len(tiles)))
    count = len(tiles)
    for t, x in enumerate(tiles):
        order[pl.ds(t * SUB, SUB), :] = x
    lines = [order[pl.ds(s, count, stride=SUB), :] for s in range(SUB)]
    straight[...] = jnp.concatenate(lines, axis=0).T

    at = (RUNS, LANES)
    run = lax.broadcasted_iota(jnp.int32, at, 0)
    lane = lax.broadcasted_iota(jnp.int32, at, 1)
    one_line = lax.broadcasted_iota(jnp.int32, (1, LANES), 1)
    start = jnp.int32(0)
    for d in range(n):
        count = ends[d] - start
        steps = lax.shift_right_logical(count + RUNS - 1, bits_for(RUNS))
        for j in range(RUNS):
            begin = start + j * steps
            off = begin & (LANES - 1)
            two = straight[pl.ds(lax.shift_right_logical(begin, bits_for(LANES)), 2), :]
            two = pltpu.roll(two, (LANES - off) & (LANES - 1), axis=1)
            runs[pl.ds(d * RUNS + j, 1), :] = jnp.where(one_line < LANES - off, two[:1], two[1:])
        mine = runs[pl.ds(d * RUNS, RUNS), :]
        valid = (lane < steps) & (run * steps + lane < count)
        there = mine & (2 * table_rows - 1)
        cell = lax.shift_right_logical(mine, row_bits) & ((1 << cell_bits) - 1)
        code = jnp.where(valid, (there << (cell_bits + 3)) | (cell << 1), dummy)
        cell = jnp.where(valid, cell, -1)
        following = pltpu.roll(cell, RUNS - 1, axis=0)
        same = (cell >= 0) & (cell == following) & (run < RUNS - 1)
        twice = jnp.max(jnp.where(same, 1.0, 0.0)).astype(jnp.int32)
        head = jnp.full((RUNS, LANES), steps | (twice << MODE), jnp.int32)
        beside = jnp.where(run < users, out_ref[d], head)
        out_ref[d] = jnp.where(lane < spare, code, beside)
        start = ends[d]


def add_kernel(
    n, head_at, cell_bits, request_ref, own_ref, other_ref, sums, table, codes, code_sems
):
    stride = RUNS * LANES
    low = (4 << cell_bits) - 1
    rows = own_ref.shape[0]

    def read(s):
        at = pl.ds(pl.multiple_of(s * stride, stride), stride)
        slot = lax.rem(s, SLOTS)
        to = pl.ds(pl.multiple_of(slot * stride, stride), stride)
        return pltpu.make_async_copy(request_ref.at[at], codes.at[to], code_sems.at[slot])

    def start_read(s, _):
        read(s).start()
        return 0

    lax.fori_loop(0, min(SLOTS, n), start_read, 0)

    def clear(i, _):
        sums[pl.ds(i * LANES, LANES), :] = jnp.zeros((LANES, LANES), jnp.float32)
        return 0

    lax.fori_loop(0, sums.shape[0] // LANES, clear, 0)

    def widen(i, _):
        for part, ref in enumerate((own_ref, other_ref)):
            x = ref[pl.ds(i * LANES, LANES), :].astype(jnp.float32)
            at = (part * rows + i * LANES) * 2
            table[pl.ds(at, LANES, stride=2), :] = x[:, :LANES]
            table[pl.ds(at + 1, LANES, stride=2), :] = x[:, LANES:]
        return 0

    lax.fori_loop(0, rows // LANES, widen, 0)

    def place(code):
        cell = pl.multiple_of(code & low, 2)
        row = pl.multiple_of(lax.shift_right_logical(code, cell_bits + 2), 2)
        return pl.ds(cell, 2), pl.ds(row, 2)

    def source(s, _):
        read(s).wait()
        begin = lax.rem(s, SLOTS) * stride
        head = codes[begin + head_at]
        steps = head & ((1 << MODE) - 1)

        @pl.when(head < (1 << MODE))
        def _():
            def step(at):
                for first in range(0, RUNS, PART):
                    new = []
                    for k in range(first, first + PART):
                        cell, row = place(codes[at + k * LANES])
                        new.append((cell, sums[cell, :] + table[row, :]))
                    for cell, value in new:
                        sums[cell, :] = value

            def two_steps(i, _):
                step(begin + 2 * i)
                step(begin + 2 * i + 1)
                return 0

            lax.fori_loop(0, lax.shift_right_logical(steps, 1), two_steps, 0)

            @pl.when((steps & 1) == 1)
            def _():
                step(begin + steps - 1)

        @pl.when(head >= (1 << MODE))
        def _():
            def single(i, _):
                for k in range(RUNS):
                    cell, row = place(codes[begin + i + k * LANES])
                    sums[cell, :] = sums[cell, :] + table[row, :]
                return 0

            lax.fori_loop(0, steps, single, 0)

        @pl.when(s + SLOTS < n)
        def _():
            read(s + SLOTS).start()

        return 0

    lax.fori_loop(0, n, source, 0)


def split_kernel(start, packet, sums, _, keep_ref, packet_ref, scales):
    rows = packet[1]
    keep_ref[...] = sums[pl.ds(start, rows), :]
    encode(packet, sums, start + rows, packet_ref, scales)


def split(sums, start, packet, after):
    rows = packet[1]
    return pl.pallas_call(
        functools.partial(split_kernel, start, packet),
        out_shape=[jax.ShapeDtypeStruct((rows, LANES), jnp.float32), packet_shape(packet)],
        in_specs=[
            pl.BlockSpec(memory_space=pltpu.VMEM),
            pl.BlockSpec(memory_space=pl.ANY),
        ],
        out_specs=[pl.BlockSpec(memory_space=pltpu.VMEM)] * 2,
        scratch_shapes=[pltpu.VMEM((scale_lines(rows), LANES), jnp.float32)],
        compiler_params=pltpu.CompilerParams(vmem_limit_bytes=16 * 1024 * 1024),
    )(sums, after)


def merge_kernel(arrived, packet, kept, came, _, keep_ref, packet_ref, total, scales):
    rows = packet[1]
    total[...] = kept[...]
    add_packet(arrived, came, total, scales)
    keep_ref[...] = total[pl.ds(0, rows), :]
    encode(packet, total, rows, packet_ref, scales)


def merge(kept, came, arrived, packet, after):
    lines = kept.shape[0]
    return pl.pallas_call(
        functools.partial(merge_kernel, arrived, packet),
        out_shape=[
            jax.ShapeDtypeStruct((lines // 2, LANES), jnp.float32),
            packet_shape(packet),
        ],
        in_specs=[pl.BlockSpec(memory_space=pltpu.VMEM)] * 2
        + [pl.BlockSpec(memory_space=pl.ANY)],
        out_specs=[pl.BlockSpec(memory_space=pltpu.VMEM)] * 2,
        scratch_shapes=[
            pltpu.VMEM((lines, LANES), jnp.float32),
            pltpu.VMEM((scale_lines(lines), LANES), jnp.float32),
        ],
        compiler_params=pltpu.CompilerParams(vmem_limit_bytes=16 * 1024 * 1024),
    )(kept, came, after)


def finish_kernel(arrived, count_ref, *refs):
    k = len(arrived)
    kept, came, out_ref = refs[:k], refs[k : 2 * k], refs[2 * k]
    totals, scales = refs[2 * k + 1 : -1], refs[-1]
    at = 0
    for packet, mine, other, total in zip(arrived, kept, came, totals):
        total[...] = mine[...]
        add_packet(packet, other, total, scales)
        rows = total.shape[0] // 2
        members = jnp.maximum(count_ref[pl.ds(at, rows), :], 1.0)
        for side in range(2):
            mean = total[pl.ds(side, rows, stride=2), :] / members
            out_ref[pl.ds(at, rows), pl.ds(side * LANES, LANES)] = mean
        at += rows


def finish(kept, came, arrived, counts):
    lines = sum(x.shape[0] for x in kept)
    return pl.pallas_call(
        functools.partial(finish_kernel, arrived),
        out_shape=jax.ShapeDtypeStruct((lines // 2, 2 * LANES), jnp.float32),
        in_specs=[pl.BlockSpec(memory_space=pltpu.VMEM)] * (1 + 2 * len(kept)),
        out_specs=pl.BlockSpec(memory_space=pltpu.VMEM),
        scratch_shapes=[pltpu.VMEM(x.shape, x.dtype) for x in kept]
        + [pltpu.VMEM((scale_lines(lines), LANES), jnp.float32)],
        compiler_params=pltpu.CompilerParams(vmem_limit_bytes=16 * 1024 * 1024),
    )(counts, *kept, *came)


def exchange(block, packet, n):
    return lax.ppermute(block, "tm", [(i, i ^ (2 << packet[0])) for i in range(n)])


def per_device(item_table, item_shard, item_row, cluster_id, lengths):
    n = lax.axis_size("tm")
    users, slab = item_row.shape[1:]
    rows, width = item_table.shape
    total = users * slab
    owned = K // n
    m = bits_for(n) - 1
    cells = users * K // 2
    cell_bits = bits_for(cells)
    row_bits = bits_for(2 * rows)
    dest_shift = cell_bits + row_bits
    most = -(-4 * total // n // RUNS)
    assert users * 2 <= RUNS and most <= LANES - owned
    chains = user_chains(users, m)
    dummy = cells * 2

    other = lax.ppermute(item_table, "tm", [(i, i ^ 1) for i in range(n)])
    buckets = pl.pallas_call(
        functools.partial(
            prepare_kernel, n, owned, rows, dest_shift, row_bits, cell_bits, dummy, chains,
        ),
        out_shape=jax.ShapeDtypeStruct((n, RUNS, LANES), jnp.int32),
        in_specs=[pl.BlockSpec(memory_space=pltpu.SMEM)]
        + [pl.BlockSpec(memory_space=pltpu.VMEM)] * 3,
        out_specs=pl.BlockSpec(memory_space=pltpu.VMEM),
        scratch_shapes=[
            pltpu.VMEM((LANES, LANES), jnp.int32),
            pltpu.VMEM((LANES, LANES), jnp.int32),
            pltpu.VMEM((n * RUNS, LANES), jnp.int32),
        ],
    )(
        lengths,
        item_shard.reshape(total // LANES, LANES),
        item_row.reshape(users, slab),
        cluster_id.reshape(users, slab),
    )
    requests = lax.all_to_all(buckets, "tm", split_axis=0, concat_axis=0, tiled=True)
    counts = jnp.sum(requests[:, :users, LANES - owned :], axis=0).astype(jnp.float32)
    counts = counts.reshape(users * owned, 1)

    requests = requests.reshape(-1)
    sums = pl.pallas_call(
        functools.partial(add_kernel, n, users * LANES + LANES - owned, cell_bits),
        out_shape=jax.ShapeDtypeStruct((cells * 2 + LANES, LANES), jnp.float32),
        in_specs=[pl.BlockSpec(memory_space=pltpu.VMEM)] * 3,
        out_specs=pl.BlockSpec(memory_space=pltpu.VMEM),
        scratch_shapes=[
            pltpu.VMEM((rows * 4, LANES), jnp.float32),
            pltpu.SMEM((SLOTS * RUNS * LANES,), jnp.int32),
            pltpu.SemaphoreType.DMA((SLOTS,)),
        ],
        compiler_params=pltpu.CompilerParams(vmem_limit_bytes=32 * 1024 * 1024),
    )(requests, item_table, other)

    after = requests
    kept, came, arrived = [], [], []
    for lo, size, order in chains:
        packet = packet_of((lo, size, order), 0, size * (K // 2))
        mine, sent = split(sums, lo * K, packet, after)
        after = mine
        kept.append(mine)
        came.append(exchange(sent, packet, n))
        arrived.append(packet)
    for stage in range(1, m):
        for c, chain in enumerate(chains):
            packet = packet_of(chain, stage, arrived[c][1] // 2)
            mine, sent = merge(kept[c], came[c], arrived[c], packet, after)
            after = mine
            kept[c], came[c], arrived[c] = mine, exchange(sent, packet, n), packet
    return finish(kept, came, arrived, counts).reshape(users, owned, width)


def solution(mesh):
    return jax.shard_map(
        per_device,
        mesh=mesh,
        in_specs=(
            P("tm", None),
            P("tm", ("groups", "users"), None, None),
            P("tm", ("groups", "users"), None),
            P("tm", ("groups", "users"), None),
            P(("groups", "users")),
        ),
        out_specs=P(("groups", "users"), "tm", None),
        check_vma=False,
    )
```

```python
import functools
import math

import jax
import jax.numpy as jnp
from jax import lax
from jax.experimental import pallas as pl
from jax.experimental.pallas import tpu as pltpu
from jax.sharding import PartitionSpec as P

K = 1024
LANES = 128
SUB = 8
RUNS = 16
PARTS = [(0, 6), (6, 11), (11, 16)]
SLOTS = 16
MODE = 16
NONE = 2**31 - 1
CODE_TOP = 32766.0
TALL = 64


def bits_for(count):
    return (count - 1).bit_length()


def user_chains(users, m):
    orders = [(0, 2, 1, 3), (2, 1, 0, 3), (1, 0, 3, 2)] if m == 4 else [tuple(range(m))] * 3
    sizes = [-(-users * 3 // 8), users * 3 // 8]
    sizes.append(users - sum(sizes))
    chains, lo = [], 0
    for size, order in zip(sizes, orders):
        if size:
            chains.append((lo, size, order))
        lo += size
    return chains


def packet_of(chain, stage, rows):
    order = chain[2]
    return (order[stage], rows, rows % TALL == 0) if stage < len(order) else None


def packet_shape(packet):
    _, lines, coded = packet
    if not coded:
        return jax.ShapeDtypeStruct((lines, LANES), jnp.float32)
    return jax.ShapeDtypeStruct((lines + scale_lines(lines), LANES), jnp.int16)


def scale_lines(lines):
    return -(-lines // TALL // 16) * 16


def scale_of(exponent):
    return jnp.exp(exponent * (math.log(2.0) / 64.0))


def several(count, block):
    def turn(t, _):
        for k in range(4):
            block(4 * t + k)
        return 0

    lax.fori_loop(0, count // 4, turn, 0)
    for i in range(count // 4 * 4, count):
        block(i)


def encode(packet, ref, start, out_ref, scales):
    _, rows, coded = packet
    if not coded:
        out_ref[...] = ref[pl.ds(start, rows), :]
        return

    def block(i):
        x = ref[pl.ds(start + i * TALL, TALL), :]
        top = jnp.maximum(jnp.max(jnp.abs(x), axis=0, keepdims=True), 1e-33)
        exponent = jnp.ceil(jnp.log(top) * (64.0 / math.log(2.0)))
        code = jnp.round(x * (CODE_TOP / scale_of(exponent)))
        code = code.astype(jnp.int32).astype(jnp.int16)
        out_ref[pl.ds(pl.multiple_of(i * TALL, TALL), TALL), :] = code
        scales[pl.ds(i, 1), :] = exponent

    several(rows // TALL, block)
    out_ref[pl.ds(rows, scale_lines(rows)), :] = (
        scales[pl.ds(0, scale_lines(rows)), :].astype(jnp.int32).astype(jnp.int16)
    )


def add_packet(packet, ref, total, scales):
    _, rows, coded = packet
    if not coded:
        total[...] = total[...] + ref[...]
        return
    scales[pl.ds(0, scale_lines(rows)), :] = ref[pl.ds(rows, scale_lines(rows)), :].astype(
        jnp.float32
    )

    def block(i):
        at = pl.ds(pl.multiple_of(i * TALL, TALL), TALL)
        scale = scale_of(scales[pl.ds(i, 1), :]) * (1.0 / CODE_TOP)
        total[at, :] = total[at, :] + ref[at, :].astype(jnp.float32) * scale

    several(rows // TALL, block)


def sort_tiles(tiles):
    count = len(tiles)
    tile_bits = bits_for(count)
    sub = lax.broadcasted_iota(jnp.int32, (SUB, LANES), 0)
    lane = lax.broadcasted_iota(jnp.int32, (SUB, LANES), 1)
    total_bits = tile_bits + 3 + 7

    def bit_mask(bit):
        if bit < tile_bits + 3:
            return ((sub >> (bit - tile_bits)) & 1) == 1
        return ((lane >> (bit - tile_bits - 3)) & 1) == 1

    masks = {b: bit_mask(b) for b in range(tile_bits, total_bits)}
    flips = {b: jnp.where(masks[b], -1, 0) for b in masks}

    def flip(t, phase):
        if phase >= total_bits:
            return 0
        if phase < tile_bits:
            return -1 if (t >> phase) & 1 else 0
        return flips[phase]

    for phase in range(1, total_bits + 1):
        changed = []
        for t in range(count):
            old = flip(t, phase - 1) if phase > 1 else 0
            new = flip(t, phase)
            if isinstance(old, int) and isinstance(new, int):
                turn = old ^ new
                changed.append(tiles[t] if turn == 0 else ~tiles[t])
            else:
                changed.append(tiles[t] ^ (old ^ new))
        tiles = changed
        for bit in reversed(range(phase)):
            if bit < tile_bits:
                step = 1 << bit
                tiles = list(tiles)
                for t in range(count):
                    if not t & step:
                        a, b = tiles[t], tiles[t | step]
                        tiles[t], tiles[t | step] = jnp.minimum(a, b), jnp.maximum(a, b)
                continue
            if bit < tile_bits + 3:
                axis, step, size = 0, 1 << (bit - tile_bits), SUB
            else:
                axis, step, size = 1, 1 << (bit - tile_bits - 3), LANES
            upper = masks[bit]
            moved = []
            for x in tiles:
                down = pltpu.roll(x, step, axis=axis)
                if 2 * step == size:
                    other = down
                else:
                    other = jnp.where(upper, down, pltpu.roll(x, size - step, axis=axis))
                moved.append(
                    jnp.where(upper, jnp.maximum(x, other), jnp.minimum(x, other))
                )
            tiles = moved
    return tiles


def prepare_kernel(
    n, owned, table_rows, dest_shift, row_bits, cell_bits, dummy, chains,
    lengths_ref, shard_ref, row_ref, cluster_ref, out_ref, order, straight, runs,
):
    users, slab = row_ref.shape
    sub = lax.broadcasted_iota(jnp.int32, (SUB, LANES), 0)
    lane = lax.broadcasted_iota(jnp.int32, (SUB, LANES), 1)
    me = lax.axis_index("tm")
    length = jnp.zeros((SUB, LANES), jnp.int32)
    live_total = jnp.int32(0)
    for u in range(users):
        length = jnp.where(sub == u, lengths_ref[u], length)
        live_total += jnp.clip(lengths_ref[u] - me * slab, 0, slab)
    length = length - me * slab

    base = jnp.zeros((SUB, LANES), jnp.int32)
    in_chain = jnp.zeros((SUB, LANES), jnp.int32)
    chain_size = jnp.zeros((SUB, LANES), jnp.int32)
    chain_at = []
    for lo, size, _ in chains:
        inside = (sub >= lo) & (sub < lo + size)
        base = jnp.where(inside, lo * (K // 2), base)
        in_chain = jnp.where(inside, sub - lo, in_chain)
        chain_size = jnp.where(inside, size, chain_size)
        chain_at.append(inside)

    owner_shift = bits_for(owned)
    tiles = []
    spare = LANES - owned
    hot_owner = [[] for _ in range(users)]
    hot_slot = [[] for _ in range(users)]
    owner_iota = lax.broadcasted_iota(jnp.int32, (n, LANES), 0)
    slot_iota = lax.broadcasted_iota(jnp.int32, (LANES, LANES), 0)
    for j in range(slab // LANES):
        at = pl.ds(j * LANES, LANES)
        row, cluster = row_ref[:, at], cluster_ref[:, at]
        shard = shard_ref[pl.ds(j, users, stride=slab // LANES), :]
        owner = lax.shift_right_logical(cluster, owner_shift)
        low = cluster & (owned - 1)
        live = lane + j * LANES < length
        dest = (shard & ~1) | (owner & 1)
        away = lax.shift_right_logical(owner ^ dest, 1)
        spread = jnp.zeros((SUB, LANES), jnp.int32)
        by_order = {}
        for (_, _, bits), inside in zip(chains, chain_at):
            if bits not in by_order:
                turned = jnp.zeros((SUB, LANES), jnp.int32)
                for bit in bits:
                    turned = turned * 2 + ((away >> bit) & 1)
                by_order[bits] = turned
            spread = jnp.where(inside, by_order[bits], spread)
        cell = base + ((spread * chain_size + in_chain) << owner_shift) + low
        there = ((shard ^ owner) & 1) * table_rows + row
        key = (dest << dest_shift) | (cell << row_bits) | there
        tiles.append(jnp.where(live, key, NONE))
        live_owner = jnp.where(live, owner, -1)
        for u in range(users):
            hot_owner[u].append((owner_iota == live_owner[u : u + 1, :]).astype(jnp.bfloat16))
            hot_slot[u].append((slot_iota == low[u : u + 1, :] + spare).astype(jnp.bfloat16))

    for u in range(users):
        counts = lax.dot_general(
            jnp.concatenate(hot_owner[u], axis=1),
            jnp.concatenate(hot_slot[u], axis=1),
            (((1,), (1,)), ((), ())),
            preferred_element_type=jnp.float32,
        ).astype(jnp.int32)
        for d in range(n):
            out_ref[d, pl.ds(u, 1), :] = counts[d : d + 1, :]

    ends = []
    for d in range(n - 1):
        below = jnp.zeros((SUB, LANES), jnp.float32)
        for x in tiles:
            below += (x < ((d + 1) << dest_shift)).astype(jnp.float32)
        ends.append(jnp.sum(below).astype(jnp.int32))
    ends.append(live_total)

    empty = jnp.full((SUB, LANES), NONE, jnp.int32)
    tiles = sort_tiles(tiles + [empty] * ((1 << bits_for(len(tiles))) - len(tiles)))
    count = len(tiles)
    for t, x in enumerate(tiles):
        order[pl.ds(t * SUB, SUB), :] = x
    lines = [order[pl.ds(s, count, stride=SUB), :] for s in range(SUB)]
    straight[...] = jnp.concatenate(lines, axis=0).T

    at = (RUNS, LANES)
    run = lax.broadcasted_iota(jnp.int32, at, 0)
    lane = lax.broadcasted_iota(jnp.int32, at, 1)
    one_line = lax.broadcasted_iota(jnp.int32, (1, LANES), 1)
    start = jnp.int32(0)
    for d in range(n):
        count = ends[d] - start
        steps = lax.shift_right_logical(count + RUNS - 1, bits_for(RUNS))
        for j in range(RUNS):
            begin = start + j * steps
            off = begin & (LANES - 1)
            two = straight[pl.ds(lax.shift_right_logical(begin, bits_for(LANES)), 2), :]
            two = pltpu.roll(two, (LANES - off) & (LANES - 1), axis=1)
            runs[pl.ds(d * RUNS + j, 1), :] = jnp.where(one_line < LANES - off, two[:1], two[1:])
        mine = runs[pl.ds(d * RUNS, RUNS), :]
        valid = (lane < steps) & (run * steps + lane < count)
        there = mine & (2 * table_rows - 1)
        cell = lax.shift_right_logical(mine, row_bits) & ((1 << cell_bits) - 1)
        code = jnp.where(valid, (there << (cell_bits + 3)) | (cell << 1), dummy)
        cell = jnp.where(valid, cell, -1)
        following = pltpu.roll(cell, RUNS - 1, axis=0)
        same = (cell >= 0) & (cell == following) & (run < RUNS - 1)
        beyond = pltpu.roll(following, 1, axis=1)
        near = (cell >= 0) & (cell == beyond) & (run == RUNS // 2 - 1) & (lane > 0)
        mode = jnp.max(jnp.where(same, 2.0, jnp.where(near, 1.0, 0.0))).astype(jnp.int32)
        head = jnp.full((RUNS, LANES), steps | (mode << MODE), jnp.int32)
        beside = jnp.where(run < users, out_ref[d], head)
        out_ref[d] = jnp.where(lane < spare, code, beside)
        start = ends[d]


def add_kernel(
    n, head_at, cell_bits, request_ref, own_ref, other_ref, sums, table, codes, code_sems
):
    stride = RUNS * LANES
    low = (4 << cell_bits) - 1
    rows = own_ref.shape[0]

    def read(s):
        at = pl.ds(pl.multiple_of(s * stride, stride), stride)
        slot = lax.rem(s, SLOTS)
        to = pl.ds(pl.multiple_of(slot * stride, stride), stride)
        return pltpu.make_async_copy(request_ref.at[at], codes.at[to], code_sems.at[slot])

    def start_read(s, _):
        read(s).start()
        return 0

    lax.fori_loop(0, min(SLOTS, n), start_read, 0)

    def clear(i, _):
        sums[pl.ds(i * LANES, LANES), :] = jnp.zeros((LANES, LANES), jnp.float32)
        return 0

    lax.fori_loop(0, sums.shape[0] // LANES, clear, 0)

    def widen(i, _):
        for part, ref in enumerate((own_ref, other_ref)):
            x = ref[pl.ds(i * LANES, LANES), :].astype(jnp.float32)
            at = (part * rows + i * LANES) * 2
            table[pl.ds(at, LANES, stride=2), :] = x[:, :LANES]
            table[pl.ds(at + 1, LANES, stride=2), :] = x[:, LANES:]
        return 0

    lax.fori_loop(0, rows // LANES, widen, 0)

    def place(code):
        cell = pl.multiple_of(code & low, 2)
        row = pl.multiple_of(lax.shift_right_logical(code, cell_bits + 2), 2)
        return pl.ds(cell, 2), pl.ds(row, 2)

    def source(s, _):
        read(s).wait()
        begin = lax.rem(s, SLOTS) * stride
        head = codes[begin + head_at]
        steps = head & ((1 << MODE) - 1)

        def load(at, part):
            new = []
            for k in range(*part):
                cell, row = place(codes[at + k * LANES])
                new.append((cell, sums[cell, :] + table[row, :]))
            return new

        def store(new):
            for cell, value in new:
                sums[cell, :] = value

        mode = lax.shift_right_logical(head, MODE)
        turns = jnp.where(mode == 0, lax.shift_right_logical(steps, 2), 0)

        @pl.when(mode < 2)
        def _():
            def overlap(ats):
                waiting = []
                for at in ats:
                    for part in PARTS:
                        new = load(at, part)
                        store(waiting)
                        waiting = new
                store(waiting)

            def turn(i, _):
                overlap([begin + 4 * i + k for k in range(4)])
                return 0

            lax.fori_loop(0, turns, turn, 0)

            def step(i, _):
                overlap([begin + i])
                return 0

            lax.fori_loop(4 * turns, steps, step, 0)

        @pl.when(mode == 2)
        def _():
            def single(i, _):
                for k in range(RUNS):
                    cell, row = place(codes[begin + i + k * LANES])
                    sums[cell, :] = sums[cell, :] + table[row, :]
                return 0

            lax.fori_loop(0, steps, single, 0)

        @pl.when(s + SLOTS < n)
        def _():
            read(s + SLOTS).start()

        return 0

    lax.fori_loop(0, n, source, 0)


def split_kernel(start, packet, sums, _, keep_ref, packet_ref, scales):
    rows = packet[1]
    keep_ref[...] = sums[pl.ds(start, rows), :]
    encode(packet, sums, start + rows, packet_ref, scales)


def split(sums, start, packet, after):
    rows = packet[1]
    return pl.pallas_call(
        functools.partial(split_kernel, start, packet),
        out_shape=[jax.ShapeDtypeStruct((rows, LANES), jnp.float32), packet_shape(packet)],
        in_specs=[
            pl.BlockSpec(memory_space=pltpu.VMEM),
            pl.BlockSpec(memory_space=pl.ANY),
        ],
        out_specs=[pl.BlockSpec(memory_space=pltpu.VMEM)] * 2,
        scratch_shapes=[pltpu.VMEM((scale_lines(rows), LANES), jnp.float32)],
        compiler_params=pltpu.CompilerParams(vmem_limit_bytes=16 * 1024 * 1024),
    )(sums, after)


def merge_kernel(arrived, packet, kept, came, _, keep_ref, packet_ref, total, scales):
    rows = packet[1]
    total[...] = kept[...]
    add_packet(arrived, came, total, scales)
    keep_ref[...] = total[pl.ds(0, rows), :]
    encode(packet, total, rows, packet_ref, scales)


def merge(kept, came, arrived, packet, after):
    lines = kept.shape[0]
    return pl.pallas_call(
        functools.partial(merge_kernel, arrived, packet),
        out_shape=[
            jax.ShapeDtypeStruct((lines // 2, LANES), jnp.float32),
            packet_shape(packet),
        ],
        in_specs=[pl.BlockSpec(memory_space=pltpu.VMEM)] * 2
        + [pl.BlockSpec(memory_space=pl.ANY)],
        out_specs=[pl.BlockSpec(memory_space=pltpu.VMEM)] * 2,
        scratch_shapes=[
            pltpu.VMEM((lines, LANES), jnp.float32),
            pltpu.VMEM((scale_lines(lines), LANES), jnp.float32),
        ],
        compiler_params=pltpu.CompilerParams(vmem_limit_bytes=16 * 1024 * 1024),
    )(kept, came, after)


def finish_kernel(arrived, count_ref, *refs):
    k = len(arrived)
    kept, came, out_ref = refs[:k], refs[k : 2 * k], refs[2 * k]
    totals, scales = refs[2 * k + 1 : -1], refs[-1]
    at = 0
    for packet, mine, other, total in zip(arrived, kept, came, totals):
        total[...] = mine[...]
        add_packet(packet, other, total, scales)
        rows = total.shape[0] // 2
        members = jnp.maximum(count_ref[pl.ds(at, rows), :], 1.0)
        for side in range(2):
            mean = total[pl.ds(side, rows, stride=2), :] / members
            out_ref[pl.ds(at, rows), pl.ds(side * LANES, LANES)] = mean
        at += rows


def finish(kept, came, arrived, counts):
    lines = sum(x.shape[0] for x in kept)
    return pl.pallas_call(
        functools.partial(finish_kernel, arrived),
        out_shape=jax.ShapeDtypeStruct((lines // 2, 2 * LANES), jnp.float32),
        in_specs=[pl.BlockSpec(memory_space=pltpu.VMEM)] * (1 + 2 * len(kept)),
        out_specs=pl.BlockSpec(memory_space=pltpu.VMEM),
        scratch_shapes=[pltpu.VMEM(x.shape, x.dtype) for x in kept]
        + [pltpu.VMEM((scale_lines(lines), LANES), jnp.float32)],
        compiler_params=pltpu.CompilerParams(vmem_limit_bytes=16 * 1024 * 1024),
    )(counts, *kept, *came)


def exchange(block, packet, n):
    return lax.ppermute(block, "tm", [(i, i ^ (2 << packet[0])) for i in range(n)])


def per_device(item_table, item_shard, item_row, cluster_id, lengths):
    n = lax.axis_size("tm")
    users, slab = item_row.shape[1:]
    rows, width = item_table.shape
    total = users * slab
    owned = K // n
    m = bits_for(n) - 1
    cells = users * K // 2
    cell_bits = bits_for(cells)
    row_bits = bits_for(2 * rows)
    dest_shift = cell_bits + row_bits
    most = -(-4 * total // n // RUNS)
    assert users * 2 <= RUNS and most <= LANES - owned
    chains = user_chains(users, m)
    dummy = cells * 2

    other = lax.ppermute(item_table, "tm", [(i, i ^ 1) for i in range(n)])
    buckets = pl.pallas_call(
        functools.partial(
            prepare_kernel, n, owned, rows, dest_shift, row_bits, cell_bits, dummy, chains,
        ),
        out_shape=jax.ShapeDtypeStruct((n, RUNS, LANES), jnp.int32),
        in_specs=[pl.BlockSpec(memory_space=pltpu.SMEM)]
        + [pl.BlockSpec(memory_space=pltpu.VMEM)] * 3,
        out_specs=pl.BlockSpec(memory_space=pltpu.VMEM),
        scratch_shapes=[
            pltpu.VMEM((LANES, LANES), jnp.int32),
            pltpu.VMEM((LANES, LANES), jnp.int32),
            pltpu.VMEM((n * RUNS, LANES), jnp.int32),
        ],
    )(
        lengths,
        item_shard.reshape(total // LANES, LANES),
        item_row.reshape(users, slab),
        cluster_id.reshape(users, slab),
    )
    requests = lax.all_to_all(buckets, "tm", split_axis=0, concat_axis=0, tiled=True)
    counts = jnp.sum(requests[:, :users, LANES - owned :], axis=0).astype(jnp.float32)
    counts = counts.reshape(users * owned, 1)

    requests = requests.reshape(-1)
    sums = pl.pallas_call(
        functools.partial(add_kernel, n, users * LANES + LANES - owned, cell_bits),
        out_shape=jax.ShapeDtypeStruct((cells * 2 + LANES, LANES), jnp.float32),
        in_specs=[pl.BlockSpec(memory_space=pltpu.VMEM)] * 3,
        out_specs=pl.BlockSpec(memory_space=pltpu.VMEM),
        scratch_shapes=[
            pltpu.VMEM((rows * 4, LANES), jnp.float32),
            pltpu.SMEM((SLOTS * RUNS * LANES,), jnp.int32),
            pltpu.SemaphoreType.DMA((SLOTS,)),
        ],
        compiler_params=pltpu.CompilerParams(vmem_limit_bytes=32 * 1024 * 1024),
    )(requests, item_table, other)

    after = requests
    kept, came, arrived = [], [], []
    for lo, size, order in chains:
        packet = packet_of((lo, size, order), 0, size * (K // 2))
        mine, sent = split(sums, lo * K, packet, after)
        after = mine
        kept.append(mine)
        came.append(exchange(sent, packet, n))
        arrived.append(packet)
    for stage in range(1, m):
        for c, chain in enumerate(chains):
            packet = packet_of(chain, stage, arrived[c][1] // 2)
            mine, sent = merge(kept[c], came[c], arrived[c], packet, after)
            after = mine
            kept[c], came[c], arrived[c] = mine, exchange(sent, packet, n), packet
    return finish(kept, came, arrived, counts).reshape(users, owned, width)


def solution(mesh):
    return jax.shard_map(
        per_device,
        mesh=mesh,
        in_specs=(
            P("tm", None),
            P("tm", ("groups", "users"), None, None),
            P("tm", ("groups", "users"), None),
            P("tm", ("groups", "users"), None),
            P(("groups", "users")),
        ),
        out_specs=P(("groups", "users"), "tm", None),
        check_vma=False,
    )
```
